32 devices in a mesh: wide: 8 (over y, x, core), narrow: 4 (over z).
Axes of the slice: x: 2, y: 2, z: 4, core: 2. Of those that a mesh axis runs over, the one named last changes fastest.
Arguments:
- hidden: bfloat16 [96, 512, 768], P(('wide', 'narrow')), may hold values from -6 to 6
- lengths: int32 [96], P(('wide', 'narrow')), may hold values from 16 to 512, as said below
- slot_order: int32 [96], P(('wide', 'narrow')), may hold values from 0 to 2, as said below
- labels: int32 [96], P(('wide', 'narrow')), may hold values from -1 to 2, as said below
- w_qkv: bfloat16 [2, 768, 2304], replicated, may hold values from -0.21875 to 0.21875
- b_query: float32 [2, 768], replicated, may hold values from -3 to 3
- b_value: float32 [2, 768], replicated, may hold values from -3 to 3
- w_out: bfloat16 [2, 768, 768], replicated, may hold values from -0.625 to 0.625
- b_out: float32 [2, 768], replicated, may hold values from -3 to 3
- ln1_gain: float32 [2, 768], replicated, may hold values from 0.1 to 1.9
- ln1_bias: float32 [2, 768], replicated, may hold values from -3 to 3
- w_in: bfloat16 [2, 768, 3072], replicated, may hold values from -0.21875 to 0.21875
- b_in: float32 [2, 3072], replicated, may hold values from -3 to 3
- w_back: bfloat16 [2, 3072, 768], replicated, may hold values from -0.15625 to 0.15625
- b_back: float32 [2, 768], replicated, may hold values from -3 to 3
- ln2_gain: float32 [2, 768], replicated, may hold values from 0.1 to 1.9
- ln2_bias: float32 [2, 768], replicated, may hold values from -3 to 3
- pool_w: float32 [2, 768, 768], replicated, may hold values from -0.21875 to 0.21875
- pool_b: float32 [2, 768], replicated, may hold values from -3 to 3
- cls_w: float32 [2, 768, 3], replicated, may hold values from -0.625 to 0.625
- cls_b: float32 [2, 3], replicated, may hold values from -3 to 3
Outputs:
- block_states: bfloat16 [2, 96, 512, 768], P(None, ('wide', 'narrow'))
- logits: float32 [2, 96, 3], P(None, ('wide', 'narrow'))
- losses: float32 [2], replicated
- grad_pool_w: float32 [2, 768, 768], replicated
- grad_pool_b: float32 [2, 768], replicated
- grad_cls_w: float32 [2, 768, 3], replicated
- grad_cls_b: float32 [2, 3], replicated
- first_grads: float32 [2, 96, 768], P(None, ('wide', 'narrow'))
The draws below stay inside these ranges and needn't reach their ends.
Inputs may be any that keep to these rules, and one draw needn't show every extreme that they name: `lengths`: sequence 0 has length 512; the last sequence has length 16. `slot_order`: within each device's 3 slots every local index appears once. `labels`: the first arriving sequence of each device carries a label.
All inputs are finite; a program needn't handle non-finite values.
Results may differ from the reference program's by a relative error of at most 0.0085.
Values sent between devices are 32-bit elements; how exact they have to be, the bound alone decides.
A program may use at most 256 MiB of HBM per device.

```python
import jax
import jax.numpy as jnp
from jax import lax

D = 768
HEADS = 12
HEAD = 64
FF = 3072
CLASSES = 3
LAYERS = 2
MAXLEN = 512
MINLEN = 16
SEQ_DEV = 3
SEQS = 96


def draw_lengths(key, part):
    key = jax.random.fold_in(key, 1)
    drawn = jax.random.randint(key, (SEQS,), MINLEN, MAXLEN + 1, dtype=jnp.int32)
    drawn = drawn.at[0].set(MAXLEN)
    if SEQS > 1:
        drawn = drawn.at[SEQS - 1].set(MINLEN)
    return drawn


def draw_slot_order(key, part):
    key = jax.random.fold_in(key, 2)
    device_keys = jax.random.split(key, SEQS // SEQ_DEV)
    orders = jax.vmap(lambda single: jax.random.permutation(single, SEQ_DEV))(device_keys)
    return orders.reshape(SEQS).astype(jnp.int32)


def draw_labels(key, part):
    key = jax.random.fold_in(key, 3)
    first_key, second_key = jax.random.split(key)
    drawn = jax.random.randint(first_key, (SEQS,), -1, CLASSES, dtype=jnp.int32)
    sure = jax.random.randint(second_key, (SEQS,), 0, CLASSES, dtype=jnp.int32)
    leading = jnp.arange(SEQS, dtype=jnp.int32) % SEQ_DEV == 0
    drawn = jnp.where(leading, sure, drawn)
    drawn = drawn.at[0].set(CLASSES - 1)
    if SEQ_DEV > 1:
        drawn = drawn.at[1].set(-1)
    return drawn


def shard_levels(key, shape, cuts, low, top_value):
    factor_of, own = 1.0, jax.random.fold_in(key, 6)
    for position, parts in cuts:
        draws = jnp.exp(jax.random.uniform(jax.random.fold_in(own, position), (parts,), jnp.float32, low / len(cuts), top_value / len(cuts)))
        factor_of = factor_of * jnp.repeat(draws, shape[position] // parts).reshape([-1 if axis == position else 1 for axis in range(len(shape))])
    return factor_of


def normal_values(rng, extent, scale, limit, pieces=(), kind=jnp.bfloat16):
    values = scale * jax.random.normal(rng, extent, jnp.float32)
    if pieces:
        values = values * shard_levels(rng, extent, pieces, -0.22, 0.18)
    return jnp.clip(values, -limit, limit).astype(kind)


def setup_inputs(seed: int = 0) -> dict:
    seeds = jax.random.split(jax.random.key(seed), 22)
    hidden = normal_values(seeds[0], (SEQS, MAXLEN, D), 1.0, 6.0, ((0, 32),))
    lengths = draw_lengths(jax.random.fold_in(seeds[21], 71), 0)
    slot_order = draw_slot_order(jax.random.fold_in(seeds[21], 71), 0)
    labels = draw_labels(jax.random.fold_in(seeds[21], 71), 0)
    w_qkv = normal_values(seeds[4], (LAYERS, D, 3 * D), D ** -0.5, 0.21875)
    b_query = normal_values(seeds[5], (LAYERS, D), 0.5, 3.0, (), jnp.float32)
    b_value = normal_values(seeds[6], (LAYERS, D), 0.5, 3.0, (), jnp.float32)
    w_out = normal_values(seeds[7], (LAYERS, D, D), (D // 8) ** -0.5, 0.625)
    b_out = normal_values(seeds[8], (LAYERS, D), 0.5, 3.0, (), jnp.float32)
    ln1_gain = jnp.clip(1.0 + 0.18 * jax.random.normal(seeds[9], (LAYERS, D), jnp.float32), 0.1, 1.9)
    ln1_bias = normal_values(seeds[10], (LAYERS, D), 0.5, 3.0, (), jnp.float32)
    w_in = normal_values(seeds[11], (LAYERS, D, FF), D ** -0.5, 0.21875)
    b_in = normal_values(seeds[12], (LAYERS, FF), 0.5, 3.0, (), jnp.float32)
    w_back = normal_values(seeds[13], (LAYERS, FF, D), (FF // 2) ** -0.5, 0.15625)
    b_back = normal_values(seeds[14], (LAYERS, D), 0.5, 3.0, (), jnp.float32)
    ln2_gain = jnp.clip(1.0 + 0.18 * jax.random.normal(seeds[15], (LAYERS, D), jnp.float32), 0.1, 1.9)
    ln2_bias = normal_values(seeds[16], (LAYERS, D), 0.5, 3.0, (), jnp.float32)
    pool_w = normal_values(seeds[17], (LAYERS, D, D), D ** -0.5, 0.21875, (), jnp.float32)
    pool_b = normal_values(seeds[18], (LAYERS, D), 0.5, 3.0, (), jnp.float32)
    cls_w = normal_values(seeds[19], (LAYERS, D, CLASSES), (D // 8) ** -0.5, 0.625, (), jnp.float32)
    cls_b = normal_values(seeds[20], (LAYERS, CLASSES), 0.5, 3.0, (), jnp.float32)
    return {"hidden": hidden, "lengths": lengths, "slot_order": slot_order, "labels": labels, "w_qkv": w_qkv, "b_query": b_query, "b_value": b_value, "w_out": w_out, "b_out": b_out, "ln1_gain": ln1_gain, "ln1_bias": ln1_bias, "w_in": w_in, "b_in": b_in, "w_back": w_back, "b_back": b_back, "ln2_gain": ln2_gain, "ln2_bias": ln2_bias, "pool_w": pool_w, "pool_b": pool_b, "cls_w": cls_w, "cls_b": cls_b}


PRECISE = lax.Precision.HIGHEST
epsilon = 1e-12

@jax.custom_vjp
def low(v):
    return lax.optimization_barrier(v.astype(jnp.bfloat16)).astype(jnp.float32)

@jax.custom_vjp
def low_back(v):
    return v

def low_keep(v):
    return (low(v), None)

def low_pass(kept, grad):
    return (grad,)

def back_keep(v):
    return (v, None)

def back_low(kept, grad):
    return (low(grad),)
low.defvjp(low_keep, low_pass)
low_back.defvjp(back_keep, back_low)

def layer_norm(values, gain, shift):
    center = values - lax.optimization_barrier(jnp.mean(values, -1, keepdims=True))
    spread = lax.optimization_barrier(jnp.mean(center * center, -1, keepdims=True))
    return center * lax.rsqrt(spread + epsilon) * gain + shift

def block_forward(inputs, seq_lengths, weights):
    w_qkv, b_query, b_value, w_out, b_out, ln1_gain, ln1_bias, w_in, b_in, w_back, b_back, ln2_gain, ln2_bias = weights
    groups, length, width = inputs.shape
    rows = inputs.reshape(groups * length, width)
    joined = jnp.dot(rows, w_qkv, precision=PRECISE)
    queries = low(joined[:, :width] + b_query).reshape(groups, length, HEADS, HEAD)
    keys_low = low(joined[:, width:2 * width]).reshape(groups, length, HEADS, HEAD)
    values_low = low(joined[:, 2 * width:] + b_value).reshape(groups, length, HEADS, HEAD)
    scores = jnp.einsum('gqhd,gkhd->ghqk', queries, keys_low, precision=PRECISE) * HEAD ** (-0.5)
    visible = jnp.arange(length, dtype=jnp.int32)[None, :] < seq_lengths[:, None]
    scores = jnp.where(visible[:, None, None, :], scores, -1e+30)
    highest = lax.optimization_barrier(jnp.max(scores, -1, keepdims=True))
    raised = jnp.exp(scores - highest)
    probs = low(raised / lax.optimization_barrier(jnp.sum(raised, -1, keepdims=True)))
    context = low(jnp.einsum('ghqk,gkhd->gqhd', probs, values_low, precision=PRECISE))
    context = context.reshape(groups * length, width)
    attended = jnp.dot(context, w_out, precision=PRECISE) + b_out
    middle = layer_norm(rows + attended, ln1_gain, ln1_bias)
    expanded = low(jax.nn.gelu(jnp.dot(low(middle), w_in, precision=PRECISE) + b_in, approximate=False))
    result = layer_norm(middle + jnp.dot(expanded, w_back, precision=PRECISE) + b_back, ln2_gain, ln2_bias)
    return low(result).reshape(groups, length, width)

def reference(hidden, lengths, slot_order, labels, w_qkv, b_query, b_value, w_out, b_out, ln1_gain, ln1_bias, w_in, b_in, w_back, b_back, ln2_gain, ln2_bias, pool_w, pool_b, cls_w, cls_b):
    f32 = jnp.float32
    base_index = jnp.arange(SEQS, dtype=jnp.int32) // SEQ_DEV * SEQ_DEV
    source = (base_index + slot_order).astype(jnp.int32)
    start_states = hidden.astype(f32)[source]
    seq_lengths = lengths[source]
    seq_labels = labels[source]
    stacks = (w_qkv.astype(f32), b_query, b_value, w_out.astype(f32), b_out, ln1_gain, ln1_bias, w_in.astype(f32), b_in, w_back.astype(f32), b_back, ln2_gain, ln2_bias)
    count = jnp.sum((seq_labels >= 0).astype(f32))
    onehot = (seq_labels[:, None] == jnp.arange(CLASSES, dtype=jnp.int32)[None, :]).astype(f32)
    labelled = (seq_labels >= 0).astype(f32)

    def whole_forward(pool_weight, pool_bias, cls_weight, cls_bias, first_offsets):
        states = start_states
        total = jnp.zeros((), f32)
        loss_list = []
        logit_list = []
        outputs_all = []
        for number in range(LAYERS):
            weights = tuple((stacked[number] for stacked in stacks))
            grouped = states.reshape(SEQS // 8, 8, MAXLEN, D)
            lengths_grouped = seq_lengths.reshape(SEQS // 8, 8)

            def run_group(packed):
                return block_forward(packed[0], packed[1], weights)
            states = lax.map(run_group, (grouped, lengths_grouped)).reshape(SEQS, MAXLEN, D)
            outputs_all.append(states)
            first_states = states[:, 0, :] + first_offsets[number]
            pooled = jnp.tanh(jnp.dot(first_states, pool_weight[number], precision=PRECISE) + pool_bias[number])
            scores = jnp.dot(pooled, cls_weight[number], precision=PRECISE) + cls_bias[number]
            highest = lax.optimization_barrier(jnp.max(scores, -1, keepdims=True))
            log_total = highest[:, 0] + jnp.log(lax.optimization_barrier(jnp.sum(jnp.exp(scores - highest), -1)))
            picked = lax.optimization_barrier(jnp.sum(scores * onehot, -1))
            mean_loss = jnp.sum(labelled * (log_total - picked)) / count
            total = total + mean_loss
            loss_list.append(mean_loss)
            logit_list.append(scores)
        return (total, (jnp.stack(loss_list), jnp.stack(logit_list), jnp.stack(outputs_all)))
    offsets = jnp.zeros((LAYERS, SEQS, D), f32)
    total, pullback, extras = jax.vjp(whole_forward, pool_w, pool_b, cls_w, cls_b, offsets, has_aux=True)
    grads = pullback(jnp.ones_like(total))
    block_states = extras[2].astype(jnp.bfloat16)
    return (block_states, extras[1], extras[0], grads[0], grads[1], grads[2], grads[3], grads[4])
```

```python
import functools
import math

import jax
import jax.numpy as jnp
from jax import lax
from jax.experimental import pallas as pl
from jax.experimental.pallas import tpu as pltpu
from jax.sharding import PartitionSpec as P

HEAD = 64
PRECISE = lax.Precision.HIGHEST
epsilon = 1e-12
bf16 = jnp.bfloat16
f32 = jnp.float32
SCALE = HEAD**-0.5 * math.log2(math.e)
SUM_LOW = 2.0**-60
SUM_HIGH = 2.0**100


def gelu(values):
    return (0.5 * values) * (1.0 + lax.erf(values * math.sqrt(0.5)))


def norm_rows(values, gain, shift):
    center = values - jnp.mean(values, -1, keepdims=True)
    spread = jnp.mean(center * center, -1, keepdims=True)
    return center * lax.rsqrt(spread + epsilon) * gain + shift


def blocks_kernel(
    order,
    lens,
    hidden,
    w_qkv,
    w_out,
    w_in,
    w_back,
    b_query,
    b_value,
    b_out,
    ln1_gain,
    ln1_bias,
    b_in,
    b_back,
    ln2_gain,
    ln2_bias,
    states,
    firsts,
    x_buf,
    qkv_buf,
    out_buf,
    in_buf,
    back_buf,
    turned,
    columns,
    q_buf,
    k_buf,
    v_buf,
    p_buf,
    ct_buf,
    c_buf,
    m_buf,
    mb_buf,
    h_buf,
    fine,
    vec_buf,
    unit_buf,
    w_sem,
    x_sem,
    o_sem,
):
    depth, width = b_query.shape
    slots, length = x_buf.shape[1], x_buf.shape[2]
    heads = width // HEAD
    hidden_units = b_in.shape[1]

    def fetch_x(s):
        return pltpu.make_async_copy(hidden.at[order[s]], x_buf.at[0, s], x_sem.at[s])

    def fetch_qkv(l, part):
        cols = pl.ds(pl.multiple_of(part * width, 128), width)
        return pltpu.make_async_copy(
            w_qkv.at[l, :, cols], qkv_buf.at[l, :, cols], w_sem.at[l, part]
        )

    def fetch_rest(l, number):
        source = (w_out, w_in, w_back)[number]
        target = (out_buf, in_buf, back_buf)[number]
        return pltpu.make_async_copy(source.at[l], target.at[l], w_sem.at[l, 3 + number])

    def put_states(l, s):
        return pltpu.make_async_copy(x_buf.at[l + 1, s], states.at[l, s], o_sem.at[l, s])

    fetch_qkv(0, 0).start()
    fetch_qkv(0, 2).start()
    fetch_x(0).start()
    fetch_qkv(0, 1).start()
    for s in range(1, slots):
        fetch_x(s).start()
    for number in range(3):
        fetch_rest(0, number).start()
    for l in range(1, depth):
        for part in range(3):
            fetch_qkv(l, part).start()
        for number in range(3):
            fetch_rest(l, number).start()

    q_buf[...] = jnp.zeros_like(q_buf)
    vectors = (b_query, b_value, b_out, ln1_gain, ln1_bias, b_back, ln2_gain, ln2_bias)
    for l in range(depth):
        for number, vector in enumerate(vectors):
            vec_buf[l, number : number + 1] = vector[l : l + 1]
        unit_buf[l, 0:1] = b_in[l : l + 1]

    def project(l, s):
        rows = x_buf[l, s]
        k_buf[...] = jnp.dot(
            rows, qkv_buf[l, :, width : 2 * width], preferred_element_type=f32
        ).astype(bf16)
        count = lens[order[s]]
        seen = (
            lax.broadcasted_iota(jnp.int32, (HEAD, length), 1) < count
        ).astype(f32)
        joined = lax.dot_general(
            turned[...], rows, (((1,), (1,)), ((), ())), preferred_element_type=f32
        )
        for h in range(heads):
            at = slice(h * HEAD, (h + 1) * HEAD)
            half = slice((h % 2) * HEAD, (h % 2 + 1) * HEAD)
            q_buf[h, half] = (
                joined[at] + jnp.tile(columns[at, :], (1, length // 128))
            ).astype(bf16)
            av = slice(width + h * HEAD, width + (h + 1) * HEAD)
            v_buf[h, :HEAD] = (
                (joined[av] + jnp.tile(columns[av, :], (1, length // 128))) * seen
            ).astype(bf16)
            v_buf[h, HEAD:] = seen.astype(bf16)

    def attend(s):
        def score(h):
            pair = slice((h // 2) * 128, (h // 2 + 1) * 128)
            scores = jnp.dot(k_buf[:, pair], q_buf[h], preferred_element_type=f32)
            p_buf[h % 4] = jnp.exp2(scores * SCALE).astype(bf16)

        def mix(h):
            both = jnp.dot(v_buf[h], p_buf[h % 4], preferred_element_type=f32)
            sums = both[HEAD:]
            good = (sums[:8] >= SUM_LOW) & (sums[:8] <= SUM_HIGH)
            fine[...] = jnp.where(good, fine[...], 0.0)
            half = slice((h % 2) * HEAD, (h % 2 + 1) * HEAD)
            ct_buf[(h // 2) % 2, half] = (both[:HEAD] * (1.0 / sums)).astype(bf16)
            if h % 2 == 1:
                pair = slice((h // 2) * 128, (h // 2 + 1) * 128)
                c_buf[s, :, pair] = ct_buf[(h // 2) % 2].T

        score(0)
        for h in range(heads):
            if h + 1 < heads:
                score(h + 1)
            mix(h)

    def attend_shifted(s):
        count = lens[order[s]]

        def pair_step(number, carry):
            lanes = pl.ds(pl.multiple_of(number * 128, 128), 128)
            for side in range(2):
                h = number * 2 + side
                scores = (
                    jnp.dot(k_buf[:, lanes], q_buf[h], preferred_element_type=f32) * SCALE
                )
                seen = lax.broadcasted_iota(jnp.int32, scores.shape, 0) < count
                scores = jnp.where(seen, scores, -1e30)
                highest = jnp.max(scores, 0, keepdims=True)
                p_buf[side] = jnp.exp2(scores - highest).astype(bf16)
                both = jnp.dot(v_buf[h], p_buf[side], preferred_element_type=f32)
                ct_buf[0, side * HEAD : (side + 1) * HEAD] = (
                    both[:HEAD] / both[HEAD:]
                ).astype(bf16)
            c_buf[s, :, lanes] = ct_buf[0].T
            return carry

        lax.fori_loop(0, heads // 2, pair_step, 0)

    def feed(l, s):
        tile = length // 2
        spans = [slice(t * tile, (t + 1) * tile) for t in range(2)]
        shift_out, gain1, shift1, shift_back, gain2, shift2 = (
            vec_buf[l, number : number + 1] for number in range(2, 8)
        )
        for span in spans:
            attended = jnp.dot(c_buf[s, span], out_buf[l], preferred_element_type=f32)
            values = x_buf[l, s, span].astype(f32) + (attended + shift_out)
            middle = norm_rows(values, gain1, shift1)
            m_buf[span] = middle
            mb_buf[span] = middle.astype(bf16)
        chunk = 512
        for span in spans:
            for j in range(hidden_units // chunk):
                units = slice(j * chunk, (j + 1) * chunk)
                inner = jnp.dot(
                    mb_buf[span], in_buf[l, :, units], preferred_element_type=f32
                )
                h_buf[span, units] = gelu(inner + unit_buf[l, 0:1, units]).astype(bf16)
        for span in spans:
            back = jnp.dot(h_buf[span], back_buf[l], preferred_element_type=f32)
            values = m_buf[span] + back + shift_back
            x_buf[l + 1, s, span] = norm_rows(
                values, gain2, shift2
            ).astype(bf16)

    def layer(l, carry):
        for part in range(3):
            fetch_qkv(l, part).wait()
        for part, offset in ((0, 0), (2, width)):
            for j in range(width // 128):
                cols = slice(part * width + j * 128, part * width + (j + 1) * 128)
                turned[offset + j * 128 : offset + (j + 1) * 128] = qkv_buf[l, :, cols].T
        for j in range(width // 128):
            lanes = slice(j * 128, (j + 1) * 128)
            for number in range(2):
                offset = number * width + j * 128
                columns[offset : offset + 128] = jnp.broadcast_to(
                    vec_buf[l, number : number + 1, lanes], (128, 128)
                ).T
        fine[...] = jnp.ones_like(fine)

        def front(s, carry):
            @pl.when(l == 0)
            def _():
                fetch_x(s).wait()

            project(l, s)
            attend(s)
            return carry

        lax.fori_loop(0, slots, front, 0)

        @pl.when(jnp.min(fine[...]) < 0.5)
        def _():
            def again(s, carry):
                project(l, s)
                attend_shifted(s)
                return carry

            lax.fori_loop(0, slots, again, 0)

        for number in range(3):
            fetch_rest(l, number).wait()

        def rear(s, carry):
            feed(l, s)
            put_states(l, s).start()
            return carry

        lax.fori_loop(0, slots, rear, 0)
        return carry

    lax.fori_loop(0, depth, layer, 0)
    for l in range(depth):
        for s in range(slots):
            number = l * slots + s
            firsts[number : number + 1] = x_buf[l + 1, s, 0:1].astype(f32)
            put_states(l, s).wait()


def run_blocks(hidden, lengths, slot_order, stacks):
    (
        w_qkv,
        b_query,
        b_value,
        w_out,
        b_out,
        ln1_gain,
        ln1_bias,
        w_in,
        b_in,
        w_back,
        b_back,
        ln2_gain,
        ln2_bias,
    ) = stacks
    slots, length, width = hidden.shape
    depth = w_qkv.shape[0]
    units = w_in.shape[2]
    heads = width // HEAD
    place_hbm = pl.BlockSpec(memory_space=pl.ANY)
    place_smem = pl.BlockSpec(memory_space=pltpu.SMEM)
    place_vmem = pl.BlockSpec(memory_space=pltpu.VMEM)
    return pl.pallas_call(
        blocks_kernel,
        name="blocks",
        out_shape=(
            jax.ShapeDtypeStruct((depth, slots, length, width), bf16),
            jax.ShapeDtypeStruct((depth * slots, width), f32),
        ),
        in_specs=[place_smem] * 2 + [place_hbm] * 5 + [place_vmem] * 9,
        out_specs=(place_hbm, place_vmem),
        scratch_shapes=[
            pltpu.VMEM((depth + 1, slots, length, width), bf16),
            pltpu.VMEM((depth, width, 3 * width), bf16),
            pltpu.VMEM((depth, width, width), bf16),
            pltpu.VMEM((depth, width, units), bf16),
            pltpu.VMEM((depth, units, width), bf16),
            pltpu.VMEM((2 * width, width), bf16),
            pltpu.VMEM((2 * width, 128), f32),
            pltpu.VMEM((heads, 2 * HEAD, length), bf16),
            pltpu.VMEM((length, width), bf16),
            pltpu.VMEM((heads, 2 * HEAD, length), bf16),
            pltpu.VMEM((4, length, length), bf16),
            pltpu.VMEM((2, 2 * HEAD, length), bf16),
            pltpu.VMEM((slots, length, width), bf16),
            pltpu.VMEM((length, width), f32),
            pltpu.VMEM((length, width), bf16),
            pltpu.VMEM((length, units), bf16),
            pltpu.VMEM((8, length), f32),
            pltpu.VMEM((depth, 8, width), f32),
            pltpu.VMEM((depth, 8, units), f32),
            pltpu.SemaphoreType.DMA((depth, 6)),
            pltpu.SemaphoreType.DMA((slots,)),
            pltpu.SemaphoreType.DMA((depth, slots)),
        ],
        compiler_params=pltpu.CompilerParams(vmem_limit_bytes=62 * 1024 * 1024),
    )(
        slot_order,
        lengths,
        hidden,
        w_qkv,
        w_out,
        w_in,
        w_back,
        b_query,
        b_value,
        b_out,
        ln1_gain,
        ln1_bias,
        b_in,
        b_back,
        ln2_gain,
        ln2_bias,
    )


def ramp(firsts, labels, count, own, own_labels, pool_w, pool_b, cls_w, cls_b):
    classes = jnp.arange(cls_w.shape[1], dtype=jnp.int32)[None, :]

    def forward(states):
        pooled = jnp.tanh(jnp.dot(states, pool_w, precision=PRECISE) + pool_b)
        return pooled, jnp.dot(pooled, cls_w, precision=PRECISE) + cls_b

    def backward(pooled, scores, label_values):
        highest = jnp.max(scores, -1, keepdims=True)
        raised = jnp.exp(scores - highest)
        totals = jnp.sum(raised, -1, keepdims=True)
        onehot = (label_values[:, None] == classes).astype(f32)
        labelled = (label_values >= 0).astype(f32)
        log_total = highest[:, 0] + jnp.log(totals[:, 0])
        loss = jnp.sum(labelled * (log_total - jnp.sum(scores * onehot, -1))) / count
        grad = labelled[:, None] * (raised / totals - onehot) / count
        inner = jnp.dot(grad, cls_w.T, precision=PRECISE) * (1.0 - pooled * pooled)
        return loss, grad, inner

    pooled, scores = forward(firsts)
    loss, grad, inner = backward(pooled, scores, labels)
    own_pooled, own_scores = forward(own)
    _, _, own_inner = backward(own_pooled, own_scores, own_labels)
    return (
        own_scores,
        loss,
        jnp.dot(firsts.T, inner, precision=PRECISE),
        jnp.sum(inner, 0),
        jnp.dot(pooled.T, grad, precision=PRECISE),
        jnp.sum(grad, 0),
        jnp.dot(own_inner, pool_w.T, precision=PRECISE),
    )


def local(
    hidden,
    lengths,
    slot_order,
    labels,
    w_qkv,
    b_query,
    b_value,
    w_out,
    b_out,
    ln1_gain,
    ln1_bias,
    w_in,
    b_in,
    w_back,
    b_back,
    ln2_gain,
    ln2_bias,
    pool_w,
    pool_b,
    cls_w,
    cls_b,
):
    depth = w_qkv.shape[0]
    slots, _, width = hidden.shape
    stacks = (
        w_qkv,
        b_query,
        b_value,
        w_out,
        b_out,
        ln1_gain,
        ln1_bias,
        w_in,
        b_in,
        w_back,
        b_back,
        ln2_gain,
        ln2_bias,
    )
    states, firsts = run_blocks(hidden, lengths, slot_order, stacks)
    own_labels = jnp.take(labels, slot_order, axis=0)
    marks = jnp.zeros((8 - depth * slots % 8, width), f32)
    marks = marks.at[0, :slots].set(own_labels.astype(f32))
    packet = jnp.concatenate([firsts, marks])
    gathered = lax.all_gather(packet, "narrow", axis=0, tiled=False)
    gathered = lax.all_gather(gathered, "wide", axis=0, tiled=False)
    gathered = gathered.reshape(-1, packet.shape[0], width)
    all_labels = gathered[:, depth * slots, :slots].reshape(-1).astype(jnp.int32)
    count = jnp.sum((all_labels >= 0).astype(f32))
    results = []
    for l in range(depth):
        mine = slice(l * slots, (l + 1) * slots)
        results.append(
            ramp(
                gathered[:, mine].reshape(-1, width),
                all_labels,
                count,
                firsts[mine],
                own_labels,
                pool_w[l],
                pool_b[l],
                cls_w[l],
                cls_b[l],
            )
        )
    return (states,) + tuple(jnp.stack(members) for members in zip(*results))


def solution(mesh):
    both = ("wide", "narrow")
    return jax.shard_map(
        local,
        mesh=mesh,
        in_specs=(P(both, None, None), P(both), P(both), P(both)) + (P(),) * 17,
        out_specs=(
            P(None, both, None, None),
            P(None, both, None),
            P(),
            P(),
            P(),
            P(),
            P(),
            P(None, both, None),
        ),
        check_vma=False,
    )
```

```python
import functools
import math

import jax
import jax.numpy as jnp
from jax import lax
from jax.experimental import pallas as pl
from jax.experimental.pallas import tpu as pltpu
from jax.sharding import PartitionSpec as P

HEAD = 64
LEAD = 128
MESH = pl.DeviceIdType.MESH
epsilon = 1e-12
bf16 = jnp.bfloat16
f32 = jnp.float32
SCALE = HEAD**-0.5 * math.log2(math.e)
SUM_LOW = 2.0**-60
SUM_HIGH = 2.0**100


def split(values):
    high = values.astype(bf16)
    return high, (values - high.astype(f32)).astype(bf16)


def gelu(values):
    return (0.5 * values) * (1.0 + lax.erf(values * math.sqrt(0.5)))


def norm_rows(values, gain, shift):
    center = values - jnp.mean(values, -1, keepdims=True)
    spread = jnp.mean(center * center, -1, keepdims=True)
    return center * lax.rsqrt(spread + epsilon) * gain + shift


def blocks_kernel(
    order,
    lens,
    labels,
    hidden,
    w_qkv,
    w_out,
    w_in,
    w_back,
    b_query,
    b_value,
    b_out,
    ln1_gain,
    ln1_bias,
    b_in,
    b_back,
    ln2_gain,
    ln2_bias,
    states,
    context,
    packet,
    x_bufs,
    last_buf,
    qkv_buf,
    out_buf,
    in_buf,
    back_buf,
    turned,
    columns,
    q_buf,
    k_buf,
    v_buf,
    p_buf,
    ct_buf,
    c_buf,
    m_buf,
    mb_buf,
    y_buf,
    h_buf,
    fine,
    w_sem,
    x_sem,
    o_sem,
    c_sem,
):
    depth, width = b_query.shape
    slots, length = x_bufs[0].shape[:2]
    heads = width // HEAD
    hidden_units = b_in.shape[1]
    lead = last_buf.shape[0] // slots
    tile = length // 2
    spans = [slice(t * tile, (t + 1) * tile) for t in range(2)]

    def fetch_x(s):
        return pltpu.make_async_copy(hidden.at[order[s]], x_bufs[0].at[s], x_sem.at[s])

    def fetch_qkv(l, part):
        cols = pl.ds(part * width, width)
        return pltpu.make_async_copy(
            w_qkv.at[l, :, cols], qkv_buf.at[l, :, cols], w_sem.at[l, part]
        )

    def fetch_rest(l, number):
        source = (w_out, w_in, w_back)[number]
        target = (out_buf, in_buf, back_buf)[number]
        return pltpu.make_async_copy(source.at[l], target.at[l], w_sem.at[l, 3 + number])

    def put_states(l, s):
        return pltpu.make_async_copy(x_bufs[l + 1].at[s], states.at[l, s], o_sem.at[l, s])

    def put_last(s):
        return pltpu.make_async_copy(
            last_buf.at[pl.ds(s * lead, lead)],
            states.at[depth - 1, s, pl.ds(0, lead)],
            o_sem.at[depth - 1, s],
        )

    def put_context(s):
        rows = pl.ds(lead, length - lead)
        return pltpu.make_async_copy(c_buf.at[s, rows], context.at[s, rows], c_sem.at[s])

    fetch_qkv(0, 0).start()
    fetch_qkv(0, 2).start()
    fetch_x(0).start()
    fetch_qkv(0, 1).start()

    q_buf[...] = jnp.zeros_like(q_buf)
    for l in range(depth):
        for number, bias in enumerate((b_query, b_value)):
            for j in range(width // 128):
                offset = number * width + j * 128
                columns[l, offset : offset + 128] = jnp.broadcast_to(
                    bias[l : l + 1, j * 128 : (j + 1) * 128], (128, 128)
                ).T

    def turn(l, block):
        skip = jnp.where(block >= width // 128, width, 0)
        lanes = pl.ds(pl.multiple_of(block * 128 + skip, 128), 128)
        rows = pl.ds(pl.multiple_of(block * 128, 128), 128)
        turned[rows] = qkv_buf[l, :, lanes].T

    def project(l, s):
        rows = x_bufs[l][s]
        k_buf[...] = jnp.dot(
            rows, qkv_buf[l, :, width : 2 * width], preferred_element_type=f32
        ).astype(bf16)
        count = lens[order[s]]
        seen = (
            lax.broadcasted_iota(jnp.int32, (HEAD, length), 1) < count
        ).astype(f32)
        joined = lax.dot_general(
            turned[...], rows, (((1,), (1,)), ((), ())), preferred_element_type=f32
        )
        for h in range(heads):
            at = slice(h * HEAD, (h + 1) * HEAD)
            half = slice((h % 2) * HEAD, (h % 2 + 1) * HEAD)
            q_buf[h, half] = (
                joined[at] + jnp.tile(columns[l, at, :], (1, length // 128))
            ).astype(bf16)
            av = slice(width + h * HEAD, width + (h + 1) * HEAD)
            v_buf[h, :HEAD] = (
                (joined[av] + jnp.tile(columns[l, av, :], (1, length // 128))) * seen
            ).astype(bf16)
            v_buf[h, HEAD:] = seen.astype(bf16)

    def attend(s):
        def score(h):
            pair = slice((h // 2) * 128, (h // 2 + 1) * 128)
            scores = jnp.dot(k_buf[:, pair], q_buf[h], preferred_element_type=f32)
            p_buf[h % 4] = jnp.exp2(scores * SCALE).astype(bf16)

        def mix(h):
            both = jnp.dot(v_buf[h], p_buf[h % 4], preferred_element_type=f32)
            sums = both[HEAD:]
            good = (sums[:8] >= SUM_LOW) & (sums[:8] <= SUM_HIGH)
            fine[...] = jnp.where(good, fine[...], 0.0)
            half = slice((h % 2) * HEAD, (h % 2 + 1) * HEAD)
            ct_buf[(h // 2) % 2, half] = (both[:HEAD] * (1.0 / sums)).astype(bf16)
            if h % 2 == 1:
                pair = slice((h // 2) * 128, (h // 2 + 1) * 128)
                c_buf[s, :, pair] = ct_buf[(h // 2) % 2].T

        score(0)
        for h in range(heads):
            if h + 1 < heads:
                score(h + 1)
            mix(h)

    def attend_shifted(s):
        count = lens[order[s]]

        def pair_step(number, carry):
            lanes = pl.ds(pl.multiple_of(number * 128, 128), 128)
            for side in range(2):
                h = number * 2 + side
                scores = (
                    jnp.dot(k_buf[:, lanes], q_buf[h], preferred_element_type=f32) * SCALE
                )
                seen = lax.broadcasted_iota(jnp.int32, scores.shape, 0) < count
                scores = jnp.where(seen, scores, -1e30)
                highest = jnp.max(scores, 0, keepdims=True)
                p_buf[side] = jnp.exp2(scores - highest).astype(bf16)
                both = jnp.dot(v_buf[h], p_buf[side], preferred_element_type=f32)
                ct_buf[0, side * HEAD : (side + 1) * HEAD] = (
                    both[:HEAD] / both[HEAD:]
                ).astype(bf16)
            c_buf[s, :, lanes] = ct_buf[0].T
            return carry

        lax.fori_loop(0, heads // 2, pair_step, 0)

    def front(l):
        fine[...] = jnp.ones_like(fine)

        def step(s, carry):
            if l == 0:
                fetch_x(s).wait()
            project(l, s)
            attend(s)
            return carry

        lax.fori_loop(0, slots, step, 0)

        @pl.when(jnp.min(fine[...]) < 0.5)
        def _():
            def again(s, carry):
                project(l, s)
                attend_shifted(s)
                return carry

            lax.fori_loop(0, slots, again, 0)

    def join(l, slot, contexts, inputs):
        attended = jnp.dot(contexts, out_buf[l], preferred_element_type=f32)
        values = inputs.astype(f32) + (attended + b_out[l : l + 1])
        middle = norm_rows(values, ln1_gain[l : l + 1], ln1_bias[l : l + 1])
        size = middle.shape[0]
        m_buf[slot, :size] = middle
        mb_buf[slot, :size] = middle.astype(bf16)

    def expand(l, slot, size=tile):
        chunk = 512
        for j in range(hidden_units // chunk):
            units = slice(j * chunk, (j + 1) * chunk)
            inner = jnp.dot(mb_buf[slot, :size], in_buf[l, :, units], preferred_element_type=f32)
            h_buf[slot, :size, units] = gelu(inner + b_in[l : l + 1, units]).astype(bf16)

    def contract(l, slot, size=tile):
        back = jnp.dot(h_buf[slot, :size], back_buf[l], preferred_element_type=f32)
        y_buf[slot, :size] = m_buf[slot, :size] + back + b_back[l : l + 1]

    def settle(l, slot, size=tile):
        return norm_rows(y_buf[slot, :size], ln2_gain[l : l + 1], ln2_bias[l : l + 1]).astype(bf16)

    def rear(l):
        def enter(s, half):
            join(l, half, c_buf[s, spans[half]], x_bufs[l][s, spans[half]])

        enter(0, 0)

        def step(s, carry):
            x_bufs[l + 1][jnp.maximum(s - 1, 0), spans[1]] = settle(l, 1)
            expand(l, 0)
            enter(s, 1)
            contract(l, 0)
            x_bufs[l + 1][s, spans[0]] = settle(l, 0)
            expand(l, 1)
            enter(jnp.minimum(s + 1, slots - 1), 0)
            contract(l, 1)
            blocks = 2 * width // 128 // slots
            for number in range(blocks):
                turn(l + 1, s * blocks + number)

            @pl.when(s > 0)
            def _():
                put_states(l, s - 1).start()

            return carry

        lax.fori_loop(0, slots, step, 0)
        x_bufs[l + 1][slots - 1, spans[1]] = settle(l, 1)
        put_states(l, slots - 1).start()

    def rear_lead(l):
        half = slots * lead // 2
        contexts = jnp.concatenate([c_buf[s, :lead] for s in range(slots)])
        inputs = jnp.concatenate([x_bufs[l][s, :lead] for s in range(slots)])
        for t in range(2):
            rows = slice(t * half, (t + 1) * half)
            join(l, t, contexts[rows], inputs[rows])
        for t in range(2):
            expand(l, t, half)
        for t in range(2):
            contract(l, t, half)
        for t in range(2):
            last_buf[t * half : (t + 1) * half] = settle(l, t, half)
        for s in range(slots):
            put_last(s).start()

    for l in range(depth):
        last = l == depth - 1
        if l == 0:
            for part in (0, 2):
                fetch_qkv(l, part).wait()
                for j in range(width // 128):
                    turn(l, part // 2 * (width // 128) + j)
            fetch_qkv(l, 1).wait()
            for s in range(1, slots):
                fetch_x(s).start()
        for number in range(3):
            fetch_rest(l, number).start()
        if not last:
            for part in range(3):
                fetch_qkv(l + 1, part).start()
        front(l)
        if last:
            for s in range(slots):
                put_context(s).start()
        for number in range(3):
            fetch_rest(l, number).wait()
        if last:
            rear_lead(l)
        else:
            for part in range(3):
                fetch_qkv(l + 1, part).wait()
            rear(l)
    lane = lax.broadcasted_iota(jnp.int32, packet.shape, 1)
    place = lax.broadcasted_iota(jnp.int32, packet.shape, 0)
    marks = jnp.zeros(packet.shape, f32)
    for s in range(slots):
        marks = jnp.where(lane == s, labels[order[s]].astype(f32), marks)
    packet[...] = jnp.where(place == slots, marks, 0.0)
    for l in range(depth):
        for s in range(slots):
            row = l * (slots + 1) + s
            if l < depth - 1:
                packet[row : row + 1] = x_bufs[l + 1][s, 0:1].astype(f32)
                put_states(l, s).wait()
            else:
                packet[row : row + 1] = last_buf[s * lead : s * lead + 1].astype(f32)
                put_last(s).wait()
                put_context(s).wait()


def run_blocks(hidden, lengths, slot_order, labels, stacks):
    (
        w_qkv,
        b_query,
        b_value,
        w_out,
        b_out,
        ln1_gain,
        ln1_bias,
        w_in,
        b_in,
        w_back,
        b_back,
        ln2_gain,
        ln2_bias,
    ) = stacks
    slots, length, width = hidden.shape
    depth = w_qkv.shape[0]
    units = w_in.shape[2]
    heads = width // HEAD
    tile = length // 2
    place_hbm = pl.BlockSpec(memory_space=pl.ANY)
    place_smem = pl.BlockSpec(memory_space=pltpu.SMEM)
    place_vmem = pl.BlockSpec(memory_space=pltpu.VMEM)
    return pl.pallas_call(
        blocks_kernel,
        name="blocks",
        out_shape=(
            jax.ShapeDtypeStruct((depth, slots, length, width), bf16),
            jax.ShapeDtypeStruct((slots, length, width), bf16),
            jax.ShapeDtypeStruct((depth * (slots + 1), width), f32),
        ),
        in_specs=[place_smem] * 3 + [place_hbm] * 5 + [place_vmem] * 9,
        out_specs=(place_hbm, place_hbm, place_vmem),
        scratch_shapes=[
            [pltpu.VMEM((slots, length, width), bf16) for _ in range(depth)],
            pltpu.VMEM((slots * LEAD, width), bf16),
            pltpu.VMEM((depth, width, 3 * width), bf16),
            pltpu.VMEM((depth, width, width), bf16),
            pltpu.VMEM((depth, width, units), bf16),
            pltpu.VMEM((depth, units, width), bf16),
            pltpu.VMEM((2 * width, width), bf16),
            pltpu.VMEM((depth, 2 * width, 128), f32),
            pltpu.VMEM((heads, 2 * HEAD, length), bf16),
            pltpu.VMEM((length, width), bf16),
            pltpu.VMEM((heads, 2 * HEAD, length), bf16),
            pltpu.VMEM((4, length, length), bf16),
            pltpu.VMEM((2, 2 * HEAD, length), bf16),
            pltpu.VMEM((slots, length, width), bf16),
            pltpu.VMEM((2, tile, width), f32),
            pltpu.VMEM((2, tile, width), bf16),
            pltpu.VMEM((2, tile, width), f32),
            pltpu.VMEM((2, tile, units), bf16),
            pltpu.VMEM((8, length), f32),
            pltpu.SemaphoreType.DMA((depth, 6)),
            pltpu.SemaphoreType.DMA((slots,)),
            pltpu.SemaphoreType.DMA((depth, slots)),
            pltpu.SemaphoreType.DMA((slots,)),
        ],
        compiler_params=pltpu.CompilerParams(vmem_limit_bytes=62 * 1024 * 1024),
    )(
        slot_order,
        lengths,
        labels,
        hidden,
        w_qkv,
        w_out,
        w_in,
        w_back,
        b_query,
        b_value,
        b_out,
        ln1_gain,
        ln1_bias,
        b_in,
        b_back,
        ln2_gain,
        ln2_bias,
    )


def finish_kernel(
    packet,
    states,
    context,
    w_out,
    w_in,
    w_back,
    b_out,
    ln1_gain,
    ln1_bias,
    b_in,
    b_back,
    ln2_gain,
    ln2_bias,
    gathered,
    rest,
    x_buf,
    c_buf,
    out_buf,
    in_buf,
    back_buf,
    m_buf,
    mb_buf,
    y_buf,
    h_buf,
    t_sem,
    w_sem,
    o_sem,
    near_send,
    near_recv,
    far_send,
    far_recv,
):
    groups, lines = gathered.shape[:2]
    group, line = lax.axis_index("wide"), lax.axis_index("narrow")
    depth, slots = states.shape[:2]
    rows, width = x_buf.shape[1:]
    hidden_units = b_in.shape[1]
    chunk = 512
    chunks = hidden_units // chunk
    l = depth - 1
    lead = pl.ds(LEAD, rows)

    def near(step):
        return (group, lax.rem(line + step, lines))

    def far(step):
        return (lax.rem(group + step, groups), line)

    def near_copy(step):
        return pltpu.make_async_remote_copy(
            src_ref=packet,
            dst_ref=gathered.at[group, line],
            send_sem=near_send,
            recv_sem=near_recv,
            device_id=near(step),
            device_id_type=MESH,
        )

    def far_copy(step):
        return pltpu.make_async_remote_copy(
            src_ref=gathered.at[group],
            dst_ref=gathered.at[group],
            send_sem=far_send,
            recv_sem=far_recv,
            device_id=far(step),
            device_id_type=MESH,
        )

    def near_all():
        return pltpu.make_async_remote_copy(
            src_ref=gathered.at[0, pl.ds(0, lines - 1)],
            dst_ref=gathered.at[0, pl.ds(0, lines - 1)],
            send_sem=near_send,
            recv_sem=near_recv,
            device_id=near(1),
            device_id_type=MESH,
        )

    def far_all():
        return pltpu.make_async_remote_copy(
            src_ref=gathered.at[pl.ds(0, groups - 1)],
            dst_ref=gathered.at[pl.ds(0, groups - 1)],
            send_sem=far_send,
            recv_sem=far_recv,
            device_id=far(1),
            device_id_type=MESH,
        )

    def begin(copy):
        def body(step, carry):
            copy(step).start()
            return carry

        return body

    def greet(place):
        def body(step, carry):
            pl.semaphore_signal(barrier, inc=1, device_id=place(step), device_id_type=MESH)
            return carry

        return body

    def fetch_tile(s):
        return (
            pltpu.make_async_copy(context.at[s, lead], c_buf.at[s], t_sem.at[0, s]),
            pltpu.make_async_copy(states.at[l - 1, s, lead], x_buf.at[s], t_sem.at[1, s]),
        )

    def fetch_out():
        return pltpu.make_async_copy(w_out.at[l], out_buf, w_sem.at[0])

    def fetch_in(j):
        units = pl.ds(j * chunk, chunk)
        return pltpu.make_async_copy(
            w_in.at[l, :, units], in_buf.at[:, units], w_sem.at[1 + j]
        )

    def fetch_back(j):
        units = pl.ds(j * chunk, chunk)
        return pltpu.make_async_copy(
            w_back.at[l, units], back_buf.at[units], w_sem.at[1 + chunks + j]
        )

    def put_rest(s):
        return pltpu.make_async_copy(x_buf.at[s], rest.at[s], o_sem.at[s])

    barrier = pltpu.get_barrier_semaphore()
    lax.fori_loop(1, lines, greet(near), 0)
    lax.fori_loop(1, groups, greet(far), 0)
    queue = [*fetch_tile(0), fetch_out()]
    queue += [fetch_in(j) for j in range(chunks)]
    queue += [fetch_back(j) for j in range(chunks)]
    for s in range(1, slots):
        queue += fetch_tile(s)
    queue.reverse()

    def advance(number):
        for _ in range(min(number, len(queue))):
            queue.pop().start()

    advance(6)

    half = rows // 2
    spans = [slice(t * half, (t + 1) * half) for t in range(2)]

    def join(s):
        for span in spans:
            attended = jnp.dot(c_buf[s, span], out_buf[...], preferred_element_type=f32)
            values = x_buf[s, span].astype(f32) + (attended + b_out[l : l + 1])
            middle = norm_rows(values, ln1_gain[l : l + 1], ln1_bias[l : l + 1])
            m_buf[s % 2, span] = middle
            mb_buf[s % 2, span] = middle.astype(bf16)

    def expand(s, j):
        units = slice(j * chunk, (j + 1) * chunk)
        inner = jnp.dot(mb_buf[s % 2], in_buf[:, units], preferred_element_type=f32)
        h_buf[:, units] = gelu(inner + b_in[l : l + 1, units]).astype(bf16)

    def contract(s):
        for span in spans:
            back = jnp.dot(h_buf[span], back_buf[...], preferred_element_type=f32)
            y_buf[span] = m_buf[s % 2, span] + back + b_back[l : l + 1]

    def settle(s):
        x_buf[s] = norm_rows(y_buf[...], ln2_gain[l : l + 1], ln2_bias[l : l + 1]).astype(bf16)

    for copy in fetch_tile(0):
        copy.wait()
    fetch_out().wait()
    advance(3)
    join(0)
    pl.semaphore_wait(barrier, lines + groups - 2)
    lax.fori_loop(1, lines, begin(near_copy), 0)
    gathered[group, line] = packet[...]
    for j in range(chunks):
        fetch_in(j).wait()
        advance(2)
        expand(0, j)
    near_all().wait()
    lax.fori_loop(1, groups, begin(far_copy), 0)
    advance(len(queue))
    for j in range(chunks):
        fetch_back(j).wait()
    for s in range(1, slots):
        for copy in fetch_tile(s):
            copy.wait()
    for s in range(slots):
        if s > 0:
            settle(s - 1)
            for j in range(chunks):
                expand(s, j)
        if s + 1 < slots:
            join(s + 1)
        contract(s)
        if s > 0:
            put_rest(s - 1).start()
    settle(slots - 1)
    put_rest(slots - 1).start()
    far_all().wait()
    for s in range(slots):
        put_rest(s).wait()


def run_finish(packet, states, context, stacks):
    (_, _, _, w_out, b_out, ln1_gain, ln1_bias, w_in, b_in, w_back, b_back, ln2_gain, ln2_bias) = (
        stacks
    )
    groups, lines = lax.axis_size("wide"), lax.axis_size("narrow")
    slots, length, width = context.shape
    units = w_in.shape[2]
    rows = length - LEAD
    place_hbm = pl.BlockSpec(memory_space=pl.ANY)
    place_vmem = pl.BlockSpec(memory_space=pltpu.VMEM)
    return pl.pallas_call(
        finish_kernel,
        name="finish",
        out_shape=(
            jax.ShapeDtypeStruct((groups, lines) + packet.shape, f32),
            jax.ShapeDtypeStruct((slots, rows, width), bf16),
        ),
        in_specs=[place_vmem] + [place_hbm] * 5 + [place_vmem] * 7,
        out_specs=(place_vmem, place_hbm),
        scratch_shapes=[
            pltpu.VMEM((slots, rows, width), bf16),
            pltpu.VMEM((slots, rows, width), bf16),
            pltpu.VMEM((width, width), bf16),
            pltpu.VMEM((width, units), bf16),
            pltpu.VMEM((units, width), bf16),
            pltpu.VMEM((2, rows, width), f32),
            pltpu.VMEM((2, rows, width), bf16),
            pltpu.VMEM((rows, width), f32),
            pltpu.VMEM((rows, units), bf16),
            pltpu.SemaphoreType.DMA((2, slots)),
            pltpu.SemaphoreType.DMA((1 + 2 * (units // 512),)),
            pltpu.SemaphoreType.DMA((slots,)),
        ]
        + [pltpu.SemaphoreType.DMA] * 4,
        compiler_params=pltpu.CompilerParams(
            collective_id=0,
            has_side_effects=True,
            vmem_limit_bytes=62 * 1024 * 1024,
        ),
    )(
        packet,
        states,
        context,
        w_out,
        w_in,
        w_back,
        b_out,
        ln1_gain,
        ln1_bias,
        b_in,
        b_back,
        ln2_gain,
        ln2_bias,
    )


def ramps_kernel(
    gathered,
    states_in,
    rest,
    pool_w,
    pool_b,
    cls_w,
    cls_b,
    states,
    logits,
    losses,
    grad_pool_w,
    grad_pool_b,
    grad_cls_w,
    grad_cls_b,
    first_grads,
    w_buf,
    g_buf,
    score_buf,
    inner_buf,
    rest_buf,
    w_sem,
    g_sem,
    s_sem,
):
    slots, depth, classes = logits.shape
    devices, packet, width = gathered.shape
    own = lax.axis_index("wide") * lax.axis_size("narrow") + lax.axis_index("narrow")

    def fetch(l):
        return pltpu.make_async_copy(pool_w.at[l], w_buf.at[l], w_sem.at[l])

    def put(l):
        return pltpu.make_async_copy(g_buf.at[l], grad_pool_w.at[l], g_sem.at[l])

    def fetch_rest():
        return pltpu.make_async_copy(rest, rest_buf, s_sem.at[slots])

    def put_rest(s):
        return pltpu.make_async_copy(
            rest_buf.at[s], states.at[depth - 1, s, pl.ds(LEAD, rest.shape[1])], s_sem.at[s]
        )

    for l in range(depth):
        fetch(l).start()
    fetch_rest().start()

    unit = slots + 1
    rows = devices * unit
    pairs = gathered[...].reshape(devices // 2, 2 * packet, width)
    even = pairs[:, :packet].reshape(rows, width)
    odd = pairs[:, packet:].reshape(rows, width)
    upper = lax.rem(lax.broadcasted_iota(jnp.int32, (rows, width), 0), packet) < unit
    firsts_all = (
        jnp.where(upper, even, pltpu.roll(odd, unit, 0)),
        jnp.where(upper, pltpu.roll(even, rows - unit, 0), odd),
    )
    place = lax.rem(lax.broadcasted_iota(jnp.int32, (rows, 128), 0), unit)
    marks = firsts_all[0][:, :128]
    spread = jnp.full((rows, 128), -1.0, f32)
    for s in range(slots):
        moved = pltpu.roll(marks, rows - (slots - s), 0)
        spread = jnp.where(place == s, moved[:, s : s + 1], spread)
    label_row = spread.T[:1]
    valid = (label_row >= 0).astype(f32)
    count = jnp.sum(valid)
    class_column = lax.broadcasted_iota(jnp.int32, (classes, rows), 0).astype(f32)
    onehot = (label_row == class_column).astype(f32)

    def mine(pair):
        return jnp.where(lax.rem(own, 2) == 0, pair[:slots], pair[unit : unit + slots])

    def dot(a, b):
        return jnp.dot(a, b, preferred_element_type=f32)

    def dot_turned(a, b):
        return lax.dot_general(a, b, (((1,), (1,)), ((), ())), preferred_element_type=f32)

    for l in range(depth):
        firsts = firsts_all[l]
        firsts_low = firsts.astype(bf16)
        firsts_turned = firsts.T.astype(bf16)
        fetch(l).wait()
        w_high, w_low = split(w_buf[l])
        pooled = jnp.tanh(dot(firsts_low, w_high) + dot(firsts_low, w_low) + pool_b[l : l + 1])
        pooled_high, pooled_low = split(pooled)
        cls = cls_w[:, l]
        cls_high, cls_low = split(cls)
        scores = (
            dot_turned(cls_high, pooled_high)
            + (dot_turned(cls_low, pooled_high) + dot_turned(cls_high, pooled_low))
            + cls_b[l : l + 1].T
        )
        highest = jnp.max(scores, 0, keepdims=True)
        raised = jnp.exp(scores - highest)
        totals = jnp.sum(raised, 0, keepdims=True)
        log_total = highest + jnp.log(totals)
        picked = jnp.sum(scores * onehot, 0, keepdims=True)
        losses[l] = jnp.sum(valid * (log_total - picked)) / count
        grad = valid * (raised / totals - onehot) / count
        score_buf[...] = scores.T.reshape(devices // 2, packet, classes)
        logits[:, l] = mine(score_buf[own // 2])
        grad_cls_b[l : l + 1] = jnp.sum(grad, 1, keepdims=True).T
        grad_column = grad.T
        inner = grad_column[:, 0:1] * cls[0:1]
        for c in range(1, classes):
            inner = inner + grad_column[:, c : c + 1] * cls[c : c + 1]
        inner = inner * (1.0 - pooled * pooled)
        inner_high, inner_low = split(inner)
        g_buf[l] = dot(firsts_turned, inner_high) + dot(firsts_turned, inner_low)
        put(l).start()
        grad_pool_b[l : l + 1] = jnp.sum(inner, 0, keepdims=True)
        grad_high, grad_low = split(grad)
        grad_cls_w[:, l] = dot(grad_high, pooled_high) + (
            dot(grad_low, pooled_high) + dot(grad_high, pooled_low)
        )
        inner_buf[...] = inner.reshape(devices // 2, packet, width)
        own_high, own_low = split(inner_buf[own // 2])
        own_grads = dot_turned(own_high, w_high) + (
            dot_turned(own_low, w_high) + dot_turned(own_high, w_low)
        )
        first_grads[:, l] = mine(own_grads)
        if l == 0:
            fetch_rest().wait()
            for s in range(slots):
                put_rest(s).start()
    for l in range(depth):
        put(l).wait()
    for s in range(slots):
        put_rest(s).wait()


def run_ramps(gathered, states, rest, pool_w, pool_b, cls_w, cls_b):
    devices, packet, width = gathered.shape
    depth, classes = cls_b.shape
    slots = rest.shape[0]
    pairs = devices // 2
    place_hbm = pl.BlockSpec(memory_space=pl.ANY)
    place_smem = pl.BlockSpec(memory_space=pltpu.SMEM)
    place_vmem = pl.BlockSpec(memory_space=pltpu.VMEM)
    states, logits, losses, pool_grad, pool_shift, cls_grad, cls_shift, first_grads = pl.pallas_call(
        ramps_kernel,
        name="ramps",
        out_shape=(
            jax.ShapeDtypeStruct(states.shape, states.dtype),
            jax.ShapeDtypeStruct((slots, depth, classes), f32),
            jax.ShapeDtypeStruct((depth,), f32),
            jax.ShapeDtypeStruct((depth, width, width), f32),
            jax.ShapeDtypeStruct((depth, width), f32),
            jax.ShapeDtypeStruct((classes, depth, width), f32),
            jax.ShapeDtypeStruct((depth, classes), f32),
            jax.ShapeDtypeStruct((slots, depth, width), f32),
        ),
        in_specs=[place_vmem] + [place_hbm] * 3 + [place_vmem] * 3,
        out_specs=(place_hbm, place_vmem, place_smem, place_hbm) + (place_vmem,) * 4,
        input_output_aliases={1: 0},
        scratch_shapes=[
            pltpu.VMEM((depth, width, width), f32),
            pltpu.VMEM((depth, width, width), f32),
            pltpu.VMEM((pairs, packet, classes), f32),
            pltpu.VMEM((pairs, packet, width), f32),
            pltpu.VMEM(rest.shape, bf16),
            pltpu.SemaphoreType.DMA((depth,)),
            pltpu.SemaphoreType.DMA((depth,)),
            pltpu.SemaphoreType.DMA((slots + 1,)),
        ],
        compiler_params=pltpu.CompilerParams(vmem_limit_bytes=62 * 1024 * 1024),
    )(gathered, states, rest, pool_w, pool_b, jnp.transpose(cls_w, (2, 0, 1)), cls_b)
    return (
        states,
        jnp.transpose(logits, (1, 0, 2)),
        losses,
        pool_grad,
        pool_shift,
        jnp.transpose(cls_grad, (1, 2, 0)),
        cls_shift,
        jnp.transpose(first_grads, (1, 0, 2)),
    )


def local(
    hidden,
    lengths,
    slot_order,
    labels,
    w_qkv,
    b_query,
    b_value,
    w_out,
    b_out,
    ln1_gain,
    ln1_bias,
    w_in,
    b_in,
    w_back,
    b_back,
    ln2_gain,
    ln2_bias,
    pool_w,
    pool_b,
    cls_w,
    cls_b,
):
    stacks = (
        w_qkv,
        b_query,
        b_value,
        w_out,
        b_out,
        ln1_gain,
        ln1_bias,
        w_in,
        b_in,
        w_back,
        b_back,
        ln2_gain,
        ln2_bias,
    )
    states, context, packet = run_blocks(hidden, lengths, slot_order, labels, stacks)
    gathered, rest = run_finish(packet, states, context, stacks)
    gathered = gathered.reshape((-1,) + packet.shape)
    return run_ramps(gathered, states, rest, pool_w, pool_b, cls_w, cls_b)


def solution(mesh):
    both = ("wide", "narrow")
    return jax.shard_map(
        local,
        mesh=mesh,
        in_specs=(P(both, None, None), P(both), P(both), P(both)) + (P(),) * 17,
        out_specs=(
            P(None, both, None, None),
            P(None, both, None),
            P(),
            P(),
            P(),
            P(),
            P(),
            P(None, both, None),
        ),
        check_vma=False,
    )
```

```python
import functools
import math

import jax
import jax.numpy as jnp
from jax import lax
from jax.experimental import pallas as pl
from jax.experimental.pallas import tpu as pltpu
from jax.sharding import PartitionSpec as P

HEAD = 64
LEAD = 128
MESH = pl.DeviceIdType.MESH
epsilon = 1e-12
bf16 = jnp.bfloat16
f32 = jnp.float32
SCALE = HEAD**-0.5 * math.log2(math.e)
SUM_LOW = 2.0**-60
SUM_HIGH = 2.0**100


def split(values):
    high = values.astype(bf16)
    return high, (values - high.astype(f32)).astype(bf16)


def gelu(values):
    return (0.5 * values) * (1.0 + lax.erf(values * math.sqrt(0.5)))


def norm_rows(values, gain, shift):
    center = values - jnp.mean(values, -1, keepdims=True)
    spread = jnp.mean(center * center, -1, keepdims=True)
    return center * lax.rsqrt(spread + epsilon) * gain + shift


def blocks_kernel(
    order,
    lens,
    labels,
    hidden,
    w_qkv,
    w_out,
    w_in,
    w_back,
    b_query,
    b_value,
    b_out,
    ln1_gain,
    ln1_bias,
    b_in,
    b_back,
    ln2_gain,
    ln2_bias,
    states,
    context,
    packet,
    x_bufs,
    last_buf,
    qkv_buf,
    out_buf,
    in_buf,
    back_buf,
    turned,
    columns,
    q_buf,
    k_buf,
    v_buf,
    p_buf,
    ct_buf,
    c_buf,
    m_buf,
    mb_buf,
    y_buf,
    h_buf,
    fine,
    vec_bufs,
    packet_buf,
    order_buf,
    lens_buf,
    labels_buf,
    w_sem,
    x_sem,
    o_sem,
    c_sem,
    v_sem,
):
    depth, width = b_query.shape
    slots, length = x_bufs[0].shape[:2]
    heads = width // HEAD
    hidden_units = b_in.shape[1]
    lead = last_buf.shape[0] // slots
    tile = length // 2
    spans = [slice(t * tile, (t + 1) * tile) for t in range(2)]

    def fetch_x(s):
        return pltpu.make_async_copy(hidden.at[order[s]], x_bufs[0].at[s], x_sem.at[s])

    def fetch_qkv(l, part):
        cols = pl.ds(part * width, width)
        return pltpu.make_async_copy(
            w_qkv.at[l, :, cols], qkv_buf.at[l, :, cols], w_sem.at[l, part]
        )

    def fetch_rest(l, number):
        source = (w_out, w_in, w_back)[number]
        target = (out_buf, in_buf, back_buf)[number]
        return pltpu.make_async_copy(source.at[l], target.at[l], w_sem.at[l, 3 + number])

    def put_states(l, s):
        return pltpu.make_async_copy(x_bufs[l + 1].at[s], states.at[l, s], o_sem.at[l, s])

    def put_last(s):
        return pltpu.make_async_copy(
            last_buf.at[pl.ds(s * lead, lead)],
            states.at[depth - 1, s, pl.ds(0, lead)],
            o_sem.at[depth - 1, s],
        )

    def put_context(s):
        rows = pl.ds(lead, length - lead)
        return pltpu.make_async_copy(c_buf.at[s, rows], context.at[s, rows], c_sem.at[s])

    vectors = (b_query, b_value, b_out, ln1_gain, ln1_bias, b_in, b_back, ln2_gain, ln2_bias)
    scalars = ((order, order_buf), (lens, lens_buf), (labels, labels_buf))
    small = [
        pltpu.make_async_copy(source, target, v_sem.at[number])
        for number, (source, target) in enumerate((*scalars, *zip(vectors, vec_bufs)))
    ]
    put_packet = pltpu.make_async_copy(packet_buf, packet, v_sem.at[0])
    order, lens, labels = order_buf, lens_buf, labels_buf
    b_query, b_value, b_out, ln1_gain, ln1_bias, b_in, b_back, ln2_gain, ln2_bias = vec_bufs
    for copy in small[:5]:
        copy.start()
    fetch_qkv(0, 0).start()
    fetch_qkv(0, 2).start()
    fetch_qkv(0, 1).start()
    for copy in small[5:]:
        copy.start()
    q_buf[...] = jnp.zeros_like(q_buf)
    for copy in small:
        copy.wait()
    fetch_x(0).start()

    for l in range(depth):
        for number, bias in enumerate((b_query, b_value)):
            for j in range(width // 128):
                offset = number * width + j * 128
                columns[l, offset : offset + 128] = jnp.broadcast_to(
                    bias[l : l + 1, j * 128 : (j + 1) * 128], (128, 128)
                ).T

    def turn(l, block):
        skip = jnp.where(block >= width // 128, width, 0)
        lanes = pl.ds(pl.multiple_of(block * 128 + skip, 128), 128)
        rows = pl.ds(pl.multiple_of(block * 128, 128), 128)
        turned[rows] = qkv_buf[l, :, lanes].T

    def project(l, s):
        rows = x_bufs[l][s]
        k_buf[...] = jnp.dot(
            rows, qkv_buf[l, :, width : 2 * width], preferred_element_type=f32
        ).astype(bf16)
        count = lens[order[s]]
        seen = (
            lax.broadcasted_iota(jnp.int32, (HEAD, length), 1) < count
        ).astype(f32)
        joined = lax.dot_general(
            turned[...], rows, (((1,), (1,)), ((), ())), preferred_element_type=f32
        )
        for h in range(heads):
            at = slice(h * HEAD, (h + 1) * HEAD)
            half = slice((h % 2) * HEAD, (h % 2 + 1) * HEAD)
            q_buf[h, half] = (
                joined[at] + jnp.tile(columns[l, at, :], (1, length // 128))
            ).astype(bf16)
            av = slice(width + h * HEAD, width + (h + 1) * HEAD)
            v_buf[h, :HEAD] = (
                (joined[av] + jnp.tile(columns[l, av, :], (1, length // 128))) * seen
            ).astype(bf16)
            v_buf[h, HEAD:] = seen.astype(bf16)

    def attend(s):
        def score(h):
            pair = slice((h // 2) * 128, (h // 2 + 1) * 128)
            scores = jnp.dot(k_buf[:, pair], q_buf[h], preferred_element_type=f32)
            p_buf[h % 4] = jnp.exp2(scores * SCALE).astype(bf16)

        def mix(h):
            both = jnp.dot(v_buf[h], p_buf[h % 4], preferred_element_type=f32)
            sums = both[HEAD:]
            good = (sums[:8] >= SUM_LOW) & (sums[:8] <= SUM_HIGH)
            fine[...] = jnp.where(good, fine[...], 0.0)
            half = slice((h % 2) * HEAD, (h % 2 + 1) * HEAD)
            ct_buf[(h // 2) % 2, half] = (both[:HEAD] * (1.0 / sums)).astype(bf16)
            if h % 2 == 1:
                pair = slice((h // 2) * 128, (h // 2 + 1) * 128)
                c_buf[s, :, pair] = ct_buf[(h // 2) % 2].T

        score(0)
        for h in range(heads):
            if h + 1 < heads:
                score(h + 1)
            mix(h)

    def attend_shifted(s):
        count = lens[order[s]]

        def pair_step(number, carry):
            lanes = pl.ds(pl.multiple_of(number * 128, 128), 128)
            for side in range(2):
                h = number * 2 + side
                scores = (
                    jnp.dot(k_buf[:, lanes], q_buf[h], preferred_element_type=f32) * SCALE
                )
                seen = lax.broadcasted_iota(jnp.int32, scores.shape, 0) < count
                scores = jnp.where(seen, scores, -1e30)
                highest = jnp.max(scores, 0, keepdims=True)
                p_buf[side] = jnp.exp2(scores - highest).astype(bf16)
                both = jnp.dot(v_buf[h], p_buf[side], preferred_element_type=f32)
                ct_buf[0, side * HEAD : (side + 1) * HEAD] = (
                    both[:HEAD] / both[HEAD:]
                ).astype(bf16)
            c_buf[s, :, lanes] = ct_buf[0].T
            return carry

        lax.fori_loop(0, heads // 2, pair_step, 0)

    def front(l):
        fine[...] = jnp.ones_like(fine)

        def step(s, carry):
            if l == 0:
                fetch_x(s).wait()
            project(l, s)
            attend(s)
            return carry

        lax.fori_loop(0, slots, step, 0)

        @pl.when(jnp.min(fine[...]) < 0.5)
        def _():
            def again(s, carry):
                project(l, s)
                attend_shifted(s)
                return carry

            lax.fori_loop(0, slots, again, 0)

    def join(l, slot, contexts, inputs):
        attended = jnp.dot(contexts, out_buf[l], preferred_element_type=f32)
        values = inputs.astype(f32) + (attended + b_out[l : l + 1])
        middle = norm_rows(values, ln1_gain[l : l + 1], ln1_bias[l : l + 1])
        size = middle.shape[0]
        m_buf[slot, :size] = middle
        mb_buf[slot, :size] = middle.astype(bf16)

    def expand(l, slot, size=tile):
        chunk = 512
        for j in range(hidden_units // chunk):
            units = slice(j * chunk, (j + 1) * chunk)
            inner = jnp.dot(mb_buf[slot, :size], in_buf[l, :, units], preferred_element_type=f32)
            h_buf[slot, :size, units] = gelu(inner + b_in[l : l + 1, units]).astype(bf16)

    def contract(l, slot, size=tile):
        back = jnp.dot(h_buf[slot, :size], back_buf[l], preferred_element_type=f32)
        y_buf[slot, :size] = m_buf[slot, :size] + back + b_back[l : l + 1]

    def settle(l, slot, size=tile):
        return norm_rows(y_buf[slot, :size], ln2_gain[l : l + 1], ln2_bias[l : l + 1]).astype(bf16)

    def rear(l):
        def enter(s, half):
            join(l, half, c_buf[s, spans[half]], x_bufs[l][s, spans[half]])

        enter(0, 0)

        def step(s, carry):
            x_bufs[l + 1][jnp.maximum(s - 1, 0), spans[1]] = settle(l, 1)
            expand(l, 0)
            enter(s, 1)
            contract(l, 0)
            x_bufs[l + 1][s, spans[0]] = settle(l, 0)
            expand(l, 1)
            enter(jnp.minimum(s + 1, slots - 1), 0)
            contract(l, 1)
            blocks = 2 * width // 128 // slots
            for number in range(blocks):
                turn(l + 1, s * blocks + number)

            @pl.when(s > 0)
            def _():
                put_states(l, s - 1).start()

            return carry

        lax.fori_loop(0, slots, step, 0)
        x_bufs[l + 1][slots - 1, spans[1]] = settle(l, 1)
        put_states(l, slots - 1).start()

    def rear_lead(l):
        half = slots * lead // 2
        contexts = jnp.concatenate([c_buf[s, :lead] for s in range(slots)])
        inputs = jnp.concatenate([x_bufs[l][s, :lead] for s in range(slots)])
        for t in range(2):
            rows = slice(t * half, (t + 1) * half)
            join(l, t, contexts[rows], inputs[rows])
        for t in range(2):
            expand(l, t, half)
        for t in range(2):
            contract(l, t, half)
        for t in range(2):
            last_buf[t * half : (t + 1) * half] = settle(l, t, half)
        for s in range(slots):
            put_last(s).start()

    for l in range(depth):
        last = l == depth - 1
        if l == 0:
            for part in (0, 2):
                fetch_qkv(l, part).wait()
                for j in range(width // 128):
                    turn(l, part // 2 * (width // 128) + j)
            fetch_qkv(l, 1).wait()
            for s in range(1, slots):
                fetch_x(s).start()
        for number in range(3):
            fetch_rest(l, number).start()
        if not last:
            for part in range(3):
                fetch_qkv(l + 1, part).start()
        front(l)
        if last:
            for s in range(slots):
                put_context(s).start()
        for number in range(3):
            fetch_rest(l, number).wait()
        if last:
            rear_lead(l)
        else:
            for part in range(3):
                fetch_qkv(l + 1, part).wait()
            rear(l)
    lane = lax.broadcasted_iota(jnp.int32, packet.shape, 1)
    place = lax.broadcasted_iota(jnp.int32, packet.shape, 0)
    marks = jnp.zeros(packet.shape, f32)
    for s in range(slots):
        marks = jnp.where(lane == s, labels[order[s]].astype(f32), marks)
    packet_buf[...] = jnp.where(place == slots, marks, 0.0)
    for l in range(depth):
        for s in range(slots):
            row = l * (slots + 1) + s
            if l < depth - 1:
                packet_buf[row : row + 1] = x_bufs[l + 1][s, 0:1].astype(f32)
            else:
                packet_buf[row : row + 1] = last_buf[s * lead : s * lead + 1].astype(f32)
    put_packet.start()
    for s in range(slots):
        for l in range(depth - 1):
            put_states(l, s).wait()
        put_last(s).wait()
        put_context(s).wait()
    put_packet.wait()


def run_blocks(hidden, lengths, slot_order, labels, stacks):
    (
        w_qkv,
        b_query,
        b_value,
        w_out,
        b_out,
        ln1_gain,
        ln1_bias,
        w_in,
        b_in,
        w_back,
        b_back,
        ln2_gain,
        ln2_bias,
    ) = stacks
    slots, length, width = hidden.shape
    depth = w_qkv.shape[0]
    units = w_in.shape[2]
    heads = width // HEAD
    tile = length // 2
    vectors = (b_query, b_value, b_out, ln1_gain, ln1_bias, b_in, b_back, ln2_gain, ln2_bias)
    place_hbm = pl.BlockSpec(memory_space=pl.ANY)
    return pl.pallas_call(
        blocks_kernel,
        name="blocks",
        out_shape=(
            jax.ShapeDtypeStruct((depth, slots, length, width), bf16),
            jax.ShapeDtypeStruct((slots, length, width), bf16),
            jax.ShapeDtypeStruct((depth * (slots + 1), width), f32),
        ),
        in_specs=[place_hbm] * 17,
        out_specs=(place_hbm,) * 3,
        scratch_shapes=[
            [pltpu.VMEM((slots, length, width), bf16) for _ in range(depth)],
            pltpu.VMEM((slots * LEAD, width), bf16),
            pltpu.VMEM((depth, width, 3 * width), bf16),
            pltpu.VMEM((depth, width, width), bf16),
            pltpu.VMEM((depth, width, units), bf16),
            pltpu.VMEM((depth, units, width), bf16),
            pltpu.VMEM((2 * width, width), bf16),
            pltpu.VMEM((depth, 2 * width, 128), f32),
            pltpu.VMEM((heads, 2 * HEAD, length), bf16),
            pltpu.VMEM((length, width), bf16),
            pltpu.VMEM((heads, 2 * HEAD, length), bf16),
            pltpu.VMEM((4, length, length), bf16),
            pltpu.VMEM((2, 2 * HEAD, length), bf16),
            pltpu.VMEM((slots, length, width), bf16),
            pltpu.VMEM((2, tile, width), f32),
            pltpu.VMEM((2, tile, width), bf16),
            pltpu.VMEM((2, tile, width), f32),
            pltpu.VMEM((2, tile, units), bf16),
            pltpu.VMEM((8, length), f32),
            [pltpu.VMEM(vector.shape, f32) for vector in vectors],
            pltpu.VMEM((depth * (slots + 1), width), f32),
            pltpu.SMEM((slots,), jnp.int32),
            pltpu.SMEM((slots,), jnp.int32),
            pltpu.SMEM((slots,), jnp.int32),
            pltpu.SemaphoreType.DMA((depth, 6)),
            pltpu.SemaphoreType.DMA((slots,)),
            pltpu.SemaphoreType.DMA((depth, slots)),
            pltpu.SemaphoreType.DMA((slots,)),
            pltpu.SemaphoreType.DMA((3 + len(vectors),)),
        ],
        compiler_params=pltpu.CompilerParams(vmem_limit_bytes=62 * 1024 * 1024),
    )(
        slot_order,
        lengths,
        labels,
        hidden,
        w_qkv,
        w_out,
        w_in,
        w_back,
        *vectors,
    )


def finish_kernel(
    packet,
    states,
    context,
    w_out,
    w_in,
    w_back,
    b_out,
    ln1_gain,
    ln1_bias,
    b_in,
    b_back,
    ln2_gain,
    ln2_bias,
    gathered,
    rest,
    x_buf,
    c_buf,
    out_buf,
    in_buf,
    back_buf,
    m_buf,
    mb_buf,
    y_buf,
    h_buf,
    packet_buf,
    vec_bufs,
    t_sem,
    w_sem,
    o_sem,
    v_sem,
    keep_sem,
    near_send,
    near_recv,
    far_send,
    far_recv,
):
    groups, lines = gathered.shape[:2]
    group, line = lax.axis_index("wide"), lax.axis_index("narrow")
    depth, slots = states.shape[:2]
    rows, width = x_buf.shape[1:]
    hidden_units = b_in.shape[1]
    chunk = 512
    chunks = hidden_units // chunk
    l = depth - 1
    lead = pl.ds(LEAD, rows)

    def near(step):
        return (group, lax.rem(line + step, lines))

    def far(step):
        return (lax.rem(group + step, groups), line)

    def near_copy(step):
        return pltpu.make_async_remote_copy(
            src_ref=packet_buf,
            dst_ref=gathered.at[group, line],
            send_sem=near_send,
            recv_sem=near_recv,
            device_id=near(step),
            device_id_type=MESH,
        )

    def far_copy(step):
        return pltpu.make_async_remote_copy(
            src_ref=gathered.at[group],
            dst_ref=gathered.at[group],
            send_sem=far_send,
            recv_sem=far_recv,
            device_id=far(step),
            device_id_type=MESH,
        )

    def near_all():
        return pltpu.make_async_remote_copy(
            src_ref=gathered.at[0, pl.ds(0, lines - 1)],
            dst_ref=gathered.at[0, pl.ds(0, lines - 1)],
            send_sem=near_send,
            recv_sem=near_recv,
            device_id=near(1),
            device_id_type=MESH,
        )

    def far_all():
        return pltpu.make_async_remote_copy(
            src_ref=gathered.at[pl.ds(0, groups - 1)],
            dst_ref=gathered.at[pl.ds(0, groups - 1)],
            send_sem=far_send,
            recv_sem=far_recv,
            device_id=far(1),
            device_id_type=MESH,
        )

    def keep_own():
        return pltpu.make_async_copy(packet_buf, gathered.at[group, line], keep_sem)

    def begin(copy):
        def body(step, carry):
            copy(step).start()
            return carry

        return body

    def greet(place):
        def body(step, carry):
            pl.semaphore_signal(barrier, inc=1, device_id=place(step), device_id_type=MESH)
            return carry

        return body

    def fetch_tile(s):
        return (
            pltpu.make_async_copy(context.at[s, lead], c_buf.at[s], t_sem.at[0, s]),
            pltpu.make_async_copy(states.at[l - 1, s, lead], x_buf.at[s], t_sem.at[1, s]),
        )

    def fetch_out():
        return pltpu.make_async_copy(w_out.at[l], out_buf, w_sem.at[0])

    def fetch_in(j):
        units = pl.ds(j * chunk, chunk)
        return pltpu.make_async_copy(
            w_in.at[l, :, units], in_buf.at[:, units], w_sem.at[1 + j]
        )

    def fetch_back(j):
        units = pl.ds(j * chunk, chunk)
        return pltpu.make_async_copy(
            w_back.at[l, units], back_buf.at[units], w_sem.at[1 + chunks + j]
        )

    def put_rest(s):
        return pltpu.make_async_copy(x_buf.at[s], rest.at[s], o_sem.at[s])

    barrier = pltpu.get_barrier_semaphore()
    lax.fori_loop(1, lines, greet(near), 0)
    lax.fori_loop(1, groups, greet(far), 0)
    vectors = (b_out, ln1_gain, ln1_bias, b_in, b_back, ln2_gain, ln2_bias)
    small = [
        pltpu.make_async_copy(source, target, v_sem.at[number])
        for number, (source, target) in enumerate(
            ((packet, packet_buf), *zip(vectors, vec_bufs))
        )
    ]
    b_out, ln1_gain, ln1_bias, b_in, b_back, ln2_gain, ln2_bias = vec_bufs
    queue = [*fetch_tile(0), fetch_out()]
    queue += [fetch_in(j) for j in range(chunks)]
    queue += [fetch_back(j) for j in range(chunks)]
    for s in range(1, slots):
        queue += fetch_tile(s)
    queue.reverse()

    def advance(number):
        for _ in range(min(number, len(queue))):
            queue.pop().start()

    advance(3)
    for copy in small:
        copy.start()
    advance(4)

    half = rows // 2
    spans = [slice(t * half, (t + 1) * half) for t in range(2)]

    def join(s):
        for span in spans:
            attended = jnp.dot(c_buf[s, span], out_buf[...], preferred_element_type=f32)
            values = x_buf[s, span].astype(f32) + (attended + b_out[l : l + 1])
            middle = norm_rows(values, ln1_gain[l : l + 1], ln1_bias[l : l + 1])
            m_buf[s % 2, span] = middle
            mb_buf[s % 2, span] = middle.astype(bf16)

    def expand(s, j):
        units = slice(j * chunk, (j + 1) * chunk)
        inner = jnp.dot(mb_buf[s % 2], in_buf[:, units], preferred_element_type=f32)
        h_buf[:, units] = gelu(inner + b_in[l : l + 1, units]).astype(bf16)

    def contract(s):
        for span in spans:
            back = jnp.dot(h_buf[span], back_buf[...], preferred_element_type=f32)
            y_buf[span] = m_buf[s % 2, span] + back + b_back[l : l + 1]

    def settle(s):
        x_buf[s] = norm_rows(y_buf[...], ln2_gain[l : l + 1], ln2_bias[l : l + 1]).astype(bf16)

    for copy in fetch_tile(0):
        copy.wait()
    fetch_out().wait()
    for copy in small:
        copy.wait()
    advance(3)
    join(0)
    pl.semaphore_wait(barrier, lines + groups - 2)
    lax.fori_loop(1, lines, begin(near_copy), 0)
    keep_own().start()
    for j in range(chunks):
        fetch_in(j).wait()
        advance(2)
        expand(0, j)
    keep_own().wait()
    near_all().wait()
    lax.fori_loop(1, groups, begin(far_copy), 0)
    advance(len(queue))
    for j in range(chunks):
        fetch_back(j).wait()
    for s in range(1, slots):
        for copy in fetch_tile(s):
            copy.wait()
    for s in range(slots):
        if s > 0:
            settle(s - 1)
            for j in range(chunks):
                expand(s, j)
        if s + 1 < slots:
            join(s + 1)
        contract(s)
        if s > 0:
            put_rest(s - 1).start()
    settle(slots - 1)
    put_rest(slots - 1).start()
    far_all().wait()
    for s in range(slots):
        put_rest(s).wait()


def run_finish(packet, states, context, stacks):
    (_, _, _, w_out, b_out, ln1_gain, ln1_bias, w_in, b_in, w_back, b_back, ln2_gain, ln2_bias) = (
        stacks
    )
    groups, lines = lax.axis_size("wide"), lax.axis_size("narrow")
    slots, length, width = context.shape
    units = w_in.shape[2]
    rows = length - LEAD
    place_hbm = pl.BlockSpec(memory_space=pl.ANY)
    vectors = (b_out, ln1_gain, ln1_bias, b_in, b_back, ln2_gain, ln2_bias)
    return pl.pallas_call(
        finish_kernel,
        name="finish",
        out_shape=(
            jax.ShapeDtypeStruct((groups, lines) + packet.shape, f32),
            jax.ShapeDtypeStruct((slots, rows, width), bf16),
        ),
        in_specs=[place_hbm] * 13,
        out_specs=(place_hbm, place_hbm),
        scratch_shapes=[
            pltpu.VMEM((slots, rows, width), bf16),
            pltpu.VMEM((slots, rows, width), bf16),
            pltpu.VMEM((width, width), bf16),
            pltpu.VMEM((width, units), bf16),
            pltpu.VMEM((units, width), bf16),
            pltpu.VMEM((2, rows, width), f32),
            pltpu.VMEM((2, rows, width), bf16),
            pltpu.VMEM((rows, width), f32),
            pltpu.VMEM((rows, units), bf16),
            pltpu.VMEM(packet.shape, f32),
            [pltpu.VMEM(vector.shape, f32) for vector in vectors],
            pltpu.SemaphoreType.DMA((2, slots)),
            pltpu.SemaphoreType.DMA((1 + 2 * (units // 512),)),
            pltpu.SemaphoreType.DMA((slots,)),
            pltpu.SemaphoreType.DMA((1 + len(vectors),)),
        ]
        + [pltpu.SemaphoreType.DMA] * 5,
        compiler_params=pltpu.CompilerParams(
            collective_id=0,
            has_side_effects=True,
            vmem_limit_bytes=62 * 1024 * 1024,
        ),
    )(
        packet,
        states,
        context,
        w_out,
        w_in,
        w_back,
        *vectors,
    )


def ramps_kernel(
    gathered,
    states_in,
    rest,
    pool_w,
    pool_b,
    cls_w,
    cls_b,
    states,
    logits,
    losses,
    grad_pool_w,
    grad_pool_b,
    grad_cls_w,
    grad_cls_b,
    first_grads,
    all_buf,
    w_buf,
    g_buf,
    score_buf,
    inner_buf,
    rest_buf,
    in_bufs,
    out_bufs,
    w_sem,
    g_sem,
    s_sem,
    i_sem,
    r_sem,
):
    slots, depth, classes = logits.shape
    devices, packet, width = gathered.shape
    own = lax.axis_index("wide") * lax.axis_size("narrow") + lax.axis_index("narrow")

    def fetch(l):
        return pltpu.make_async_copy(pool_w.at[l], w_buf.at[l], w_sem.at[l])

    def put(l, t):
        span = pl.ds(t * 256, 256)
        return pltpu.make_async_copy(
            g_buf.at[l, span], grad_pool_w.at[l, span], g_sem.at[l, t]
        )

    def fetch_rest():
        return pltpu.make_async_copy(rest, rest_buf, s_sem.at[slots])

    def put_rest(s):
        return pltpu.make_async_copy(
            rest_buf.at[s], states.at[depth - 1, s, pl.ds(LEAD, rest.shape[1])], s_sem.at[s]
        )

    inputs = [
        pltpu.make_async_copy(source, target, i_sem.at[number])
        for number, (source, target) in enumerate(zip((pool_b, cls_w, cls_b), in_bufs))
    ]
    results = (logits, losses, grad_pool_b, grad_cls_w, grad_cls_b, first_grads)
    outputs = [
        pltpu.make_async_copy(source, target, r_sem.at[number])
        for number, (source, target) in enumerate(zip(out_bufs, results))
    ]
    pool_b, cls_w, cls_b = in_bufs
    logits, losses, grad_pool_b, grad_cls_w, grad_cls_b, first_grads = out_bufs
    gather_in = pltpu.make_async_copy(gathered, all_buf, s_sem.at[slots + 1])
    gather_in.start()
    for copy in inputs:
        copy.start()
    for l in range(depth):
        fetch(l).start()
    fetch_rest().start()
    gather_in.wait()
    for copy in inputs:
        copy.wait()

    unit = slots + 1
    rows = devices * unit
    pairs = all_buf[...].reshape(devices // 2, 2 * packet, width)
    even = pairs[:, :packet].reshape(rows, width)
    odd = pairs[:, packet:].reshape(rows, width)
    upper = lax.rem(lax.broadcasted_iota(jnp.int32, (rows, width), 0), packet) < unit
    firsts_all = (
        jnp.where(upper, even, pltpu.roll(odd, unit, 0)),
        jnp.where(upper, pltpu.roll(even, rows - unit, 0), odd),
    )
    place = lax.rem(lax.broadcasted_iota(jnp.int32, (rows, 128), 0), unit)
    marks = firsts_all[0][:, :128]
    spread = jnp.full((rows, 128), -1.0, f32)
    for s in range(slots):
        moved = pltpu.roll(marks, rows - (slots - s), 0)
        spread = jnp.where(place == s, moved[:, s : s + 1], spread)
    label_row = spread.T[:1]
    valid = (label_row >= 0).astype(f32)
    count = jnp.sum(valid)
    class_column = lax.broadcasted_iota(jnp.int32, (classes, rows), 0).astype(f32)
    onehot = (label_row == class_column).astype(f32)

    def mine(pair):
        return jnp.where(lax.rem(own, 2) == 0, pair[:slots], pair[unit : unit + slots])

    def dot(a, b):
        return jnp.dot(a, b, preferred_element_type=f32)

    def dot_turned(a, b):
        return lax.dot_general(a, b, (((1,), (1,)), ((), ())), preferred_element_type=f32)

    for l in range(depth):
        firsts_low = firsts_all[l].astype(bf16)
        firsts_turned = firsts_all[l].T.astype(bf16)
        cls = cls_w[:, l]
        cls_high, cls_low = split(cls)
        fetch(l).wait()
        weights, weights_low = split(w_buf[l])
        pooled = jnp.tanh(
            dot(firsts_low, weights) + dot(firsts_low, weights_low) + pool_b[l : l + 1]
        )
        pooled_high, pooled_low = split(pooled)
        scores = (
            dot_turned(cls_high, pooled_high)
            + (dot_turned(cls_low, pooled_high) + dot_turned(cls_high, pooled_low))
            + cls_b[l : l + 1].T
        )
        highest = jnp.max(scores, 0, keepdims=True)
        raised = jnp.exp(scores - highest)
        totals = jnp.sum(raised, 0, keepdims=True)
        grad = valid * (raised / totals - onehot) / count
        grad_column = grad.T
        inner = grad_column[:, 0:1] * cls[0:1]
        for c in range(1, classes):
            inner = inner + grad_column[:, c : c + 1] * cls[c : c + 1]
        inner = inner * (1.0 - pooled * pooled)
        inner_high, inner_low = split(inner)
        for t in range(width // 256):
            span = slice(t * 256, (t + 1) * 256)
            g_buf[l, span] = dot(firsts_turned[span], inner_high) + dot(
                firsts_turned[span], inner_low
            )
            put(l, t).start()
        grad_high, grad_low = split(grad)
        grad_cls_w[:, l] = dot(grad_high, pooled_high) + (
            dot(grad_low, pooled_high) + dot(grad_high, pooled_low)
        )
        inner_buf[...] = inner.reshape(devices // 2, packet, width)
        own_high, own_low = split(inner_buf[own // 2])
        own_grads = dot_turned(own_high, weights) + dot_turned(own_low, weights)
        first_grads[:, l] = mine(own_grads)
        grad_pool_b[l : l + 1] = jnp.sum(inner, 0, keepdims=True)
        grad_cls_b[l : l + 1] = jnp.sum(grad, 1, keepdims=True).T
        log_total = highest + jnp.log(totals)
        picked = jnp.sum(scores * onehot, 0, keepdims=True)
        losses[l] = jnp.sum(valid * (log_total - picked)) / count
        score_buf[...] = scores.T.reshape(devices // 2, packet, classes)
        logits[:, l] = mine(score_buf[own // 2])
        if l == 0:
            fetch_rest().wait()
            for s in range(slots):
                put_rest(s).start()
    for copy in outputs:
        copy.start()
    for l in range(depth):
        for t in range(width // 256):
            put(l, t).wait()
    for copy in outputs:
        copy.wait()
    for s in range(slots):
        put_rest(s).wait()


def run_ramps(gathered, states, rest, pool_w, pool_b, cls_w, cls_b):
    devices, packet, width = gathered.shape
    depth, classes = cls_b.shape
    slots = rest.shape[0]
    pairs = devices // 2
    place_hbm = pl.BlockSpec(memory_space=pl.ANY)
    cls_turned = jnp.transpose(cls_w, (2, 0, 1))
    states, logits, losses, pool_grad, pool_shift, cls_grad, cls_shift, first_grads = pl.pallas_call(
        ramps_kernel,
        name="ramps",
        out_shape=(
            jax.ShapeDtypeStruct(states.shape, states.dtype),
            jax.ShapeDtypeStruct((slots, depth, classes), f32),
            jax.ShapeDtypeStruct((depth,), f32),
            jax.ShapeDtypeStruct((depth, width, width), f32),
            jax.ShapeDtypeStruct((depth, width), f32),
            jax.ShapeDtypeStruct((classes, depth, width), f32),
            jax.ShapeDtypeStruct((depth, classes), f32),
            jax.ShapeDtypeStruct((slots, depth, width), f32),
        ),
        in_specs=[place_hbm] * 7,
        out_specs=(place_hbm,) * 8,
        input_output_aliases={1: 0},
        scratch_shapes=[
            pltpu.VMEM(gathered.shape, f32),
            pltpu.VMEM((depth, width, width), f32),
            pltpu.VMEM((depth, width, width), f32),
            pltpu.VMEM((pairs, packet, classes), f32),
            pltpu.VMEM((pairs, packet, width), f32),
            pltpu.VMEM(rest.shape, bf16),
            [pltpu.VMEM(member.shape, f32) for member in (pool_b, cls_turned, cls_b)],
            [
                pltpu.VMEM((slots, depth, classes), f32),
                pltpu.SMEM((depth,), f32),
                pltpu.VMEM((depth, width), f32),
                pltpu.VMEM((classes, depth, width), f32),
                pltpu.VMEM((depth, classes), f32),
                pltpu.VMEM((slots, depth, width), f32),
            ],
            pltpu.SemaphoreType.DMA((depth,)),
            pltpu.SemaphoreType.DMA((depth, width // 256)),
            pltpu.SemaphoreType.DMA((slots + 2,)),
            pltpu.SemaphoreType.DMA((3,)),
            pltpu.SemaphoreType.DMA((6,)),
        ],
        compiler_params=pltpu.CompilerParams(vmem_limit_bytes=62 * 1024 * 1024),
    )(gathered, states, rest, pool_w, pool_b, cls_turned, cls_b)
    return (
        states,
        jnp.transpose(logits, (1, 0, 2)),
        losses,
        pool_grad,
        pool_shift,
        jnp.transpose(cls_grad, (1, 2, 0)),
        cls_shift,
        jnp.transpose(first_grads, (1, 0, 2)),
    )


def local(
    hidden,
    lengths,
    slot_order,
    labels,
    w_qkv,
    b_query,
    b_value,
    w_out,
    b_out,
    ln1_gain,
    ln1_bias,
    w_in,
    b_in,
    w_back,
    b_back,
    ln2_gain,
    ln2_bias,
    pool_w,
    pool_b,
    cls_w,
    cls_b,
):
    stacks = (
        w_qkv,
        b_query,
        b_value,
        w_out,
        b_out,
        ln1_gain,
        ln1_bias,
        w_in,
        b_in,
        w_back,
        b_back,
        ln2_gain,
        ln2_bias,
    )
    states, context, packet = run_blocks(hidden, lengths, slot_order, labels, stacks)
    gathered, rest = run_finish(packet, states, context, stacks)
    gathered = gathered.reshape((-1,) + packet.shape)
    return run_ramps(gathered, states, rest, pool_w, pool_b, cls_w, cls_b)


def solution(mesh):
    both = ("wide", "narrow")
    return jax.shard_map(
        local,
        mesh=mesh,
        in_specs=(P(both, None, None), P(both), P(both), P(both)) + (P(),) * 17,
        out_specs=(
            P(None, both, None, None),
            P(None, both, None),
            P(),
            P(),
            P(),
            P(),
            P(),
            P(None, both, None),
        ),
        check_vma=False,
    )
```

```python
import functools
import math

import jax
import jax.numpy as jnp
from jax import lax
from jax.experimental import pallas as pl
from jax.experimental.pallas import tpu as pltpu
from jax.sharding import PartitionSpec as P

HEAD = 64
LEAD = 128
MESH = pl.DeviceIdType.MESH
epsilon = 1e-12
bf16 = jnp.bfloat16
f32 = jnp.float32
SCALE = HEAD**-0.5 * math.log2(math.e)
SUM_LOW = 2.0**-60
SUM_HIGH = 2.0**100


def split(values):
    high = values.astype(bf16)
    return high, (values - high.astype(f32)).astype(bf16)


def gelu(values):
    return (0.5 * values) * (1.0 + lax.erf(values * math.sqrt(0.5)))


def norm_rows(values, gain, shift):
    center = values - jnp.mean(values, -1, keepdims=True)
    spread = jnp.mean(center * center, -1, keepdims=True)
    return center * lax.rsqrt(spread + epsilon) * gain + shift


def blocks_kernel(
    order,
    lens,
    labels,
    hidden,
    w_qkv,
    w_out,
    w_in,
    w_back,
    b_query,
    b_value,
    b_out,
    ln1_gain,
    ln1_bias,
    b_in,
    b_back,
    ln2_gain,
    ln2_bias,
    states,
    context,
    packet,
    x_buf,
    last_buf,
    qkv_buf,
    out_buf,
    in_buf,
    back_buf,
    turned,
    columns,
    q_buf,
    k_buf,
    v_buf,
    p_buf,
    ct_buf,
    c_buf,
    m_buf,
    mb_buf,
    y_buf,
    h_buf,
    fine,
    vec_bufs,
    packet_buf,
    order_buf,
    lens_buf,
    labels_buf,
    w_sem,
    x_sem,
    o_sem,
    c_sem,
    v_sem,
):
    depth, width = b_query.shape
    slots, length = x_buf.shape[1:3]
    heads = width // HEAD
    hidden_units = b_in.shape[1]
    lead = last_buf.shape[0] // slots
    tile = length // 2
    spans = [slice(t * tile, (t + 1) * tile) for t in range(2)]

    def fetch_x(s):
        return pltpu.make_async_copy(hidden.at[order[s]], x_buf.at[0, s], x_sem.at[s])

    def fetch_qkv(l, part):
        cols = pl.ds(part * width, width)
        return pltpu.make_async_copy(
            w_qkv.at[l, :, cols], qkv_buf.at[l, :, cols], w_sem.at[l, part]
        )

    def fetch_rest(l, number):
        source = (w_out, w_in, w_back)[number]
        target = (out_buf, in_buf, back_buf)[number]
        return pltpu.make_async_copy(source.at[l], target.at[l], w_sem.at[l, 3 + number])

    def put_states(l, s):
        return pltpu.make_async_copy(x_buf.at[l + 1, s], states.at[l, s], o_sem.at[l, s])

    def put_last(s):
        return pltpu.make_async_copy(
            last_buf.at[pl.ds(s * lead, lead)],
            states.at[depth - 1, s, pl.ds(0, lead)],
            o_sem.at[depth - 1, s],
        )

    def put_context(s):
        rows = pl.ds(lead, length - lead)
        return pltpu.make_async_copy(c_buf.at[s, rows], context.at[s, rows], c_sem.at[s])

    vectors = (b_query, b_value, b_out, ln1_gain, ln1_bias, b_in, b_back, ln2_gain, ln2_bias)
    scalars = ((order, order_buf), (lens, lens_buf), (labels, labels_buf))
    small = [
        pltpu.make_async_copy(source, target, v_sem.at[number])
        for number, (source, target) in enumerate((*scalars, *zip(vectors, vec_bufs)))
    ]
    put_packet = pltpu.make_async_copy(packet_buf, packet, v_sem.at[0])
    order, lens, labels = order_buf, lens_buf, labels_buf
    b_query, b_value, b_out, ln1_gain, ln1_bias, b_in, b_back, ln2_gain, ln2_bias = vec_bufs
    for copy in small[:5]:
        copy.start()
    fetch_qkv(0, 0).start()
    fetch_qkv(0, 2).start()
    fetch_qkv(0, 1).start()
    for copy in small[5:]:
        copy.start()
    q_buf[...] = jnp.zeros_like(q_buf)
    small[0].wait()
    for number in range(slots):
        fetch_x(number).start()
    for copy in small[1:]:
        copy.wait()

    for l in range(depth):
        for number, bias in enumerate((b_query, b_value)):
            for j in range(width // 128):
                offset = number * width + j * 128
                columns[l, offset : offset + 128] = jnp.broadcast_to(
                    bias[l : l + 1, j * 128 : (j + 1) * 128], (128, 128)
                ).T

    def turn(l, block):
        skip = jnp.where(block >= width // 128, width, 0)
        lanes = pl.ds(pl.multiple_of(block * 128 + skip, 128), 128)
        rows = pl.ds(pl.multiple_of(block * 128, 128), 128)
        turned[rows] = qkv_buf[l, :, lanes].T

    def project(l, s, keys):
        rows = x_buf[l, s]
        some = rows[:keys]
        k_buf[:keys] = jnp.dot(
            some, qkv_buf[l, :, width : 2 * width], preferred_element_type=f32
        ).astype(bf16)
        seen = (
            lax.broadcasted_iota(jnp.int32, (HEAD, keys), 1) < lens[order[s]]
        ).astype(f32)
        queries = lax.dot_general(
            turned[:width], rows, (((1,), (1,)), ((), ())), preferred_element_type=f32
        )
        values = lax.dot_general(
            turned[width:], some, (((1,), (1,)), ((), ())), preferred_element_type=f32
        )
        for h in range(heads):
            at = slice(h * HEAD, (h + 1) * HEAD)
            half = slice((h % 2) * HEAD, (h % 2 + 1) * HEAD)
            q_buf[h, half] = (
                queries[at] + jnp.tile(columns[l, at, :], (1, length // 128))
            ).astype(bf16)
            av = slice(width + h * HEAD, width + (h + 1) * HEAD)
            v_buf[h, :HEAD, :keys] = (
                (values[at] + jnp.tile(columns[l, av, :], (1, keys // 128))) * seen
            ).astype(bf16)
            v_buf[h, HEAD:, :keys] = seen.astype(bf16)

    def attend(s, keys):
        def score(h):
            pair = slice((h // 2) * 128, (h // 2 + 1) * 128)
            scores = jnp.dot(k_buf[:keys, pair], q_buf[h], preferred_element_type=f32)
            p_buf[h % 4, :keys] = jnp.exp2(scores * SCALE).astype(bf16)

        def mix(h):
            both = jnp.dot(
                v_buf[h, :, :keys], p_buf[h % 4, :keys], preferred_element_type=f32
            )
            sums = both[HEAD:]
            good = (sums[:8] >= SUM_LOW) & (sums[:8] <= SUM_HIGH)
            fine[...] = jnp.where(good, fine[...], 0.0)
            half = slice((h % 2) * HEAD, (h % 2 + 1) * HEAD)
            ct_buf[(h // 2) % 2, half] = (both[:HEAD] * (1.0 / sums)).astype(bf16)
            if h % 2 == 1:
                pair = slice((h // 2) * 128, (h // 2 + 1) * 128)
                c_buf[s, :, pair] = ct_buf[(h // 2) % 2].T

        score(0)
        for h in range(heads):
            if h + 1 < heads:
                score(h + 1)
            mix(h)

    def attend_shifted(s):
        count = lens[order[s]]

        def pair_step(number, carry):
            lanes = pl.ds(pl.multiple_of(number * 128, 128), 128)
            for side in range(2):
                h = number * 2 + side
                scores = (
                    jnp.dot(k_buf[:, lanes], q_buf[h], preferred_element_type=f32) * SCALE
                )
                seen = lax.broadcasted_iota(jnp.int32, scores.shape, 0) < count
                scores = jnp.where(seen, scores, -1e30)
                highest = jnp.max(scores, 0, keepdims=True)
                p_buf[side] = jnp.exp2(scores - highest).astype(bf16)
                both = jnp.dot(v_buf[h], p_buf[side], preferred_element_type=f32)
                ct_buf[0, side * HEAD : (side + 1) * HEAD] = (
                    both[:HEAD] / both[HEAD:]
                ).astype(bf16)
            c_buf[s, :, lanes] = ct_buf[0].T
            return carry

        lax.fori_loop(0, heads // 2, pair_step, 0)

    def front(l):
        fine[...] = jnp.ones_like(fine)

        def step(s, carry):
            @pl.when(l == 0)
            def _():
                fetch_x(s).wait()

            tiles = (lens[order[s]] + 127) // 128
            for number in range(2, length // 128 + 1):
                here = (tiles <= number) if number == 2 else (tiles == number)

                @pl.when(here)
                def _(number=number):
                    project(l, s, number * 128)
                    attend(s, number * 128)

            return carry

        lax.fori_loop(0, slots, step, 0)

        @pl.when(jnp.min(fine[...]) < 0.5)
        def _():
            def again(s, carry):
                project(l, s, length)
                attend_shifted(s)
                return carry

            lax.fori_loop(0, slots, again, 0)

    def join(l, slot, contexts, inputs):
        attended = jnp.dot(contexts, out_buf[l], preferred_element_type=f32)
        values = inputs.astype(f32) + (attended + b_out[l : l + 1])
        middle = norm_rows(values, ln1_gain[l : l + 1], ln1_bias[l : l + 1])
        size = middle.shape[0]
        m_buf[slot, :size] = middle
        mb_buf[slot, :size] = middle.astype(bf16)

    def expand(l, slot, size=tile):
        chunk = 512
        for j in range(hidden_units // chunk):
            units = slice(j * chunk, (j + 1) * chunk)
            inner = jnp.dot(mb_buf[slot, :size], in_buf[l, :, units], preferred_element_type=f32)
            h_buf[slot, :size, units] = gelu(inner + b_in[l : l + 1, units]).astype(bf16)

    def contract(l, slot, size=tile):
        back = jnp.dot(h_buf[slot, :size], back_buf[l], preferred_element_type=f32)
        y_buf[slot, :size] = m_buf[slot, :size] + back + b_back[l : l + 1]

    def settle(l, slot, size=tile):
        return norm_rows(y_buf[slot, :size], ln2_gain[l : l + 1], ln2_bias[l : l + 1]).astype(bf16)

    def rear(l):
        def enter(s, half):
            join(l, half, c_buf[s, spans[half]], x_buf[l, s, spans[half]])

        enter(0, 0)

        def step(s, carry):
            x_buf[l + 1, jnp.maximum(s - 1, 0), spans[1]] = settle(l, 1)
            expand(l, 0)
            enter(s, 1)
            contract(l, 0)
            x_buf[l + 1, s, spans[0]] = settle(l, 0)
            expand(l, 1)
            enter(jnp.minimum(s + 1, slots - 1), 0)
            contract(l, 1)
            blocks = 2 * width // 128 // slots
            for number in range(blocks):
                turn(l + 1, s * blocks + number)

            @pl.when(s > 0)
            def _():
                put_states(l, s - 1).start()

            return carry

        lax.fori_loop(0, slots, step, 0)
        x_buf[l + 1, slots - 1, spans[1]] = settle(l, 1)
        put_states(l, slots - 1).start()

    def rear_lead(l):
        half = slots * lead // 2
        contexts = jnp.concatenate([c_buf[s, :lead] for s in range(slots)])
        inputs = jnp.concatenate([x_buf[l, s, :lead] for s in range(slots)])
        for t in range(2):
            rows = slice(t * half, (t + 1) * half)
            join(l, t, contexts[rows], inputs[rows])
        for t in range(2):
            expand(l, t, half)
        for t in range(2):
            contract(l, t, half)
        for t in range(2):
            last_buf[t * half : (t + 1) * half] = settle(l, t, half)
        for s in range(slots):
            put_last(s).start()

    for part in (0, 2):
        fetch_qkv(0, part).wait()
        for j in range(width // 128):
            turn(0, part // 2 * (width // 128) + j)
    fetch_qkv(0, 1).wait()

    def layer(l, carry):
        for number in range(3):
            fetch_rest(l, number).start()

        @pl.when(l < depth - 1)
        def _():
            for part in range(3):
                fetch_qkv(l + 1, part).start()

        front(l)

        @pl.when(l == depth - 1)
        def _():
            for s in range(slots):
                put_context(s).start()

        for number in range(3):
            fetch_rest(l, number).wait()

        for k in range(depth - 1):

            @pl.when(l == k)
            def _(k=k):
                for part in range(3):
                    fetch_qkv(k + 1, part).wait()
                rear(k)

        return carry

    lax.fori_loop(0, depth, layer, 0)
    rear_lead(depth - 1)
    lane = lax.broadcasted_iota(jnp.int32, packet.shape, 1)
    place = lax.broadcasted_iota(jnp.int32, packet.shape, 0)
    marks = jnp.zeros(packet.shape, f32)
    for s in range(slots):
        marks = jnp.where(lane == s, labels[order[s]].astype(f32), marks)
    packet_buf[...] = jnp.where(place == slots, marks, 0.0)
    for l in range(depth):
        for s in range(slots):
            row = l * (slots + 1) + s
            if l < depth - 1:
                packet_buf[row : row + 1] = x_buf[l + 1, s, 0:1].astype(f32)
            else:
                packet_buf[row : row + 1] = last_buf[s * lead : s * lead + 1].astype(f32)
    put_packet.start()
    for s in range(slots):
        for l in range(depth - 1):
            put_states(l, s).wait()
        put_last(s).wait()
        put_context(s).wait()
    put_packet.wait()


def run_blocks(hidden, lengths, slot_order, labels, stacks):
    (
        w_qkv,
        b_query,
        b_value,
        w_out,
        b_out,
        ln1_gain,
        ln1_bias,
        w_in,
        b_in,
        w_back,
        b_back,
        ln2_gain,
        ln2_bias,
    ) = stacks
    slots, length, width = hidden.shape
    depth = w_qkv.shape[0]
    units = w_in.shape[2]
    heads = width // HEAD
    tile = length // 2
    vectors = (b_query, b_value, b_out, ln1_gain, ln1_bias, b_in, b_back, ln2_gain, ln2_bias)
    place_hbm = pl.BlockSpec(memory_space=pl.ANY)
    return pl.pallas_call(
        blocks_kernel,
        name="blocks",
        out_shape=(
            jax.ShapeDtypeStruct((depth, slots, length, width), bf16),
            jax.ShapeDtypeStruct((slots, length, width), bf16),
            jax.ShapeDtypeStruct((depth * (slots + 1), width), f32),
        ),
        in_specs=[place_hbm] * 17,
        out_specs=(place_hbm,) * 3,
        scratch_shapes=[
            pltpu.VMEM((depth, slots, length, width), bf16),
            pltpu.VMEM((slots * LEAD, width), bf16),
            pltpu.VMEM((depth, width, 3 * width), bf16),
            pltpu.VMEM((depth, width, width), bf16),
            pltpu.VMEM((depth, width, units), bf16),
            pltpu.VMEM((depth, units, width), bf16),
            pltpu.VMEM((2 * width, width), bf16),
            pltpu.VMEM((depth, 2 * width, 128), f32),
            pltpu.VMEM((heads, 2 * HEAD, length), bf16),
            pltpu.VMEM((length, width), bf16),
            pltpu.VMEM((heads, 2 * HEAD, length), bf16),
            pltpu.VMEM((4, length, length), bf16),
            pltpu.VMEM((2, 2 * HEAD, length), bf16),
            pltpu.VMEM((slots, length, width), bf16),
            pltpu.VMEM((2, tile, width), f32),
            pltpu.VMEM((2, tile, width), bf16),
            pltpu.VMEM((2, tile, width), f32),
            pltpu.VMEM((2, tile, units), bf16),
            pltpu.VMEM((8, length), f32),
            [pltpu.VMEM(vector.shape, f32) for vector in vectors],
            pltpu.VMEM((depth * (slots + 1), width), f32),
            pltpu.SMEM((slots,), jnp.int32),
            pltpu.SMEM((slots,), jnp.int32),
            pltpu.SMEM((slots,), jnp.int32),
            pltpu.SemaphoreType.DMA((depth, 6)),
            pltpu.SemaphoreType.DMA((slots,)),
            pltpu.SemaphoreType.DMA((depth, slots)),
            pltpu.SemaphoreType.DMA((slots,)),
            pltpu.SemaphoreType.DMA((3 + len(vectors),)),
        ],
        compiler_params=pltpu.CompilerParams(vmem_limit_bytes=62 * 1024 * 1024),
    )(
        slot_order,
        lengths,
        labels,
        hidden,
        w_qkv,
        w_out,
        w_in,
        w_back,
        *vectors,
    )


def finish_kernel(
    packet,
    states,
    context,
    w_out,
    w_in,
    w_back,
    b_out,
    ln1_gain,
    ln1_bias,
    b_in,
    b_back,
    ln2_gain,
    ln2_bias,
    gathered,
    rest,
    x_buf,
    c_buf,
    out_buf,
    in_buf,
    back_buf,
    m_buf,
    mb_buf,
    h_buf,
    vec_bufs,
    t_sem,
    w_sem,
    o_sem,
    v_sem,
    keep_sem,
    near_send,
    near_recv,
    far_send,
    far_recv,
    twin_send,
    twin_recv,
):
    groups, lines = gathered.shape[:2]
    group, line = lax.axis_index("wide"), lax.axis_index("narrow")
    depth, slots = states.shape[:2]
    rows, width = x_buf.shape[1:]
    hidden_units = b_in.shape[1]
    chunk = 512
    chunks = hidden_units // chunk
    l = depth - 1
    lead = pl.ds(LEAD, rows)

    def near(step):
        return (group, lax.rem(line + step, lines))

    side = lax.rem(group, 2)

    def far(step):
        return (lax.rem(group + 2 * step, groups), line)

    twin = (group + 1 - 2 * side, line)

    def near_copy(step):
        return pltpu.make_async_remote_copy(
            src_ref=packet,
            dst_ref=gathered.at[group, line],
            send_sem=near_send,
            recv_sem=near_recv,
            device_id=near(step),
            device_id_type=MESH,
        )

    def far_copy(step):
        return pltpu.make_async_remote_copy(
            src_ref=gathered.at[group],
            dst_ref=gathered.at[group],
            send_sem=far_send,
            recv_sem=far_recv,
            device_id=far(step),
            device_id_type=MESH,
        )

    def near_all():
        return pltpu.make_async_remote_copy(
            src_ref=gathered.at[0, pl.ds(0, lines - 1)],
            dst_ref=gathered.at[0, pl.ds(0, lines - 1)],
            send_sem=near_send,
            recv_sem=near_recv,
            device_id=near(1),
            device_id_type=MESH,
        )

    def far_all():
        return pltpu.make_async_remote_copy(
            src_ref=gathered.at[pl.ds(0, groups // 2 - 1)],
            dst_ref=gathered.at[pl.ds(0, groups // 2 - 1)],
            send_sem=far_send,
            recv_sem=far_recv,
            device_id=far(1),
            device_id_type=MESH,
        )

    def twin_copy(step):
        return pltpu.make_async_remote_copy(
            src_ref=gathered.at[2 * step + side],
            dst_ref=gathered.at[2 * step + side],
            send_sem=twin_send,
            recv_sem=twin_recv,
            device_id=twin,
            device_id_type=MESH,
        )

    def twin_all():
        return pltpu.make_async_remote_copy(
            src_ref=gathered.at[pl.ds(0, groups // 2)],
            dst_ref=gathered.at[pl.ds(0, groups // 2)],
            send_sem=twin_send,
            recv_sem=twin_recv,
            device_id=twin,
            device_id_type=MESH,
        )

    def keep_own():
        return pltpu.make_async_copy(packet, gathered.at[group, line], keep_sem)

    def begin(copy):
        def body(step, carry):
            copy(step).start()
            return carry

        return body

    def greet(place):
        def body(step, carry):
            pl.semaphore_signal(barrier, inc=1, device_id=place(step), device_id_type=MESH)
            return carry

        return body

    def fetch_tile(s):
        return (
            pltpu.make_async_copy(context.at[s, lead], c_buf.at[s], t_sem.at[0, s]),
            pltpu.make_async_copy(states.at[l - 1, s, lead], x_buf.at[s], t_sem.at[1, s]),
        )

    def fetch_out():
        return pltpu.make_async_copy(w_out.at[l], out_buf, w_sem.at[0])

    def fetch_in(j):
        units = pl.ds(j * chunk, chunk)
        return pltpu.make_async_copy(
            w_in.at[l, :, units], in_buf.at[:, units], w_sem.at[1 + j]
        )

    def fetch_back(j):
        units = pl.ds(j * chunk, chunk)
        return pltpu.make_async_copy(
            w_back.at[l, units], back_buf.at[units], w_sem.at[1 + chunks + j]
        )

    def put_rest(s):
        return pltpu.make_async_copy(x_buf.at[s], rest.at[s], o_sem.at[s])

    barrier = pltpu.get_barrier_semaphore()
    lax.fori_loop(1, lines, greet(near), 0)
    lax.fori_loop(1, groups // 2, greet(far), 0)
    pl.semaphore_signal(barrier, inc=1, device_id=twin, device_id_type=MESH)
    vectors = (b_out, ln1_gain, ln1_bias, b_in, b_back, ln2_gain, ln2_bias)
    small = [
        pltpu.make_async_copy(source, target, v_sem.at[number])
        for number, (source, target) in enumerate(zip(vectors, vec_bufs))
    ]
    b_out, ln1_gain, ln1_bias, b_in, b_back, ln2_gain, ln2_bias = vec_bufs
    queue = [*fetch_tile(0), fetch_out()]
    for j in range(chunks):
        queue.append(fetch_in(j))
        if 0 < j < slots:
            queue += fetch_tile(j)
    queue += [fetch_back(j) for j in range(chunks)]
    queue.reverse()

    def advance(number):
        for _ in range(min(number, len(queue))):
            queue.pop().start()

    for copy in small:
        copy.start()
    advance(3)
    pl.semaphore_wait(barrier, lines + groups // 2 - 1)
    lax.fori_loop(1, lines, begin(near_copy), 0)
    keep_own().start()
    for copy in small:
        copy.wait()
    advance(4)

    def join(s):
        attended = jnp.dot(c_buf[s], out_buf[...], preferred_element_type=f32)
        m_buf[s] = x_buf[s].astype(f32) + (attended + b_out[l : l + 1])

    def norm_first(s, span):
        middle = norm_rows(m_buf[s, span], ln1_gain[l : l + 1], ln1_bias[l : l + 1])
        m_buf[s, span] = middle
        mb_buf[s, span] = middle.astype(bf16)

    def expand(s, j):
        units = slice(j * chunk, (j + 1) * chunk)
        inner = jnp.dot(mb_buf[s], in_buf[:, units], preferred_element_type=f32)
        h_buf[s, :, units] = gelu(inner + b_in[l : l + 1, units]).astype(bf16)

    def contract(s, span):
        back = jnp.dot(h_buf[s, span], back_buf[...], preferred_element_type=f32)
        m_buf[s, span] = m_buf[s, span] + back + b_back[l : l + 1]

    def settle(s, span):
        x_buf[s, span] = norm_rows(
            m_buf[s, span], ln2_gain[l : l + 1], ln2_bias[l : l + 1]
        ).astype(bf16)

    def cut(parts):
        size = rows // parts
        return [slice(t * size, (t + 1) * size) for t in range(parts)]

    for copy in fetch_tile(0):
        copy.wait()
    fetch_out().wait()
    advance(3)
    join(0)
    for span in cut(2):
        norm_first(0, span)
    for s in range(slots):
        if s + 1 < slots:
            for copy in fetch_tile(s + 1):
                copy.wait()
        for j, span in enumerate(cut(chunks)):
            if s == 0:
                fetch_in(j).wait()
                advance(2)
            expand(s, j)
            if j == 0 and s + 1 < slots:
                join(s + 1)
            if s + 1 < slots:
                norm_first(s + 1, span)
            if s == 0 and j == chunks // 2:
                keep_own().wait()
                near_all().wait()
                lax.fori_loop(1, groups // 2, begin(far_copy), 0)
        if s == 0:
            advance(len(queue))
    for j in range(chunks):
        fetch_back(j).wait()
    halves = cut(2)
    steps = [(s, span) for s in range(slots) for span in halves]
    for number, (s, span) in enumerate(steps):
        contract(s, span)
        if number > 0:
            settle(*steps[number - 1])
            if number % 2 == 0:
                put_rest(s - 1).start()
        if number == 2 * slots - 3:
            far_all().wait()
            lax.fori_loop(0, groups // 2, begin(twin_copy), 0)
    settle(*steps[-1])
    put_rest(slots - 1).start()
    twin_all().wait()
    for s in range(slots):
        put_rest(s).wait()


def run_finish(packet, states, context, stacks):
    (_, _, _, w_out, b_out, ln1_gain, ln1_bias, w_in, b_in, w_back, b_back, ln2_gain, ln2_bias) = (
        stacks
    )
    groups, lines = lax.axis_size("wide"), lax.axis_size("narrow")
    slots, length, width = context.shape
    units = w_in.shape[2]
    rows = length - LEAD
    place_hbm = pl.BlockSpec(memory_space=pl.ANY)
    vectors = (b_out, ln1_gain, ln1_bias, b_in, b_back, ln2_gain, ln2_bias)
    return pl.pallas_call(
        finish_kernel,
        name="finish",
        out_shape=(
            jax.ShapeDtypeStruct((groups, lines) + packet.shape, f32),
            jax.ShapeDtypeStruct((slots, rows, width), bf16),
        ),
        in_specs=[place_hbm] * 13,
        out_specs=(place_hbm, place_hbm),
        scratch_shapes=[
            pltpu.VMEM((slots, rows, width), bf16),
            pltpu.VMEM((slots, rows, width), bf16),
            pltpu.VMEM((width, width), bf16),
            pltpu.VMEM((width, units), bf16),
            pltpu.VMEM((units, width), bf16),
            pltpu.VMEM((slots, rows, width), f32),
            pltpu.VMEM((slots, rows, width), bf16),
            pltpu.VMEM((slots, rows, units), bf16),
            [pltpu.VMEM(vector.shape, f32) for vector in vectors],
            pltpu.SemaphoreType.DMA((2, slots)),
            pltpu.SemaphoreType.DMA((1 + 2 * (units // 512),)),
            pltpu.SemaphoreType.DMA((slots,)),
            pltpu.SemaphoreType.DMA((len(vectors),)),
        ]
        + [pltpu.SemaphoreType.DMA] * 7,
        compiler_params=pltpu.CompilerParams(
            collective_id=0,
            has_side_effects=True,
            vmem_limit_bytes=62 * 1024 * 1024,
        ),
    )(
        packet,
        states,
        context,
        w_out,
        w_in,
        w_back,
        *vectors,
    )


def ramps_kernel(
    gathered,
    states_in,
    rest,
    pool_w,
    pool_b,
    cls_w,
    cls_b,
    states,
    logits,
    losses,
    grad_pool_w,
    grad_pool_b,
    grad_cls_w,
    grad_cls_b,
    first_grads,
    all_buf,
    w_buf,
    g_buf,
    score_buf,
    inner_buf,
    rest_buf,
    in_bufs,
    out_bufs,
    w_sem,
    g_sem,
    s_sem,
    i_sem,
    r_sem,
):
    slots, depth, classes = logits.shape
    devices, packet, width = gathered.shape
    own = lax.axis_index("wide") * lax.axis_size("narrow") + lax.axis_index("narrow")

    def fetch(l):
        return pltpu.make_async_copy(pool_w.at[l], w_buf.at[l], w_sem.at[l])

    def put(l, t):
        span = pl.ds(t * 256, 256)
        return pltpu.make_async_copy(
            g_buf.at[l, span], grad_pool_w.at[l, span], g_sem.at[l, t]
        )

    def fetch_rest():
        return pltpu.make_async_copy(rest, rest_buf, s_sem.at[slots])

    def put_rest(s):
        return pltpu.make_async_copy(
            rest_buf.at[s], states.at[depth - 1, s, pl.ds(LEAD, rest.shape[1])], s_sem.at[s]
        )

    inputs = [
        pltpu.make_async_copy(source, target, i_sem.at[number])
        for number, (source, target) in enumerate(zip((pool_b, cls_w, cls_b), in_bufs))
    ]
    results = (logits, losses, grad_pool_b, grad_cls_w, grad_cls_b, first_grads)
    outputs = [
        pltpu.make_async_copy(source, target, r_sem.at[number])
        for number, (source, target) in enumerate(zip(out_bufs, results))
    ]
    pool_b, cls_w, cls_b = in_bufs
    logits, losses, grad_pool_b, grad_cls_w, grad_cls_b, first_grads = out_bufs
    gather_in = pltpu.make_async_copy(gathered, all_buf, s_sem.at[slots + 1])
    gather_in.start()
    for copy in inputs:
        copy.start()
    for l in range(depth):
        fetch(l).start()
    fetch_rest().start()
    gather_in.wait()
    for copy in inputs:
        copy.wait()

    unit = slots + 1
    rows = devices * unit
    pairs = all_buf[...].reshape(devices // 2, 2 * packet, width)
    even = pairs[:, :packet].reshape(rows, width)
    odd = pairs[:, packet:].reshape(rows, width)
    upper = lax.rem(lax.broadcasted_iota(jnp.int32, (rows, width), 0), packet) < unit
    firsts_all = (
        jnp.where(upper, even, pltpu.roll(odd, unit, 0)),
        jnp.where(upper, pltpu.roll(even, rows - unit, 0), odd),
    )
    place = lax.rem(lax.broadcasted_iota(jnp.int32, (rows, 128), 0), unit)
    marks = firsts_all[0][:, :128]
    spread = jnp.full((rows, 128), -1.0, f32)
    for s in range(slots):
        moved = pltpu.roll(marks, rows - (slots - s), 0)
        spread = jnp.where(place == s, moved[:, s : s + 1], spread)
    label_row = spread.T[:1]
    valid = (label_row >= 0).astype(f32)
    count = jnp.sum(valid)
    class_column = lax.broadcasted_iota(jnp.int32, (classes, rows), 0).astype(f32)
    onehot = (label_row == class_column).astype(f32)

    def mine(pair):
        return jnp.where(lax.rem(own, 2) == 0, pair[:slots], pair[unit : unit + slots])

    def dot(a, b):
        return jnp.dot(a, b, preferred_element_type=f32)

    def dot_turned(a, b):
        return lax.dot_general(a, b, (((1,), (1,)), ((), ())), preferred_element_type=f32)

    for l in range(depth):
        firsts_low = firsts_all[l].astype(bf16)
        firsts_turned = firsts_all[l].T.astype(bf16)
        cls = cls_w[:, l]
        cls_high, cls_low = split(cls)
        fetch(l).wait()
        weights, weights_low = split(w_buf[l])
        pooled = jnp.tanh(
            dot(firsts_low, weights) + dot(firsts_low, weights_low) + pool_b[l : l + 1]
        )
        pooled_high, pooled_low = split(pooled)
        scores = (
            dot_turned(cls_high, pooled_high)
            + (dot_turned(cls_low, pooled_high) + dot_turned(cls_high, pooled_low))
            + cls_b[l : l + 1].T
        )
        highest = jnp.max(scores, 0, keepdims=True)
        raised = jnp.exp(scores - highest)
        totals = jnp.sum(raised, 0, keepdims=True)
        grad = valid * (raised / totals - onehot) / count
        grad_column = grad.T
        inner = grad_column[:, 0:1] * cls[0:1]
        for c in range(1, classes):
            inner = inner + grad_column[:, c : c + 1] * cls[c : c + 1]
        inner = inner * (1.0 - pooled * pooled)
        inner_high, inner_low = split(inner)
        for t in range(width // 256):
            span = slice(t * 256, (t + 1) * 256)
            g_buf[l, span] = dot(firsts_turned[span], inner_high) + dot(
                firsts_turned[span], inner_low
            )
            put(l, t).start()
        grad_high, grad_low = split(grad)
        grad_cls_w[:, l] = dot(grad_high, pooled_high) + (
            dot(grad_low, pooled_high) + dot(grad_high, pooled_low)
        )
        inner_buf[...] = inner.reshape(devices // 2, packet, width)
        own_high, own_low = split(inner_buf[own // 2])
        own_grads = dot_turned(own_high, weights) + dot_turned(own_low, weights)
        first_grads[:, l] = mine(own_grads)
        grad_pool_b[l : l + 1] = jnp.sum(inner, 0, keepdims=True)
        grad_cls_b[l : l + 1] = jnp.sum(grad, 1, keepdims=True).T
        log_total = highest + jnp.log(totals)
        picked = jnp.sum(scores * onehot, 0, keepdims=True)
        losses[l] = jnp.sum(valid * (log_total - picked)) / count
        score_buf[...] = scores.T.reshape(devices // 2, packet, classes)
        logits[:, l] = mine(score_buf[own // 2])
        if l == 0:
            fetch_rest().wait()
            for s in range(slots):
                put_rest(s).start()
    for copy in outputs:
        copy.start()
    for l in range(depth):
        for t in range(width // 256):
            put(l, t).wait()
    for copy in outputs:
        copy.wait()
    for s in range(slots):
        put_rest(s).wait()


def run_ramps(gathered, states, rest, pool_w, pool_b, cls_w, cls_b):
    devices, packet, width = gathered.shape
    depth, classes = cls_b.shape
    slots = rest.shape[0]
    pairs = devices // 2
    place_hbm = pl.BlockSpec(memory_space=pl.ANY)
    cls_turned = jnp.transpose(cls_w, (2, 0, 1))
    states, logits, losses, pool_grad, pool_shift, cls_grad, cls_shift, first_grads = pl.pallas_call(
        ramps_kernel,
        name="ramps",
        out_shape=(
            jax.ShapeDtypeStruct(states.shape, states.dtype),
            jax.ShapeDtypeStruct((slots, depth, classes), f32),
            jax.ShapeDtypeStruct((depth,), f32),
            jax.ShapeDtypeStruct((depth, width, width), f32),
            jax.ShapeDtypeStruct((depth, width), f32),
            jax.ShapeDtypeStruct((classes, depth, width), f32),
            jax.ShapeDtypeStruct((depth, classes), f32),
            jax.ShapeDtypeStruct((slots, depth, width), f32),
        ),
        in_specs=[place_hbm] * 7,
        out_specs=(place_hbm,) * 8,
        input_output_aliases={1: 0},
        scratch_shapes=[
            pltpu.VMEM(gathered.shape, f32),
            pltpu.VMEM((depth, width, width), f32),
            pltpu.VMEM((depth, width, width), f32),
            pltpu.VMEM((pairs, packet, classes), f32),
            pltpu.VMEM((pairs, packet, width), f32),
            pltpu.VMEM(rest.shape, bf16),
            [pltpu.VMEM(member.shape, f32) for member in (pool_b, cls_turned, cls_b)],
            [
                pltpu.VMEM((slots, depth, classes), f32),
                pltpu.SMEM((depth,), f32),
                pltpu.VMEM((depth, width), f32),
                pltpu.VMEM((classes, depth, width), f32),
                pltpu.VMEM((depth, classes), f32),
                pltpu.VMEM((slots, depth, width), f32),
            ],
            pltpu.SemaphoreType.DMA((depth,)),
            pltpu.SemaphoreType.DMA((depth, width // 256)),
            pltpu.SemaphoreType.DMA((slots + 2,)),
            pltpu.SemaphoreType.DMA((3,)),
            pltpu.SemaphoreType.DMA((6,)),
        ],
        compiler_params=pltpu.CompilerParams(vmem_limit_bytes=62 * 1024 * 1024),
    )(gathered, states, rest, pool_w, pool_b, cls_turned, cls_b)
    return (
        states,
        jnp.transpose(logits, (1, 0, 2)),
        losses,
        pool_grad,
        pool_shift,
        jnp.transpose(cls_grad, (1, 2, 0)),
        cls_shift,
        jnp.transpose(first_grads, (1, 0, 2)),
    )


def local(
    hidden,
    lengths,
    slot_order,
    labels,
    w_qkv,
    b_query,
    b_value,
    w_out,
    b_out,
    ln1_gain,
    ln1_bias,
    w_in,
    b_in,
    w_back,
    b_back,
    ln2_gain,
    ln2_bias,
    pool_w,
    pool_b,
    cls_w,
    cls_b,
):
    stacks = (
        w_qkv,
        b_query,
        b_value,
        w_out,
        b_out,
        ln1_gain,
        ln1_bias,
        w_in,
        b_in,
        w_back,
        b_back,
        ln2_gain,
        ln2_bias,
    )
    states, context, packet = run_blocks(hidden, lengths, slot_order, labels, stacks)
    gathered, rest = run_finish(packet, states, context, stacks)
    gathered = gathered.reshape((-1,) + packet.shape)
    return run_ramps(gathered, states, rest, pool_w, pool_b, cls_w, cls_b)


def solution(mesh):
    both = ("wide", "narrow")
    return jax.shard_map(
        local,
        mesh=mesh,
        in_specs=(P(both, None, None), P(both), P(both), P(both)) + (P(),) * 17,
        out_specs=(
            P(None, both, None, None),
            P(None, both, None),
            P(),
            P(),
            P(),
            P(),
            P(),
            P(None, both, None),
        ),
        check_vma=False,
    )
```

```python
import functools
import math

import jax
import jax.numpy as jnp
from jax import lax
from jax.experimental import pallas as pl
from jax.experimental.pallas import tpu as pltpu
from jax.sharding import PartitionSpec as P

HEAD = 64
LEAD = 128
MESH = pl.DeviceIdType.MESH
epsilon = 1e-12
bf16 = jnp.bfloat16
f32 = jnp.float32
SCALE = HEAD**-0.5 * math.log2(math.e)
SUM_LOW = 2.0**-60
SUM_HIGH = 2.0**100


def split(values):
    high = values.astype(bf16)
    return high, (values - high.astype(f32)).astype(bf16)


def gelu_twice(values):
    return values * (1.0 + lax.erf(values * math.sqrt(0.5)))


def norm_rows(values, gain, shift):
    center = values - jnp.mean(values, -1, keepdims=True)
    spread = jnp.mean(center * center, -1, keepdims=True)
    return center * lax.rsqrt(spread + epsilon) * gain + shift


def blocks_kernel(
    order,
    lens,
    labels,
    hidden,
    w_qkv,
    w_out,
    w_in,
    w_back,
    b_query,
    b_value,
    b_out,
    ln1_gain,
    ln1_bias,
    b_in,
    b_back,
    ln2_gain,
    ln2_bias,
    states,
    context,
    packet,
    x_buf,
    last_buf,
    qkv_buf,
    out_buf,
    in_buf,
    back_buf,
    turned,
    columns,
    q_buf,
    k_buf,
    v_buf,
    p_buf,
    ct_buf,
    c_buf,
    m_buf,
    mb_buf,
    y_buf,
    h_buf,
    fine,
    vec_bufs,
    packet_buf,
    order_buf,
    lens_buf,
    labels_buf,
    w_sem,
    x_sem,
    o_sem,
    c_sem,
    v_sem,
):
    depth, width = b_query.shape
    slots, length = x_buf.shape[1:3]
    heads = width // HEAD
    hidden_units = b_in.shape[1]
    lead = last_buf.shape[0] // slots
    tile = length // 2
    spans = [slice(t * tile, (t + 1) * tile) for t in range(2)]

    def fetch_x(s):
        return pltpu.make_async_copy(hidden.at[order[s]], x_buf.at[0, s], x_sem.at[s])

    def fetch_qkv(l, part):
        cols = pl.ds(part * width, width)
        return pltpu.make_async_copy(
            w_qkv.at[l, :, cols], qkv_buf.at[l, :, cols], w_sem.at[l, part]
        )

    def fetch_rest(l, number):
        source = (w_out, w_in, w_back)[number]
        target = (out_buf, in_buf, back_buf)[number]
        return pltpu.make_async_copy(source.at[l], target.at[l], w_sem.at[l, 3 + number])

    def put_states(l, s):
        return pltpu.make_async_copy(x_buf.at[l + 1, s], states.at[l, s], o_sem.at[l, s])

    def put_last(s):
        return pltpu.make_async_copy(
            last_buf.at[pl.ds(s * lead, lead)],
            states.at[depth - 1, s, pl.ds(0, lead)],
            o_sem.at[depth - 1, s],
        )

    def put_context(s):
        rows = pl.ds(lead, length - lead)
        return pltpu.make_async_copy(c_buf.at[s, rows], context.at[s, rows], c_sem.at[s])

    vectors = (b_query, b_value, b_out, ln1_gain, ln1_bias, b_in, b_back, ln2_gain, ln2_bias)
    scalars = ((order, order_buf), (lens, lens_buf), (labels, labels_buf))
    small = [
        pltpu.make_async_copy(source, target, v_sem.at[number])
        for number, (source, target) in enumerate((*scalars, *zip(vectors, vec_bufs)))
    ]
    put_packet = pltpu.make_async_copy(packet_buf, packet, v_sem.at[0])
    order, lens, labels = order_buf, lens_buf, labels_buf
    b_query, b_value, b_out, ln1_gain, ln1_bias, b_in, b_back, ln2_gain, ln2_bias = vec_bufs
    for copy in small[:5]:
        copy.start()
    fetch_qkv(0, 0).start()
    fetch_qkv(0, 2).start()
    fetch_qkv(0, 1).start()
    for copy in small[5:]:
        copy.start()
    q_buf[...] = jnp.zeros_like(q_buf)
    small[0].wait()
    fetch_x(0).start()
    for copy in small[1:]:
        copy.wait()

    for l in range(depth):
        for number, bias in enumerate((b_query, b_value)):
            for j in range(width // 128):
                offset = number * width + j * 128
                columns[l, offset : offset + 128] = jnp.broadcast_to(
                    bias[l : l + 1, j * 128 : (j + 1) * 128], (128, 128)
                ).T

    def turn(l, block):
        skip = jnp.where(block >= width // 128, width, 0)
        lanes = pl.ds(pl.multiple_of(block * 128 + skip, 128), 128)
        rows = pl.ds(pl.multiple_of(block * 128, 128), 128)
        turned[rows] = qkv_buf[l, :, lanes].T

    def project(l, s, keys):
        rows = x_buf[l, s]
        some = rows[:keys]
        k_buf[:keys] = jnp.dot(
            some, qkv_buf[l, :, width : 2 * width], preferred_element_type=f32
        ).astype(bf16)
        seen = (
            lax.broadcasted_iota(jnp.int32, (HEAD, keys), 1) < lens[order[s]]
        ).astype(f32)
        queries = lax.dot_general(
            turned[:width], rows, (((1,), (1,)), ((), ())), preferred_element_type=f32
        )
        values = lax.dot_general(
            turned[width:], some, (((1,), (1,)), ((), ())), preferred_element_type=f32
        )
        for h in range(heads):
            at = slice(h * HEAD, (h + 1) * HEAD)
            half = slice((h % 2) * HEAD, (h % 2 + 1) * HEAD)
            q_buf[h, half] = (
                queries[at] + jnp.tile(columns[l, at, :], (1, length // 128))
            ).astype(bf16)
            av = slice(width + h * HEAD, width + (h + 1) * HEAD)
            v_buf[h, :HEAD, :keys] = (
                (values[at] + jnp.tile(columns[l, av, :], (1, keys // 128))) * seen
            ).astype(bf16)
            v_buf[h, HEAD:, :keys] = seen.astype(bf16)

    def attend(s, keys):
        def score(h):
            pair = slice((h // 2) * 128, (h // 2 + 1) * 128)
            scores = jnp.dot(k_buf[:keys, pair], q_buf[h], preferred_element_type=f32)
            p_buf[h % 4, :keys] = jnp.exp2(scores * SCALE).astype(bf16)

        def mix(h):
            both = jnp.dot(
                v_buf[h, :, :keys], p_buf[h % 4, :keys], preferred_element_type=f32
            )
            sums = both[HEAD:]
            good = (sums[:8] >= SUM_LOW) & (sums[:8] <= SUM_HIGH)
            fine[...] = jnp.where(good, fine[...], 0.0)
            half = slice((h % 2) * HEAD, (h % 2 + 1) * HEAD)
            ct_buf[(h // 2) % 2, half] = (both[:HEAD] * (1.0 / sums)).astype(bf16)
            if h % 2 == 1:
                pair = slice((h // 2) * 128, (h // 2 + 1) * 128)
                c_buf[s, :, pair] = ct_buf[(h // 2) % 2].T

        score(0)
        for h in range(heads):
            if h + 1 < heads:
                score(h + 1)
            mix(h)

    def attend_shifted(s):
        count = lens[order[s]]

        def pair_step(number, carry):
            lanes = pl.ds(pl.multiple_of(number * 128, 128), 128)
            for side in range(2):
                h = number * 2 + side
                scores = (
                    jnp.dot(k_buf[:, lanes], q_buf[h], preferred_element_type=f32) * SCALE
                )
                seen = lax.broadcasted_iota(jnp.int32, scores.shape, 0) < count
                scores = jnp.where(seen, scores, -1e30)
                highest = jnp.max(scores, 0, keepdims=True)
                p_buf[side] = jnp.exp2(scores - highest).astype(bf16)
                both = jnp.dot(v_buf[h], p_buf[side], preferred_element_type=f32)
                ct_buf[0, side * HEAD : (side + 1) * HEAD] = (
                    both[:HEAD] / both[HEAD:]
                ).astype(bf16)
            c_buf[s, :, lanes] = ct_buf[0].T
            return carry

        lax.fori_loop(0, heads // 2, pair_step, 0)

    def front(l):
        fine[...] = jnp.ones_like(fine)

        def step(s, carry):
            @pl.when(l == 0)
            def _():
                fetch_x(s).wait()

            tiles = (lens[order[s]] + 127) // 128
            for number in range(1, length // 128 + 1):

                @pl.when(tiles == number)
                def _(number=number):
                    project(l, s, number * 128)
                    attend(s, number * 128)

            return carry

        lax.fori_loop(0, slots, step, 0)

        @pl.when(jnp.min(fine[...]) < 0.5)
        def _():
            def again(s, carry):
                project(l, s, length)
                attend_shifted(s)
                return carry

            lax.fori_loop(0, slots, again, 0)

    def join(l, slot, contexts, inputs):
        attended = jnp.dot(contexts, out_buf[l], preferred_element_type=f32)
        values = inputs.astype(f32) + (attended + b_out[l : l + 1])
        middle = norm_rows(values, ln1_gain[l : l + 1], ln1_bias[l : l + 1])
        size = middle.shape[0]
        m_buf[slot, :size] = middle
        mb_buf[slot, :size] = middle.astype(bf16)

    def expand(l, slot, size=tile):
        chunk = 512
        for j in range(hidden_units // chunk):
            units = slice(j * chunk, (j + 1) * chunk)
            inner = jnp.dot(mb_buf[slot, :size], in_buf[l, :, units], preferred_element_type=f32)
            h_buf[slot, :size, units] = gelu_twice(inner + b_in[l : l + 1, units]).astype(bf16)

    def contract(l, slot, size=tile):
        back = jnp.dot(h_buf[slot, :size], back_buf[l], preferred_element_type=f32)
        y_buf[slot, :size] = m_buf[slot, :size] + 0.5 * back + b_back[l : l + 1]

    def settle(l, slot, size=tile):
        return norm_rows(y_buf[slot, :size], ln2_gain[l : l + 1], ln2_bias[l : l + 1]).astype(bf16)

    def rear(l):
        def enter(s, half):
            join(l, half, c_buf[s, spans[half]], x_buf[l, s, spans[half]])

        enter(0, 0)

        def step(s, carry):
            x_buf[l + 1, jnp.maximum(s - 1, 0), spans[1]] = settle(l, 1)
            expand(l, 0)
            enter(s, 1)
            contract(l, 0)
            x_buf[l + 1, s, spans[0]] = settle(l, 0)
            expand(l, 1)
            enter(jnp.minimum(s + 1, slots - 1), 0)
            contract(l, 1)
            blocks = 2 * width // 128 // slots
            for number in range(blocks):
                turn(l + 1, s * blocks + number)

            @pl.when(s > 0)
            def _():
                put_states(l, s - 1).start()

            return carry

        lax.fori_loop(0, slots, step, 0)
        x_buf[l + 1, slots - 1, spans[1]] = settle(l, 1)
        put_states(l, slots - 1).start()

    def rear_lead(l):
        half = slots * lead // 2
        contexts = jnp.concatenate([c_buf[s, :lead] for s in range(slots)])
        inputs = jnp.concatenate([x_buf[l, s, :lead] for s in range(slots)])
        for t in range(2):
            rows = slice(t * half, (t + 1) * half)
            join(l, t, contexts[rows], inputs[rows])
        for t in range(2):
            expand(l, t, half)
        for t in range(2):
            contract(l, t, half)
        for t in range(2):
            last_buf[t * half : (t + 1) * half] = settle(l, t, half)
        for s in range(slots):
            put_last(s).start()

    for part in (0, 2):
        fetch_qkv(0, part).wait()
        for j in range(width // 128):
            turn(0, part // 2 * (width // 128) + j)
    fetch_qkv(0, 1).wait()
    for number in range(1, slots):
        fetch_x(number).start()

    def layer(l, carry):
        for number in range(3):
            fetch_rest(l, number).start()

        @pl.when(l < depth - 1)
        def _():
            for part in range(3):
                fetch_qkv(l + 1, part).start()

        front(l)

        @pl.when(l == depth - 1)
        def _():
            for s in range(slots):
                put_context(s).start()

        for number in range(3):
            fetch_rest(l, number).wait()

        for k in range(depth - 1):

            @pl.when(l == k)
            def _(k=k):
                for part in range(3):
                    fetch_qkv(k + 1, part).wait()
                rear(k)

        return carry

    lax.fori_loop(0, depth, layer, 0)
    rear_lead(depth - 1)
    lane = lax.broadcasted_iota(jnp.int32, packet.shape, 1)
    place = lax.broadcasted_iota(jnp.int32, packet.shape, 0)
    marks = jnp.zeros(packet.shape, f32)
    for s in range(slots):
        marks = jnp.where(lane == s, labels[order[s]].astype(f32), marks)
    packet_buf[...] = jnp.where(place == slots, marks, 0.0)
    for l in range(depth):
        for s in range(slots):
            row = l * (slots + 1) + s
            if l < depth - 1:
                packet_buf[row : row + 1] = x_buf[l + 1, s, 0:1].astype(f32)
            else:
                packet_buf[row : row + 1] = last_buf[s * lead : s * lead + 1].astype(f32)
    put_packet.start()
    for s in range(slots):
        for l in range(depth - 1):
            put_states(l, s).wait()
        put_last(s).wait()
        put_context(s).wait()
    put_packet.wait()


def run_blocks(hidden, lengths, slot_order, labels, stacks):
    (
        w_qkv,
        b_query,
        b_value,
        w_out,
        b_out,
        ln1_gain,
        ln1_bias,
        w_in,
        b_in,
        w_back,
        b_back,
        ln2_gain,
        ln2_bias,
    ) = stacks
    slots, length, width = hidden.shape
    depth = w_qkv.shape[0]
    units = w_in.shape[2]
    heads = width // HEAD
    tile = length // 2
    vectors = (b_query, b_value, b_out, ln1_gain, ln1_bias, b_in, b_back, ln2_gain, ln2_bias)
    place_hbm = pl.BlockSpec(memory_space=pl.ANY)
    return pl.pallas_call(
        blocks_kernel,
        name="blocks",
        out_shape=(
            jax.ShapeDtypeStruct((depth, slots, length, width), bf16),
            jax.ShapeDtypeStruct((slots, length, width), bf16),
            jax.ShapeDtypeStruct((depth * (slots + 1), width), f32),
        ),
        in_specs=[place_hbm] * 17,
        out_specs=(place_hbm,) * 3,
        scratch_shapes=[
            pltpu.VMEM((depth, slots, length, width), bf16),
            pltpu.VMEM((slots * LEAD, width), bf16),
            pltpu.VMEM((depth, width, 3 * width), bf16),
            pltpu.VMEM((depth, width, width), bf16),
            pltpu.VMEM((depth, width, units), bf16),
            pltpu.VMEM((depth, units, width), bf16),
            pltpu.VMEM((2 * width, width), bf16),
            pltpu.VMEM((depth, 2 * width, 128), f32),
            pltpu.VMEM((heads, 2 * HEAD, length), bf16),
            pltpu.VMEM((length, width), bf16),
            pltpu.VMEM((heads, 2 * HEAD, length), bf16),
            pltpu.VMEM((4, length, length), bf16),
            pltpu.VMEM((2, 2 * HEAD, length), bf16),
            pltpu.VMEM((slots, length, width), bf16),
            pltpu.VMEM((2, tile, width), f32),
            pltpu.VMEM((2, tile, width), bf16),
            pltpu.VMEM((2, tile, width), f32),
            pltpu.VMEM((2, tile, units), bf16),
            pltpu.VMEM((8, length), f32),
            [pltpu.VMEM(vector.shape, f32) for vector in vectors],
            pltpu.VMEM((depth * (slots + 1), width), f32),
            pltpu.SMEM((slots,), jnp.int32),
            pltpu.SMEM((slots,), jnp.int32),
            pltpu.SMEM((slots,), jnp.int32),
            pltpu.SemaphoreType.DMA((depth, 6)),
            pltpu.SemaphoreType.DMA((slots,)),
            pltpu.SemaphoreType.DMA((depth, slots)),
            pltpu.SemaphoreType.DMA((slots,)),
            pltpu.SemaphoreType.DMA((3 + len(vectors),)),
        ],
        compiler_params=pltpu.CompilerParams(vmem_limit_bytes=62 * 1024 * 1024),
    )(
        slot_order,
        lengths,
        labels,
        hidden,
        w_qkv,
        w_out,
        w_in,
        w_back,
        *vectors,
    )


def finish_kernel(
    packet,
    states,
    context,
    w_out,
    w_in,
    w_back,
    b_out,
    ln1_gain,
    ln1_bias,
    b_in,
    b_back,
    ln2_gain,
    ln2_bias,
    gathered,
    rest,
    x_buf,
    c_buf,
    out_buf,
    in_buf,
    back_buf,
    m_buf,
    mb_buf,
    h_buf,
    vec_bufs,
    t_sem,
    w_sem,
    o_sem,
    v_sem,
    keep_sem,
    near_send,
    near_recv,
    far_send,
    far_recv,
    twin_send,
    twin_recv,
):
    groups, lines = gathered.shape[:2]
    group, line = lax.axis_index("wide"), lax.axis_index("narrow")
    depth, slots = states.shape[:2]
    rows, width = x_buf.shape[1:]
    hidden_units = b_in.shape[1]
    chunk = 512
    chunks = hidden_units // chunk
    l = depth - 1
    lead = pl.ds(LEAD, rows)

    def near(step):
        return (group, lax.rem(line + step, lines))

    side = lax.rem(group, 2)

    def far(step):
        return (lax.rem(group + 2 * step, groups), line)

    twin = (group + 1 - 2 * side, line)

    def near_copy(step):
        return pltpu.make_async_remote_copy(
            src_ref=packet,
            dst_ref=gathered.at[group, line],
            send_sem=near_send,
            recv_sem=near_recv,
            device_id=near(step),
            device_id_type=MESH,
        )

    def far_copy(step):
        return pltpu.make_async_remote_copy(
            src_ref=gathered.at[group],
            dst_ref=gathered.at[group],
            send_sem=far_send,
            recv_sem=far_recv,
            device_id=far(step),
            device_id_type=MESH,
        )

    def near_all():
        return pltpu.make_async_remote_copy(
            src_ref=gathered.at[0, pl.ds(0, lines - 1)],
            dst_ref=gathered.at[0, pl.ds(0, lines - 1)],
            send_sem=near_send,
            recv_sem=near_recv,
            device_id=near(1),
            device_id_type=MESH,
        )

    def far_all():
        return pltpu.make_async_remote_copy(
            src_ref=gathered.at[pl.ds(0, groups // 2 - 1)],
            dst_ref=gathered.at[pl.ds(0, groups // 2 - 1)],
            send_sem=far_send,
            recv_sem=far_recv,
            device_id=far(1),
            device_id_type=MESH,
        )

    def twin_copy(step):
        return pltpu.make_async_remote_copy(
            src_ref=gathered.at[2 * step + side],
            dst_ref=gathered.at[2 * step + side],
            send_sem=twin_send,
            recv_sem=twin_recv,
            device_id=twin,
            device_id_type=MESH,
        )

    def twin_all():
        return pltpu.make_async_remote_copy(
            src_ref=gathered.at[pl.ds(0, groups // 2)],
            dst_ref=gathered.at[pl.ds(0, groups // 2)],
            send_sem=twin_send,
            recv_sem=twin_recv,
            device_id=twin,
            device_id_type=MESH,
        )

    def keep_own():
        return pltpu.make_async_copy(packet, gathered.at[group, line], keep_sem)

    def begin(copy):
        def body(step, carry):
            copy(step).start()
            return carry

        return body

    def greet(place):
        def body(step, carry):
            pl.semaphore_signal(barrier, inc=1, device_id=place(step), device_id_type=MESH)
            return carry

        return body

    def fetch_tile(s):
        return (
            pltpu.make_async_copy(context.at[s, lead], c_buf.at[s], t_sem.at[0, s]),
            pltpu.make_async_copy(states.at[l - 1, s, lead], x_buf.at[s], t_sem.at[1, s]),
        )

    def fetch_out():
        return pltpu.make_async_copy(w_out.at[l], out_buf, w_sem.at[0])

    def fetch_in(j):
        units = pl.ds(j * chunk, chunk)
        return pltpu.make_async_copy(
            w_in.at[l, :, units], in_buf.at[:, units], w_sem.at[1 + j]
        )

    def fetch_back(j):
        units = pl.ds(j * chunk, chunk)
        return pltpu.make_async_copy(
            w_back.at[l, units], back_buf.at[units], w_sem.at[1 + chunks + j]
        )

    def put_rest(s):
        return pltpu.make_async_copy(x_buf.at[s], rest.at[s], o_sem.at[s])

    barrier = pltpu.get_barrier_semaphore()
    lax.fori_loop(1, lines, greet(near), 0)
    lax.fori_loop(1, groups // 2, greet(far), 0)
    pl.semaphore_signal(barrier, inc=1, device_id=twin, device_id_type=MESH)
    vectors = (b_out, ln1_gain, ln1_bias, b_in, b_back, ln2_gain, ln2_bias)
    small = [
        pltpu.make_async_copy(source, target, v_sem.at[number])
        for number, (source, target) in enumerate(zip(vectors, vec_bufs))
    ]
    b_out, ln1_gain, ln1_bias, b_in, b_back, ln2_gain, ln2_bias = vec_bufs
    queue = [*fetch_tile(0), fetch_out()]
    for j in range(chunks):
        queue.append(fetch_in(j))
        if 0 < j < slots:
            queue += fetch_tile(j)
    queue += [fetch_back(j) for j in range(chunks)]
    queue.reverse()

    def advance(number):
        for _ in range(min(number, len(queue))):
            queue.pop().start()

    for copy in small:
        copy.start()
    advance(3)
    pl.semaphore_wait(barrier, lines + groups // 2 - 1)
    lax.fori_loop(1, lines, begin(near_copy), 0)
    keep_own().start()
    for copy in small:
        copy.wait()
    advance(4)

    def join(s):
        attended = jnp.dot(c_buf[s], out_buf[...], preferred_element_type=f32)
        m_buf[s] = x_buf[s].astype(f32) + (attended + b_out[l : l + 1])

    def norm_first(s, span):
        middle = norm_rows(m_buf[s, span], ln1_gain[l : l + 1], ln1_bias[l : l + 1])
        m_buf[s, span] = middle
        mb_buf[s, span] = middle.astype(bf16)

    def expand(s, j):
        units = slice(j * chunk, (j + 1) * chunk)
        inner = jnp.dot(mb_buf[s], in_buf[:, units], preferred_element_type=f32)
        h_buf[s, :, units] = gelu_twice(inner + b_in[l : l + 1, units]).astype(bf16)

    def contract(s, span):
        back = jnp.dot(h_buf[s, span], back_buf[...], preferred_element_type=f32)
        m_buf[s, span] = m_buf[s, span] + 0.5 * back + b_back[l : l + 1]

    def settle(s, span):
        x_buf[s, span] = norm_rows(
            m_buf[s, span], ln2_gain[l : l + 1], ln2_bias[l : l + 1]
        ).astype(bf16)

    def cut(parts):
        size = rows // parts
        return [slice(t * size, (t + 1) * size) for t in range(parts)]

    for copy in fetch_tile(0):
        copy.wait()
    fetch_out().wait()
    advance(3)
    join(0)
    for span in cut(2):
        norm_first(0, span)
    for s in range(slots):
        if s + 1 < slots:
            for copy in fetch_tile(s + 1):
                copy.wait()
        for j, span in enumerate(cut(chunks)):
            if s == 0:
                fetch_in(j).wait()
                advance(2)
            expand(s, j)
            if j == 0 and s + 1 < slots:
                join(s + 1)
            if s + 1 < slots:
                norm_first(s + 1, span)
            if s == 0 and j == chunks // 2:
                keep_own().wait()
                near_all().wait()
                lax.fori_loop(1, groups // 2, begin(far_copy), 0)
        if s == 0:
            advance(len(queue))
    for j in range(chunks):
        fetch_back(j).wait()
    halves = cut(2)
    steps = [(s, span) for s in range(slots) for span in halves]
    for number, (s, span) in enumerate(steps):
        contract(s, span)
        if number > 0:
            settle(*steps[number - 1])
            if number % 2 == 0:
                put_rest(s - 1).start()
        if number == 2 * slots - 3:
            far_all().wait()
            lax.fori_loop(0, groups // 2, begin(twin_copy), 0)
    settle(*steps[-1])
    put_rest(slots - 1).start()
    twin_all().wait()
    for s in range(slots):
        put_rest(s).wait()


def run_finish(packet, states, context, stacks):
    (_, _, _, w_out, b_out, ln1_gain, ln1_bias, w_in, b_in, w_back, b_back, ln2_gain, ln2_bias) = (
        stacks
    )
    groups, lines = lax.axis_size("wide"), lax.axis_size("narrow")
    slots, length, width = context.shape
    units = w_in.shape[2]
    rows = length - LEAD
    place_hbm = pl.BlockSpec(memory_space=pl.ANY)
    vectors = (b_out, ln1_gain, ln1_bias, b_in, b_back, ln2_gain, ln2_bias)
    return pl.pallas_call(
        finish_kernel,
        name="finish",
        out_shape=(
            jax.ShapeDtypeStruct((groups, lines) + packet.shape, f32),
            jax.ShapeDtypeStruct((slots, rows, width), bf16),
        ),
        in_specs=[place_hbm] * 13,
        out_specs=(place_hbm, place_hbm),
        scratch_shapes=[
            pltpu.VMEM((slots, rows, width), bf16),
            pltpu.VMEM((slots, rows, width), bf16),
            pltpu.VMEM((width, width), bf16),
            pltpu.VMEM((width, units), bf16),
            pltpu.VMEM((units, width), bf16),
            pltpu.VMEM((slots, rows, width), f32),
            pltpu.VMEM((slots, rows, width), bf16),
            pltpu.VMEM((slots, rows, units), bf16),
            [pltpu.VMEM(vector.shape, f32) for vector in vectors],
            pltpu.SemaphoreType.DMA((2, slots)),
            pltpu.SemaphoreType.DMA((1 + 2 * (units // 512),)),
            pltpu.SemaphoreType.DMA((slots,)),
            pltpu.SemaphoreType.DMA((len(vectors),)),
        ]
        + [pltpu.SemaphoreType.DMA] * 7,
        compiler_params=pltpu.CompilerParams(
            collective_id=0,
            has_side_effects=True,
            vmem_limit_bytes=62 * 1024 * 1024,
        ),
    )(
        packet,
        states,
        context,
        w_out,
        w_in,
        w_back,
        *vectors,
    )


def ramps_kernel(
    gathered,
    states_in,
    rest,
    pool_w,
    pool_b,
    cls_w,
    cls_b,
    states,
    logits,
    losses,
    grad_pool_w,
    grad_pool_b,
    grad_cls_w,
    grad_cls_b,
    first_grads,
    all_buf,
    w_buf,
    g_buf,
    score_buf,
    inner_buf,
    rest_buf,
    in_bufs,
    out_bufs,
    w_sem,
    g_sem,
    s_sem,
    i_sem,
    r_sem,
):
    slots, depth, classes = logits.shape
    devices, packet, width = gathered.shape
    own = lax.axis_index("wide") * lax.axis_size("narrow") + lax.axis_index("narrow")

    def fetch(l):
        return pltpu.make_async_copy(pool_w.at[l], w_buf.at[l], w_sem.at[l])

    def put(l, t):
        span = pl.ds(t * 256, 256)
        return pltpu.make_async_copy(
            g_buf.at[l, span], grad_pool_w.at[l, span], g_sem.at[l, t]
        )

    def fetch_rest():
        return pltpu.make_async_copy(rest, rest_buf, s_sem.at[slots])

    def put_rest(s):
        return pltpu.make_async_copy(
            rest_buf.at[s], states.at[depth - 1, s, pl.ds(LEAD, rest.shape[1])], s_sem.at[s]
        )

    inputs = [
        pltpu.make_async_copy(source, target, i_sem.at[number])
        for number, (source, target) in enumerate(zip((pool_b, cls_w, cls_b), in_bufs))
    ]
    results = (logits, losses, grad_pool_b, grad_cls_w, grad_cls_b, first_grads)
    outputs = [
        pltpu.make_async_copy(source, target, r_sem.at[number])
        for number, (source, target) in enumerate(zip(out_bufs, results))
    ]
    pool_b, cls_w, cls_b = in_bufs
    logits, losses, grad_pool_b, grad_cls_w, grad_cls_b, first_grads = out_bufs
    gather_in = pltpu.make_async_copy(gathered, all_buf, s_sem.at[slots + 1])
    gather_in.start()
    for copy in inputs:
        copy.start()
    fetch(0).start()
    gather_in.wait()
    for l in range(1, depth):
        fetch(l).start()
    fetch_rest().start()
    for copy in inputs:
        copy.wait()

    unit = slots + 1
    rows = devices * unit
    pairs = all_buf[...].reshape(devices // 2, 2 * packet, width)
    even = pairs[:, :packet].reshape(rows, width)
    odd = pairs[:, packet:].reshape(rows, width)
    upper = lax.rem(lax.broadcasted_iota(jnp.int32, (rows, width), 0), packet) < unit
    firsts_all = (
        jnp.where(upper, even, pltpu.roll(odd, unit, 0)),
        jnp.where(upper, pltpu.roll(even, rows - unit, 0), odd),
    )
    place = lax.rem(lax.broadcasted_iota(jnp.int32, (rows, 128), 0), unit)
    marks = firsts_all[0][:, :128]
    spread = jnp.full((rows, 128), -1.0, f32)
    for s in range(slots):
        moved = pltpu.roll(marks, rows - (slots - s), 0)
        spread = jnp.where(place == s, moved[:, s : s + 1], spread)
    label_row = spread.T[:1]
    valid = (label_row >= 0).astype(f32)
    count = jnp.sum(valid, 1, keepdims=True)
    class_column = lax.broadcasted_iota(jnp.int32, (classes, rows), 0).astype(f32)
    onehot = (label_row == class_column).astype(f32)

    def mine(pair):
        return jnp.where(lax.rem(own, 2) == 0, pair[:slots], pair[unit : unit + slots])

    def dot(a, b):
        return jnp.dot(a, b, preferred_element_type=f32)

    def dot_turned(a, b):
        return lax.dot_general(a, b, (((1,), (1,)), ((), ())), preferred_element_type=f32)

    for l in range(depth):
        firsts_low = firsts_all[l].astype(bf16)
        firsts_turned = firsts_all[l].T.astype(bf16)
        cls = cls_w[:, l]
        cls_high, cls_low = split(cls)
        fetch(l).wait()
        weights, weights_low = split(w_buf[l])
        pooled = jnp.tanh(
            dot(firsts_low, weights) + dot(firsts_low, weights_low) + pool_b[l : l + 1]
        )
        pooled_high, pooled_low = split(pooled)
        scores = (
            dot_turned(cls_high, pooled_high)
            + (dot_turned(cls_low, pooled_high) + dot_turned(cls_high, pooled_low))
            + cls_b[l : l + 1].T
        )
        highest = jnp.max(scores, 0, keepdims=True)
        raised = jnp.exp(scores - highest)
        totals = jnp.sum(raised, 0, keepdims=True)
        grad = valid * (raised / totals - onehot) / count
        grad_column = grad.T
        inner = grad_column[:, 0:1] * cls[0:1]
        for c in range(1, classes):
            inner = inner + grad_column[:, c : c + 1] * cls[c : c + 1]
        inner = inner * (1.0 - pooled * pooled)
        inner_high, inner_low = split(inner)
        for t in range(width // 256):
            span = slice(t * 256, (t + 1) * 256)
            g_buf[l, span] = dot(firsts_turned[span], inner_high) + dot(
                firsts_turned[span], inner_low
            )
            put(l, t).start()
        grad_high, grad_low = split(grad)
        grad_cls_w[:, l] = dot(grad_high, pooled_high) + (
            dot(grad_low, pooled_high) + dot(grad_high, pooled_low)
        )
        inner_buf[...] = inner.reshape(devices // 2, packet, width)
        own_high, own_low = split(inner_buf[own // 2])
        own_grads = dot_turned(own_high, weights) + dot_turned(own_low, weights)
        first_grads[:, l] = mine(own_grads)
        grad_pool_b[l : l + 1] = jnp.sum(inner, 0, keepdims=True)
        grad_cls_b[l : l + 1] = jnp.sum(grad, 1, keepdims=True).T
        log_total = highest + jnp.log(totals)
        picked = jnp.sum(scores * onehot, 0, keepdims=True)
        losses[l] = jnp.sum(valid * (log_total - picked) / count)
        score_buf[...] = scores.T.reshape(devices // 2, packet, classes)
        logits[:, l] = mine(score_buf[own // 2])
        if l == 0:
            fetch_rest().wait()
            for s in range(slots):
                put_rest(s).start()
    for copy in outputs:
        copy.start()
    for l in range(depth):
        for t in range(width // 256):
            put(l, t).wait()
    for copy in outputs:
        copy.wait()
    for s in range(slots):
        put_rest(s).wait()


def run_ramps(gathered, states, rest, pool_w, pool_b, cls_w, cls_b):
    devices, packet, width = gathered.shape
    depth, classes = cls_b.shape
    slots = rest.shape[0]
    pairs = devices // 2
    place_hbm = pl.BlockSpec(memory_space=pl.ANY)
    cls_turned = jnp.transpose(cls_w, (2, 0, 1))
    states, logits, losses, pool_grad, pool_shift, cls_grad, cls_shift, first_grads = pl.pallas_call(
        ramps_kernel,
        name="ramps",
        out_shape=(
            jax.ShapeDtypeStruct(states.shape, states.dtype),
            jax.ShapeDtypeStruct((slots, depth, classes), f32),
            jax.ShapeDtypeStruct((depth,), f32),
            jax.ShapeDtypeStruct((depth, width, width), f32),
            jax.ShapeDtypeStruct((depth, width), f32),
            jax.ShapeDtypeStruct((classes, depth, width), f32),
            jax.ShapeDtypeStruct((depth, classes), f32),
            jax.ShapeDtypeStruct((slots, depth, width), f32),
        ),
        in_specs=[place_hbm] * 7,
        out_specs=(place_hbm,) * 8,
        input_output_aliases={1: 0},
        scratch_shapes=[
            pltpu.VMEM(gathered.shape, f32),
            pltpu.VMEM((depth, width, width), f32),
            pltpu.VMEM((depth, width, width), f32),
            pltpu.VMEM((pairs, packet, classes), f32),
            pltpu.VMEM((pairs, packet, width), f32),
            pltpu.VMEM(rest.shape, bf16),
            [pltpu.VMEM(member.shape, f32) for member in (pool_b, cls_turned, cls_b)],
            [
                pltpu.VMEM((slots, depth, classes), f32),
                pltpu.SMEM((depth,), f32),
                pltpu.VMEM((depth, width), f32),
                pltpu.VMEM((classes, depth, width), f32),
                pltpu.VMEM((depth, classes), f32),
                pltpu.VMEM((slots, depth, width), f32),
            ],
            pltpu.SemaphoreType.DMA((depth,)),
            pltpu.SemaphoreType.DMA((depth, width // 256)),
            pltpu.SemaphoreType.DMA((slots + 2,)),
            pltpu.SemaphoreType.DMA((3,)),
            pltpu.SemaphoreType.DMA((6,)),
        ],
        compiler_params=pltpu.CompilerParams(vmem_limit_bytes=62 * 1024 * 1024),
    )(gathered, states, rest, pool_w, pool_b, cls_turned, cls_b)
    return (
        states,
        jnp.transpose(logits, (1, 0, 2)),
        losses,
        pool_grad,
        pool_shift,
        jnp.transpose(cls_grad, (1, 2, 0)),
        cls_shift,
        jnp.transpose(first_grads, (1, 0, 2)),
    )


def local(
    hidden,
    lengths,
    slot_order,
    labels,
    w_qkv,
    b_query,
    b_value,
    w_out,
    b_out,
    ln1_gain,
    ln1_bias,
    w_in,
    b_in,
    w_back,
    b_back,
    ln2_gain,
    ln2_bias,
    pool_w,
    pool_b,
    cls_w,
    cls_b,
):
    stacks = (
        w_qkv,
        b_query,
        b_value,
        w_out,
        b_out,
        ln1_gain,
        ln1_bias,
        w_in,
        b_in,
        w_back,
        b_back,
        ln2_gain,
        ln2_bias,
    )
    states, context, packet = run_blocks(hidden, lengths, slot_order, labels, stacks)
    gathered, rest = run_finish(packet, states, context, stacks)
    gathered = gathered.reshape((-1,) + packet.shape)
    return run_ramps(gathered, states, rest, pool_w, pool_b, cls_w, cls_b)


def solution(mesh):
    both = ("wide", "narrow")
    return jax.shard_map(
        local,
        mesh=mesh,
        in_specs=(P(both, None, None), P(both), P(both), P(both)) + (P(),) * 17,
        out_specs=(
            P(None, both, None, None),
            P(None, both, None),
            P(),
            P(),
            P(),
            P(),
            P(),
            P(None, both, None),
        ),
        check_vma=False,
    )
```

```python
import functools
import math

import jax
import jax.numpy as jnp
from jax import lax
from jax.experimental import pallas as pl
from jax.experimental.pallas import tpu as pltpu
from jax.sharding import PartitionSpec as P

HEAD = 64
LEAD = 128
MESH = pl.DeviceIdType.MESH
epsilon = 1e-12
bf16 = jnp.bfloat16
f32 = jnp.float32
SCALE = HEAD**-0.5 * math.log2(math.e)
SUM_LOW = 2.0**-60
SUM_HIGH = 2.0**100


def split(values):
    high = values.astype(bf16)
    return high, (values - high.astype(f32)).astype(bf16)


def gelu_twice(values):
    return values * (1.0 + lax.erf(values * math.sqrt(0.5)))


def norm_rows(values, gain, shift):
    center = values - jnp.mean(values, -1, keepdims=True)
    spread = jnp.mean(center * center, -1, keepdims=True)
    return center * lax.rsqrt(spread + epsilon) * gain + shift


def blocks_kernel(
    order,
    lens,
    labels,
    hidden,
    w_qkv,
    w_out,
    w_in,
    w_back,
    b_query,
    b_value,
    b_out,
    ln1_gain,
    ln1_bias,
    b_in,
    b_back,
    ln2_gain,
    ln2_bias,
    states,
    context,
    packet,
    x_buf,
    last_buf,
    qkv_buf,
    out_buf,
    in_buf,
    back_buf,
    turned,
    columns,
    q_buf,
    k_buf,
    v_buf,
    p_buf,
    ct_buf,
    c_buf,
    m_buf,
    mb_buf,
    y_buf,
    h_buf,
    fine,
    vec_bufs,
    packet_buf,
    order_buf,
    lens_buf,
    labels_buf,
    w_sem,
    x_sem,
    o_sem,
    c_sem,
    v_sem,
):
    depth, width = b_query.shape
    slots, length = x_buf.shape[1:3]
    heads = width // HEAD
    hidden_units = b_in.shape[1]
    lead = last_buf.shape[0] // slots
    tile = length // 2
    spans = [slice(t * tile, (t + 1) * tile) for t in range(2)]

    def fetch_x(s):
        return pltpu.make_async_copy(hidden.at[order[s]], x_buf.at[0, s], x_sem.at[s])

    def fetch_qkv(l, part):
        cols = pl.ds(part * width, width)
        return pltpu.make_async_copy(
            w_qkv.at[l, :, cols], qkv_buf.at[l, :, cols], w_sem.at[l, part]
        )

    def fetch_rest(l, number):
        source = (w_out, w_in, w_back)[number]
        target = (out_buf, in_buf, back_buf)[number]
        return pltpu.make_async_copy(source.at[l], target.at[l], w_sem.at[l, 3 + number])

    def put_states(l, s):
        return pltpu.make_async_copy(x_buf.at[l + 1, s], states.at[l, s], o_sem.at[l, s])

    def put_last(s):
        return pltpu.make_async_copy(
            last_buf.at[pl.ds(s * lead, lead)],
            states.at[depth - 1, s, pl.ds(0, lead)],
            o_sem.at[depth - 1, s],
        )

    def put_context(s):
        rows = pl.ds(lead, length - lead)
        return pltpu.make_async_copy(c_buf.at[s, rows], context.at[s, rows], c_sem.at[s])

    vectors = (b_query, b_value, b_out, ln1_gain, ln1_bias, b_in, b_back, ln2_gain, ln2_bias)
    scalars = ((order, order_buf), (lens, lens_buf), (labels, labels_buf))
    small = [
        pltpu.make_async_copy(source, target, v_sem.at[number])
        for number, (source, target) in enumerate((*scalars, *zip(vectors, vec_bufs)))
    ]
    put_packet = pltpu.make_async_copy(packet_buf, packet, v_sem.at[0])
    order, lens, labels = order_buf, lens_buf, labels_buf
    b_query, b_value, b_out, ln1_gain, ln1_bias, b_in, b_back, ln2_gain, ln2_bias = vec_bufs
    for copy in small[:5]:
        copy.start()
    fetch_qkv(0, 0).start()
    fetch_qkv(0, 2).start()
    fetch_qkv(0, 1).start()
    for copy in small[5:]:
        copy.start()
    q_buf[...] = jnp.zeros_like(q_buf)
    small[0].wait()
    fetch_x(0).start()
    for copy in small[1:]:
        copy.wait()

    for l in range(depth):
        for number, bias in enumerate((b_query, b_value)):
            for j in range(width // 128):
                offset = number * width + j * 128
                columns[l, offset : offset + 128] = jnp.broadcast_to(
                    bias[l : l + 1, j * 128 : (j + 1) * 128], (128, 128)
                ).T

    def turn(l, block):
        skip = jnp.where(block >= width // 128, width, 0)
        lanes = pl.ds(pl.multiple_of(block * 128 + skip, 128), 128)
        rows = pl.ds(pl.multiple_of(block * 128, 128), 128)
        turned[rows] = qkv_buf[l, :, lanes].T

    def project(l, s, keys):
        rows = x_buf[l, s]
        some = rows[:keys]
        k_buf[:keys] = jnp.dot(
            some, qkv_buf[l, :, width : 2 * width], preferred_element_type=f32
        ).astype(bf16)
        seen = (
            lax.broadcasted_iota(jnp.int32, (HEAD, keys), 1) < lens[order[s]]
        ).astype(f32)
        queries = lax.dot_general(
            turned[:width], rows, (((1,), (1,)), ((), ())), preferred_element_type=f32
        )
        values = lax.dot_general(
            turned[width:], some, (((1,), (1,)), ((), ())), preferred_element_type=f32
        )
        for h in range(heads):
            at = slice(h * HEAD, (h + 1) * HEAD)
            half = slice((h % 2) * HEAD, (h % 2 + 1) * HEAD)
            q_buf[h, half] = (
                queries[at] + jnp.tile(columns[l, at, :], (1, length // 128))
            ).astype(bf16)
            av = slice(width + h * HEAD, width + (h + 1) * HEAD)
            v_buf[h, :HEAD, :keys] = (
                (values[at] + jnp.tile(columns[l, av, :], (1, keys // 128))) * seen
            ).astype(bf16)
            v_buf[h, HEAD:, :keys] = seen.astype(bf16)

    def attend(s, keys):
        def score(h):
            pair = slice((h // 2) * 128, (h // 2 + 1) * 128)
            scores = jnp.dot(k_buf[:keys, pair], q_buf[h], preferred_element_type=f32)
            p_buf[h % 4, :keys] = jnp.exp2(scores * SCALE).astype(bf16)

        def mix(h):
            both = jnp.dot(
                v_buf[h, :, :keys], p_buf[h % 4, :keys], preferred_element_type=f32
            )
            sums = both[HEAD:]
            good = (sums[:8] >= SUM_LOW) & (sums[:8] <= SUM_HIGH)
            fine[...] = jnp.where(good, fine[...], 0.0)
            half = slice((h % 2) * HEAD, (h % 2 + 1) * HEAD)
            ct_buf[(h // 2) % 2, half] = (both[:HEAD] * (1.0 / sums)).astype(bf16)
            if h % 2 == 1:
                pair = slice((h // 2) * 128, (h // 2 + 1) * 128)
                c_buf[s, :, pair] = ct_buf[(h // 2) % 2].T

        score(0)
        for h in range(heads):
            if h + 1 < heads:
                score(h + 1)
            mix(h)

    def attend_shifted(s):
        count = lens[order[s]]

        def pair_step(number, carry):
            lanes = pl.ds(pl.multiple_of(number * 128, 128), 128)
            for side in range(2):
                h = number * 2 + side
                scores = (
                    jnp.dot(k_buf[:, lanes], q_buf[h], preferred_element_type=f32) * SCALE
                )
                seen = lax.broadcasted_iota(jnp.int32, scores.shape, 0) < count
                scores = jnp.where(seen, scores, -1e30)
                highest = jnp.max(scores, 0, keepdims=True)
                p_buf[side] = jnp.exp2(scores - highest).astype(bf16)
                both = jnp.dot(v_buf[h], p_buf[side], preferred_element_type=f32)
                ct_buf[0, side * HEAD : (side + 1) * HEAD] = (
                    both[:HEAD] / both[HEAD:]
                ).astype(bf16)
            c_buf[s, :, lanes] = ct_buf[0].T
            return carry

        lax.fori_loop(0, heads // 2, pair_step, 0)

    def front(l):
        fine[...] = jnp.ones_like(fine)

        def step(s, carry):
            @pl.when(l == 0)
            def _():
                fetch_x(s).wait()

            tiles = (lens[order[s]] + 127) // 128
            for number in range(1, length // 128 + 1):

                @pl.when(tiles == number)
                def _(number=number):
                    project(l, s, number * 128)
                    attend(s, number * 128)

            return carry

        lax.fori_loop(0, slots, step, 0)

        @pl.when(jnp.min(fine[...]) < 0.5)
        def _():
            def again(s, carry):
                project(l, s, length)
                attend_shifted(s)
                return carry

            lax.fori_loop(0, slots, again, 0)

    def join(l, slot, contexts, inputs):
        attended = jnp.dot(contexts, out_buf[l], preferred_element_type=f32)
        values = inputs.astype(f32) + (attended + b_out[l : l + 1])
        middle = norm_rows(values, ln1_gain[l : l + 1], ln1_bias[l : l + 1])
        size = middle.shape[0]
        m_buf[slot, :size] = middle
        mb_buf[slot, :size] = middle.astype(bf16)

    def expand(l, slot, size=tile):
        chunk = 512
        for j in range(hidden_units // chunk):
            units = slice(j * chunk, (j + 1) * chunk)
            inner = jnp.dot(mb_buf[slot, :size], in_buf[l, :, units], preferred_element_type=f32)
            h_buf[slot, :size, units] = gelu_twice(inner + b_in[l : l + 1, units]).astype(bf16)

    def contract(l, slot, size=tile):
        back = jnp.dot(h_buf[slot, :size], back_buf[l], preferred_element_type=f32)
        y_buf[slot, :size] = m_buf[slot, :size] + 0.5 * back + b_back[l : l + 1]

    def settle(l, slot, size=tile):
        return norm_rows(y_buf[slot, :size], ln2_gain[l : l + 1], ln2_bias[l : l + 1]).astype(bf16)

    def rear(l):
        def enter(s, half):
            join(l, half, c_buf[s, spans[half]], x_buf[l, s, spans[half]])

        enter(0, 0)

        def step(s, carry):
            x_buf[l + 1, jnp.maximum(s - 1, 0), spans[1]] = settle(l, 1)
            expand(l, 0)
            enter(s, 1)
            contract(l, 0)
            x_buf[l + 1, s, spans[0]] = settle(l, 0)
            expand(l, 1)
            enter(jnp.minimum(s + 1, slots - 1), 0)
            contract(l, 1)
            blocks = 2 * width // 128 // slots
            for number in range(blocks):
                turn(l + 1, s * blocks + number)

            @pl.when(s > 0)
            def _():
                put_states(l, s - 1).start()

            return carry

        lax.fori_loop(0, slots, step, 0)
        x_buf[l + 1, slots - 1, spans[1]] = settle(l, 1)
        put_states(l, slots - 1).start()

    def rear_lead(l):
        half = slots * lead // 2
        contexts = jnp.concatenate([c_buf[s, :lead] for s in range(slots)])
        inputs = jnp.concatenate([x_buf[l, s, :lead] for s in range(slots)])
        for t in range(2):
            rows = slice(t * half, (t + 1) * half)
            join(l, t, contexts[rows], inputs[rows])
        for t in range(2):
            expand(l, t, half)
        for t in range(2):
            contract(l, t, half)
        for t in range(2):
            last_buf[t * half : (t + 1) * half] = settle(l, t, half)
        for s in range(slots):
            put_last(s).start()

    for part in (0, 2):
        fetch_qkv(0, part).wait()
        for j in range(width // 128):
            turn(0, part // 2 * (width // 128) + j)
    fetch_qkv(0, 1).wait()
    for number in range(1, slots):
        fetch_x(number).start()

    def layer(l, carry):
        for number in range(3):
            fetch_rest(l, number).start()

        @pl.when(l < depth - 1)
        def _():
            for part in range(3):
                fetch_qkv(l + 1, part).start()

        front(l)

        @pl.when(l == depth - 1)
        def _():
            for s in range(slots):
                put_context(s).start()

        for number in range(3):
            fetch_rest(l, number).wait()

        for k in range(depth - 1):

            @pl.when(l == k)
            def _(k=k):
                for part in range(3):
                    fetch_qkv(k + 1, part).wait()
                rear(k)

        return carry

    lax.fori_loop(0, depth, layer, 0)
    rear_lead(depth - 1)
    lane = lax.broadcasted_iota(jnp.int32, packet.shape, 1)
    place = lax.broadcasted_iota(jnp.int32, packet.shape, 0)
    marks = jnp.zeros(packet.shape, f32)
    for s in range(slots):
        marks = jnp.where(lane == s, labels[order[s]].astype(f32), marks)
    packet_buf[...] = jnp.where(place == slots, marks, 0.0)
    for l in range(depth):
        for s in range(slots):
            row = l * (slots + 1) + s
            if l < depth - 1:
                packet_buf[row : row + 1] = x_buf[l + 1, s, 0:1].astype(f32)
            else:
                packet_buf[row : row + 1] = last_buf[s * lead : s * lead + 1].astype(f32)
    put_packet.start()
    for s in range(slots):
        for l in range(depth - 1):
            put_states(l, s).wait()
        put_last(s).wait()
        put_context(s).wait()
    put_packet.wait()


def run_blocks(hidden, lengths, slot_order, labels, stacks):
    (
        w_qkv,
        b_query,
        b_value,
        w_out,
        b_out,
        ln1_gain,
        ln1_bias,
        w_in,
        b_in,
        w_back,
        b_back,
        ln2_gain,
        ln2_bias,
    ) = stacks
    slots, length, width = hidden.shape
    depth = w_qkv.shape[0]
    units = w_in.shape[2]
    heads = width // HEAD
    tile = length // 2
    vectors = (b_query, b_value, b_out, ln1_gain, ln1_bias, b_in, b_back, ln2_gain, ln2_bias)
    place_hbm = pl.BlockSpec(memory_space=pl.ANY)
    return pl.pallas_call(
        blocks_kernel,
        name="blocks",
        out_shape=(
            jax.ShapeDtypeStruct((depth, slots, length, width), bf16),
            jax.ShapeDtypeStruct((slots, length, width), bf16),
            jax.ShapeDtypeStruct((depth * (slots + 1), width), f32),
        ),
        in_specs=[place_hbm] * 17,
        out_specs=(place_hbm,) * 3,
        scratch_shapes=[
            pltpu.VMEM((depth, slots, length, width), bf16),
            pltpu.VMEM((slots * LEAD, width), bf16),
            pltpu.VMEM((depth, width, 3 * width), bf16),
            pltpu.VMEM((depth, width, width), bf16),
            pltpu.VMEM((depth, width, units), bf16),
            pltpu.VMEM((depth, units, width), bf16),
            pltpu.VMEM((2 * width, width), bf16),
            pltpu.VMEM((depth, 2 * width, 128), f32),
            pltpu.VMEM((heads, 2 * HEAD, length), bf16),
            pltpu.VMEM((length, width), bf16),
            pltpu.VMEM((heads, 2 * HEAD, length), bf16),
            pltpu.VMEM((4, length, length), bf16),
            pltpu.VMEM((2, 2 * HEAD, length), bf16),
            pltpu.VMEM((slots, length, width), bf16),
            pltpu.VMEM((2, tile, width), f32),
            pltpu.VMEM((2, tile, width), bf16),
            pltpu.VMEM((2, tile, width), f32),
            pltpu.VMEM((2, tile, units), bf16),
            pltpu.VMEM((8, length), f32),
            [pltpu.VMEM(vector.shape, f32) for vector in vectors],
            pltpu.VMEM((depth * (slots + 1), width), f32),
            pltpu.SMEM((slots,), jnp.int32),
            pltpu.SMEM((slots,), jnp.int32),
            pltpu.SMEM((slots,), jnp.int32),
            pltpu.SemaphoreType.DMA((depth, 6)),
            pltpu.SemaphoreType.DMA((slots,)),
            pltpu.SemaphoreType.DMA((depth, slots)),
            pltpu.SemaphoreType.DMA((slots,)),
            pltpu.SemaphoreType.DMA((3 + len(vectors),)),
        ],
        compiler_params=pltpu.CompilerParams(vmem_limit_bytes=62 * 1024 * 1024),
    )(
        slot_order,
        lengths,
        labels,
        hidden,
        w_qkv,
        w_out,
        w_in,
        w_back,
        *vectors,
    )


def finish_kernel(
    packet,
    states,
    context,
    w_out,
    w_in,
    w_back,
    b_out,
    ln1_gain,
    ln1_bias,
    b_in,
    b_back,
    ln2_gain,
    ln2_bias,
    gathered,
    rest,
    x_buf,
    c_buf,
    out_buf,
    in_buf,
    back_buf,
    m_buf,
    mb_buf,
    h_buf,
    vec_bufs,
    t_sem,
    w_sem,
    o_sem,
    v_sem,
    keep_sem,
    near_send,
    near_recv,
    far_send,
    far_recv,
    twin_send,
    twin_recv,
):
    groups, lines = gathered.shape[:2]
    group, line = lax.axis_index("wide"), lax.axis_index("narrow")
    depth, slots = states.shape[:2]
    rows, width = x_buf.shape[1:]
    hidden_units = b_in.shape[1]
    chunk = 512
    chunks = hidden_units // chunk
    l = depth - 1
    lead = pl.ds(LEAD, rows)

    def near(step):
        return (group, lax.rem(line + step, lines))

    side = lax.rem(group, 2)

    def far(step):
        return (lax.rem(group + 2 * step, groups), line)

    twin = (group + 1 - 2 * side, line)

    def near_copy(step):
        return pltpu.make_async_remote_copy(
            src_ref=packet,
            dst_ref=gathered.at[group, line],
            send_sem=near_send,
            recv_sem=near_recv,
            device_id=near(step),
            device_id_type=MESH,
        )

    def far_copy(step):
        return pltpu.make_async_remote_copy(
            src_ref=gathered.at[group],
            dst_ref=gathered.at[group],
            send_sem=far_send,
            recv_sem=far_recv,
            device_id=far(step),
            device_id_type=MESH,
        )

    def near_all():
        return pltpu.make_async_remote_copy(
            src_ref=gathered.at[0, pl.ds(0, lines - 1)],
            dst_ref=gathered.at[0, pl.ds(0, lines - 1)],
            send_sem=near_send,
            recv_sem=near_recv,
            device_id=near(1),
            device_id_type=MESH,
        )

    def far_all():
        return pltpu.make_async_remote_copy(
            src_ref=gathered.at[pl.ds(0, groups // 2 - 1)],
            dst_ref=gathered.at[pl.ds(0, groups // 2 - 1)],
            send_sem=far_send,
            recv_sem=far_recv,
            device_id=far(1),
            device_id_type=MESH,
        )

    def twin_copy(step):
        return pltpu.make_async_remote_copy(
            src_ref=gathered.at[2 * step + side],
            dst_ref=gathered.at[2 * step + side],
            send_sem=twin_send,
            recv_sem=twin_recv,
            device_id=twin,
            device_id_type=MESH,
        )

    def twin_all():
        return pltpu.make_async_remote_copy(
            src_ref=gathered.at[pl.ds(0, groups // 2)],
            dst_ref=gathered.at[pl.ds(0, groups // 2)],
            send_sem=twin_send,
            recv_sem=twin_recv,
            device_id=twin,
            device_id_type=MESH,
        )

    def keep_own():
        return pltpu.make_async_copy(packet, gathered.at[group, line], keep_sem)

    def begin(copy):
        def body(step, carry):
            copy(step).start()
            return carry

        return body

    def greet(place):
        def body(step, carry):
            pl.semaphore_signal(barrier, inc=1, device_id=place(step), device_id_type=MESH)
            return carry

        return body

    def fetch_tile(s):
        return (
            pltpu.make_async_copy(context.at[s, lead], c_buf.at[s], t_sem.at[0, s]),
            pltpu.make_async_copy(states.at[l - 1, s, lead], x_buf.at[s], t_sem.at[1, s]),
        )

    def fetch_out():
        return pltpu.make_async_copy(w_out.at[l], out_buf, w_sem.at[0])

    def fetch_in(j):
        units = pl.ds(j * chunk, chunk)
        return pltpu.make_async_copy(
            w_in.at[l, :, units], in_buf.at[:, units], w_sem.at[1 + j]
        )

    def fetch_back(j):
        units = pl.ds(j * chunk, chunk)
        return pltpu.make_async_copy(
            w_back.at[l, units], back_buf.at[units], w_sem.at[1 + chunks + j]
        )

    def put_rest(s, span):
        part = pl.ds(span.start, span.stop - span.start)
        return pltpu.make_async_copy(
            x_buf.at[s, part], rest.at[s, part], o_sem.at[s, span.start * 2 // rows]
        )

    barrier = pltpu.get_barrier_semaphore()
    vectors = (b_out, ln1_gain, ln1_bias, b_in, b_back, ln2_gain, ln2_bias)
    small = [
        pltpu.make_async_copy(source, target, v_sem.at[number])
        for number, (source, target) in enumerate(zip(vectors, vec_bufs))
    ]
    b_out, ln1_gain, ln1_bias, b_in, b_back, ln2_gain, ln2_bias = vec_bufs
    queue = [*fetch_tile(0), fetch_out()]
    for j in range(chunks):
        queue.append(fetch_in(j))
        if 0 < j < slots:
            queue += fetch_tile(j)
    queue += [fetch_back(j) for j in range(chunks)]
    queue.reverse()

    def advance(number):
        for _ in range(min(number, len(queue))):
            queue.pop().start()

    advance(3)
    for copy in small:
        copy.start()
    lax.fori_loop(1, lines, greet(near), 0)
    lax.fori_loop(1, groups // 2, greet(far), 0)
    pl.semaphore_signal(barrier, inc=1, device_id=twin, device_id_type=MESH)
    pl.semaphore_wait(barrier, lines + groups // 2 - 1)
    lax.fori_loop(1, lines, begin(near_copy), 0)
    keep_own().start()
    for copy in small:
        copy.wait()
    advance(4)

    def join(s):
        attended = jnp.dot(c_buf[s], out_buf[...], preferred_element_type=f32)
        m_buf[s] = x_buf[s].astype(f32) + (attended + b_out[l : l + 1])

    def norm_first(s, span):
        middle = norm_rows(m_buf[s, span], ln1_gain[l : l + 1], ln1_bias[l : l + 1])
        m_buf[s, span] = middle
        mb_buf[s, span] = middle.astype(bf16)

    def expand(s, j):
        units = slice(j * chunk, (j + 1) * chunk)
        inner = jnp.dot(mb_buf[s], in_buf[:, units], preferred_element_type=f32)
        h_buf[s, :, units] = gelu_twice(inner + b_in[l : l + 1, units]).astype(bf16)

    def contract(s, span):
        back = jnp.dot(h_buf[s, span], back_buf[...], preferred_element_type=f32)
        m_buf[s, span] = m_buf[s, span] + 0.5 * back + b_back[l : l + 1]

    def settle(s, span):
        x_buf[s, span] = norm_rows(
            m_buf[s, span], ln2_gain[l : l + 1], ln2_bias[l : l + 1]
        ).astype(bf16)

    def cut(parts):
        size = rows // parts
        return [slice(t * size, (t + 1) * size) for t in range(parts)]

    for copy in fetch_tile(0):
        copy.wait()
    fetch_out().wait()
    advance(3)
    join(0)
    for span in cut(2):
        norm_first(0, span)
    for s in range(slots):
        if s + 1 < slots:
            for copy in fetch_tile(s + 1):
                copy.wait()
        for j, span in enumerate(cut(chunks)):
            if s == 0:
                fetch_in(j).wait()
                advance(2)
            expand(s, j)
            if j == 0 and s + 1 < slots:
                join(s + 1)
            if s + 1 < slots:
                norm_first(s + 1, span)
            if s == 0 and j == chunks // 2:
                keep_own().wait()
                near_all().wait()
                lax.fori_loop(1, groups // 2, begin(far_copy), 0)
        if s == 0:
            advance(len(queue))
    for j in range(chunks):
        fetch_back(j).wait()
    halves = cut(2)
    steps = [(s, span) for s in range(slots) for span in halves]
    for number, (s, span) in enumerate(steps):
        contract(s, span)
        if number > 0:
            settle(*steps[number - 1])
            put_rest(*steps[number - 1]).start()
        if number == 2 * slots - 3:
            far_all().wait()
            lax.fori_loop(0, groups // 2, begin(twin_copy), 0)
    settle(*steps[-1])
    put_rest(*steps[-1]).start()
    twin_all().wait()
    for step in steps:
        put_rest(*step).wait()


def run_finish(packet, states, context, stacks):
    (_, _, _, w_out, b_out, ln1_gain, ln1_bias, w_in, b_in, w_back, b_back, ln2_gain, ln2_bias) = (
        stacks
    )
    groups, lines = lax.axis_size("wide"), lax.axis_size("narrow")
    slots, length, width = context.shape
    units = w_in.shape[2]
    rows = length - LEAD
    place_hbm = pl.BlockSpec(memory_space=pl.ANY)
    vectors = (b_out, ln1_gain, ln1_bias, b_in, b_back, ln2_gain, ln2_bias)
    return pl.pallas_call(
        finish_kernel,
        name="finish",
        out_shape=(
            jax.ShapeDtypeStruct((groups, lines) + packet.shape, f32),
            jax.ShapeDtypeStruct((slots, rows, width), bf16),
        ),
        in_specs=[place_hbm] * 13,
        out_specs=(place_hbm, place_hbm),
        scratch_shapes=[
            pltpu.VMEM((slots, rows, width), bf16),
            pltpu.VMEM((slots, rows, width), bf16),
            pltpu.VMEM((width, width), bf16),
            pltpu.VMEM((width, units), bf16),
            pltpu.VMEM((units, width), bf16),
            pltpu.VMEM((slots, rows, width), f32),
            pltpu.VMEM((slots, rows, width), bf16),
            pltpu.VMEM((slots, rows, units), bf16),
            [pltpu.VMEM(vector.shape, f32) for vector in vectors],
            pltpu.SemaphoreType.DMA((2, slots)),
            pltpu.SemaphoreType.DMA((1 + 2 * (units // 512),)),
            pltpu.SemaphoreType.DMA((slots, 2)),
            pltpu.SemaphoreType.DMA((len(vectors),)),
        ]
        + [pltpu.SemaphoreType.DMA] * 7,
        compiler_params=pltpu.CompilerParams(
            collective_id=0,
            has_side_effects=True,
            vmem_limit_bytes=62 * 1024 * 1024,
        ),
    )(
        packet,
        states,
        context,
        w_out,
        w_in,
        w_back,
        *vectors,
    )


def ramps_kernel(
    gathered,
    states_in,
    rest,
    pool_w,
    pool_b,
    cls_w,
    cls_b,
    states,
    logits,
    losses,
    grad_pool_w,
    grad_pool_b,
    grad_cls_w,
    grad_cls_b,
    first_grads,
    all_buf,
    w_buf,
    g_buf,
    score_buf,
    inner_buf,
    rest_buf,
    in_bufs,
    out_bufs,
    w_sem,
    g_sem,
    s_sem,
    i_sem,
    r_sem,
):
    slots, depth, classes = logits.shape
    devices, packet, width = gathered.shape
    own = lax.axis_index("wide") * lax.axis_size("narrow") + lax.axis_index("narrow")

    def fetch(l):
        return pltpu.make_async_copy(pool_w.at[l], w_buf.at[l], w_sem.at[l])

    def put(l, t):
        span = pl.ds(t * 256, 256)
        return pltpu.make_async_copy(
            g_buf.at[l, span], grad_pool_w.at[l, span], g_sem.at[l, t]
        )

    def fetch_rest():
        return pltpu.make_async_copy(rest, rest_buf, s_sem.at[slots])

    def put_rest(s):
        return pltpu.make_async_copy(
            rest_buf.at[s], states.at[depth - 1, s, pl.ds(LEAD, rest.shape[1])], s_sem.at[s]
        )

    inputs = [
        pltpu.make_async_copy(source, target, i_sem.at[number])
        for number, (source, target) in enumerate(zip((pool_b, cls_w, cls_b), in_bufs))
    ]
    results = (logits, losses, grad_pool_b, grad_cls_w, grad_cls_b, first_grads)
    outputs = [
        pltpu.make_async_copy(source, target, r_sem.at[number])
        for number, (source, target) in enumerate(zip(out_bufs, results))
    ]
    pool_b, cls_w, cls_b = in_bufs
    logits, losses, grad_pool_b, grad_cls_w, grad_cls_b, first_grads = out_bufs
    gather_in = pltpu.make_async_copy(gathered, all_buf, s_sem.at[slots + 1])
    gather_in.start()
    for copy in inputs:
        copy.start()
    fetch(0).start()
    gather_in.wait()
    for l in range(1, depth):
        fetch(l).start()
    fetch_rest().start()
    for copy in inputs:
        copy.wait()

    unit = slots + 1
    rows = devices * unit
    pairs = all_buf[...].reshape(devices // 2, 2 * packet, width)
    even = pairs[:, :packet].reshape(rows, width)
    odd = pairs[:, packet:].reshape(rows, width)
    upper = lax.rem(lax.broadcasted_iota(jnp.int32, (rows, width), 0), packet) < unit
    firsts_all = (
        jnp.where(upper, even, pltpu.roll(odd, unit, 0)),
        jnp.where(upper, pltpu.roll(even, rows - unit, 0), odd),
    )
    place = lax.rem(lax.broadcasted_iota(jnp.int32, (rows, 128), 0), unit)
    marks = firsts_all[0][:, :128]
    spread = jnp.full((rows, 128), -1.0, f32)
    for s in range(slots):
        moved = pltpu.roll(marks, rows - (slots - s), 0)
        spread = jnp.where(place == s, moved[:, s : s + 1], spread)
    label_row = spread.T[:1]
    valid = (label_row >= 0).astype(f32)
    count = jnp.sum(valid, 1, keepdims=True)
    class_column = lax.broadcasted_iota(jnp.int32, (classes, rows), 0).astype(f32)
    onehot = (label_row == class_column).astype(f32)

    def mine(pair):
        return jnp.where(lax.rem(own, 2) == 0, pair[:slots], pair[unit : unit + slots])

    def dot(a, b):
        return jnp.dot(a, b, preferred_element_type=f32)

    def dot_turned(a, b):
        return lax.dot_general(a, b, (((1,), (1,)), ((), ())), preferred_element_type=f32)

    for l in range(depth):
        firsts_low = firsts_all[l].astype(bf16)
        firsts_turned = firsts_all[l].T.astype(bf16)
        cls = cls_w[:, l]
        cls_high, cls_low = split(cls)
        fetch(l).wait()
        weights, weights_low = split(w_buf[l])
        pooled = jnp.tanh(
            dot(firsts_low, weights) + dot(firsts_low, weights_low) + pool_b[l : l + 1]
        )
        pooled_high, pooled_low = split(pooled)
        scores = (
            dot_turned(cls_high, pooled_high)
            + (dot_turned(cls_low, pooled_high) + dot_turned(cls_high, pooled_low))
            + cls_b[l : l + 1].T
        )
        highest = jnp.max(scores, 0, keepdims=True)
        raised = jnp.exp(scores - highest)
        totals = jnp.sum(raised, 0, keepdims=True)
        grad = valid * (raised / totals - onehot) / count
        grad_column = grad.T
        inner = grad_column[:, 0:1] * cls[0:1]
        for c in range(1, classes):
            inner = inner + grad_column[:, c : c + 1] * cls[c : c + 1]
        inner = inner * (1.0 - pooled * pooled)
        inner_high, inner_low = split(inner)
        for t in range(width // 256):
            span = slice(t * 256, (t + 1) * 256)
            g_buf[l, span] = dot(firsts_turned[span], inner_high) + dot(
                firsts_turned[span], inner_low
            )
            put(l, t).start()
        grad_high, grad_low = split(grad)
        grad_cls_w[:, l] = dot(grad_high, pooled_high) + (
            dot(grad_low, pooled_high) + dot(grad_high, pooled_low)
        )
        inner_buf[...] = inner.reshape(devices // 2, packet, width)
        own_high, own_low = split(inner_buf[own // 2])
        own_grads = dot_turned(own_high, weights) + dot_turned(own_low, weights)
        first_grads[:, l] = mine(own_grads)
        grad_pool_b[l : l + 1] = jnp.sum(inner, 0, keepdims=True)
        grad_cls_b[l : l + 1] = jnp.sum(grad, 1, keepdims=True).T
        log_total = highest + jnp.log(totals)
        picked = jnp.sum(scores * onehot, 0, keepdims=True)
        losses[l] = jnp.sum(valid * (log_total - picked) / count)
        score_buf[...] = scores.T.reshape(devices // 2, packet, classes)
        logits[:, l] = mine(score_buf[own // 2])
        if l == 0:
            fetch_rest().wait()
            for s in range(slots):
                put_rest(s).start()
    for copy in outputs:
        copy.start()
    for l in range(depth):
        for t in range(width // 256):
            put(l, t).wait()
    for copy in outputs:
        copy.wait()
    for s in range(slots):
        put_rest(s).wait()


def run_ramps(gathered, states, rest, pool_w, pool_b, cls_w, cls_b):
    devices, packet, width = gathered.shape
    depth, classes = cls_b.shape
    slots = rest.shape[0]
    pairs = devices // 2
    place_hbm = pl.BlockSpec(memory_space=pl.ANY)
    cls_turned = jnp.transpose(cls_w, (2, 0, 1))
    states, logits, losses, pool_grad, pool_shift, cls_grad, cls_shift, first_grads = pl.pallas_call(
        ramps_kernel,
        name="ramps",
        out_shape=(
            jax.ShapeDtypeStruct(states.shape, states.dtype),
            jax.ShapeDtypeStruct((slots, depth, classes), f32),
            jax.ShapeDtypeStruct((depth,), f32),
            jax.ShapeDtypeStruct((depth, width, width), f32),
            jax.ShapeDtypeStruct((depth, width), f32),
            jax.ShapeDtypeStruct((classes, depth, width), f32),
            jax.ShapeDtypeStruct((depth, classes), f32),
            jax.ShapeDtypeStruct((slots, depth, width), f32),
        ),
        in_specs=[place_hbm] * 7,
        out_specs=(place_hbm,) * 8,
        input_output_aliases={1: 0},
        scratch_shapes=[
            pltpu.VMEM(gathered.shape, f32),
            pltpu.VMEM((depth, width, width), f32),
            pltpu.VMEM((depth, width, width), f32),
            pltpu.VMEM((pairs, packet, classes), f32),
            pltpu.VMEM((pairs, packet, width), f32),
            pltpu.VMEM(rest.shape, bf16),
            [pltpu.VMEM(member.shape, f32) for member in (pool_b, cls_turned, cls_b)],
            [
                pltpu.VMEM((slots, depth, classes), f32),
                pltpu.SMEM((depth,), f32),
                pltpu.VMEM((depth, width), f32),
                pltpu.VMEM((classes, depth, width), f32),
                pltpu.VMEM((depth, classes), f32),
                pltpu.VMEM((slots, depth, width), f32),
            ],
            pltpu.SemaphoreType.DMA((depth,)),
            pltpu.SemaphoreType.DMA((depth, width // 256)),
            pltpu.SemaphoreType.DMA((slots + 2,)),
            pltpu.SemaphoreType.DMA((3,)),
            pltpu.SemaphoreType.DMA((6,)),
        ],
        compiler_params=pltpu.CompilerParams(vmem_limit_bytes=62 * 1024 * 1024),
    )(gathered, states, rest, pool_w, pool_b, cls_turned, cls_b)
    return (
        states,
        jnp.transpose(logits, (1, 0, 2)),
        losses,
        pool_grad,
        pool_shift,
        jnp.transpose(cls_grad, (1, 2, 0)),
        cls_shift,
        jnp.transpose(first_grads, (1, 0, 2)),
    )


def local(
    hidden,
    lengths,
    slot_order,
    labels,
    w_qkv,
    b_query,
    b_value,
    w_out,
    b_out,
    ln1_gain,
    ln1_bias,
    w_in,
    b_in,
    w_back,
    b_back,
    ln2_gain,
    ln2_bias,
    pool_w,
    pool_b,
    cls_w,
    cls_b,
):
    stacks = (
        w_qkv,
        b_query,
        b_value,
        w_out,
        b_out,
        ln1_gain,
        ln1_bias,
        w_in,
        b_in,
        w_back,
        b_back,
        ln2_gain,
        ln2_bias,
    )
    states, context, packet = run_blocks(hidden, lengths, slot_order, labels, stacks)
    gathered, rest = run_finish(packet, states, context, stacks)
    gathered = gathered.reshape((-1,) + packet.shape)
    return run_ramps(gathered, states, rest, pool_w, pool_b, cls_w, cls_b)


def solution(mesh):
    both = ("wide", "narrow")
    return jax.shard_map(
        local,
        mesh=mesh,
        in_specs=(P(both, None, None), P(both), P(both), P(both)) + (P(),) * 17,
        out_specs=(
            P(None, both, None, None),
            P(None, both, None),
            P(),
            P(),
            P(),
            P(),
            P(),
            P(None, both, None),
        ),
        check_vma=False,
    )
```
